128 devices in a mesh: section: 2 (over z_hi), fsdp: 64 (over y, x, z_lo, core).
Axes of the slice: x: 4, y: 4, z: 4 (z_hi: 2, z_lo: 2; z = z_hi * 2 + z_lo), core: 2. Of those that a mesh axis runs over, the one named last changes fastest.
Arguments:
- tokens_in: bfloat16 [2, 6144, 1024], P(None, 'fsdp'), may hold values from -6 to 6
- attn_proj: bfloat16 [2, 1024, 3072], P('section', 'fsdp'), may hold values from -0.1875 to 0.1875
- attn_out: bfloat16 [2, 1024, 1024], P('section', 'fsdp'), may hold values from -1 to 1
- mlp_in: bfloat16 [2, 1024, 5248], P('section', 'fsdp'), may hold values from -0.1875 to 0.1875
- mlp_out: bfloat16 [2, 1024, 2624], P('section', 'fsdp'), may hold values from -0.125 to 0.125
- gain_attn: bfloat16 [2, 1024], P('section', 'fsdp'), may hold values from 0.25 to 1.75
- gain_mlp: bfloat16 [2, 1024], P('section', 'fsdp'), may hold values from 0.25 to 1.75
- lengths: int32 [2, 64, 4], P(None, 'fsdp'), may hold values from 1 to 78, 96 in all within a row
- cotangent: bfloat16 [2, 6144, 1024], P(None, 'fsdp'), may hold values from -16 to 16
Outputs:
- section_outputs: bfloat16 [2, 2, 6144, 1024], P('section', None, 'fsdp')
- section_input_grads: bfloat16 [2, 2, 6144, 1024], P('section', None, 'fsdp')
- grad_attn_proj: float32 [2, 1024, 3072], P('section', 'fsdp')
- grad_attn_out: float32 [2, 1024, 1024], P('section', 'fsdp')
- grad_mlp_in: float32 [2, 1024, 5248], P('section', 'fsdp')
- grad_mlp_out: float32 [2, 1024, 2624], P('section', 'fsdp')
- grad_gain_attn: float32 [2, 1024], P('section', 'fsdp')
- grad_gain_mlp: float32 [2, 1024], P('section', 'fsdp')
The draws below stay inside these ranges and needn't reach their ends.
Inputs may be any that keep to these rules, and one draw needn't show every extreme that they name: Each row of 4 lengths sums to 96, and every row's longest is at most 78.
All inputs are finite; a program needn't handle non-finite values.
Results may differ from the reference program's by a relative error of at most 0.025.
Values may be sent and summed in bfloat16 or wider, within the bound.
No kernel may reach another device: no remote copies, remote signals or barrier semaphores. Data moves between devices by JAX's collectives and lax.ppermute only.
A program may use at most 256 MiB of HBM per device.

```python
import math
import jax
import jax.numpy as jnp
import numpy as np
from jax import lax

D = 1024
HEADS = 16
HEAD_DIM = 64
F = 2624
WINDOW = 128
ROW = 96
SEQS = 4
MB = 2
SEQ_MOST = 78
LAYERS = 2
SHARDS = 64
TOKENS = 6144


def raised(result, rng, source, target, parts, factor):
    def block_of(axis_at):
        return (jnp.arange(result.shape[axis_at]) // (result.shape[axis_at] // parts)).reshape((-1,) + (1,) * (result.ndim - 1 - axis_at))

    one_side = jax.random.permutation(rng, parts)[block_of(target)]
    other_side = (block_of(target) + parts // 2) % parts
    return jnp.where((block_of(source) == one_side) | (block_of(source) == other_side), factor * result, result)


def block_scale(key, extent, split, least, top_value):
    def one(dim, shards_of):
        steps = jax.random.uniform(jax.random.fold_in(jax.random.fold_in(key, 6), dim), (shards_of,), jnp.float32, least / len(split), top_value / len(split))
        return jnp.repeat(jnp.exp(steps), extent[dim] // shards_of).reshape((-1,) + (1,) * (len(extent) - dim - 1))

    factor_of = one(*split[0])
    for cut in split[1:]:
        factor_of = factor_of * one(*cut)
    return factor_of


def length_profile(number_of, total, reach, lean):
    loads = [(1 << 20) // math.isqrt(rank ** lean) + 1 for rank in range(2, number_of + 1)]
    spare, holding = total - reach - (number_of - 1), [1] * (number_of - 1)
    while spare > 0:
        candidates = [i for i in range(number_of - 1) if holding[i] < reach]
        whole, left = sum([loads[i] for i in candidates]), spare
        for i in candidates:
            extra = min(reach - holding[i], max(1, left * loads[i] // whole), spare)
            holding[i] = holding[i] + extra
            spare = spare - extra
    return np.array([reach] + holding)


def uneven(own_key, count, total, bound, skew):
    if count == 2:
        one = jax.random.randint(own_key, (), max(1, total - bound), min(bound, total - 1) + 1)
        return jnp.stack([one, total - one])
    tallies = jnp.asarray(length_profile(count, total, bound, skew), jnp.int32)
    twos = (count - 1) // 2
    source_of, receiver = tallies[1:1 + 2 * twos:2], tallies[2:2 + 2 * twos:2]
    room = jnp.minimum(source_of - 1, bound - receiver)
    shifted = jax.random.randint(jax.random.fold_in(own_key, 1), (twos,), 0, 1 << 20) % (room + 1)
    tallies = tallies.at[1:1 + 2 * twos:2].set(source_of - shifted).at[2:2 + 2 * twos:2].set(receiver + shifted)
    return tallies[jax.random.permutation(jax.random.fold_in(own_key, 2), count)]


def bell_draw(own_key, extent, deviation, reach, pieces=(), kind=jnp.bfloat16):
    factor_of = block_scale(own_key, extent, pieces, -0.22, 0.18) if pieces else 1.0
    values = jax.random.normal(own_key, extent, jnp.float32) * deviation * factor_of
    return jnp.minimum(jnp.maximum(values, -reach), reach).astype(kind)


def bell_draw_with(own_key, extent, deviation, most, shards, heavy, kind=jnp.bfloat16):
    result = deviation * jax.random.normal(own_key, extent, jnp.float32)
    if shards:
        result = result * block_scale(own_key, extent, shards, -0.22, 0.18)
    return jnp.clip(raised(result, jax.random.fold_in(own_key, 3), *heavy), -most, most).astype(kind)


def setup_inputs(seed: int = 0) -> dict:
    arg_keys = jax.random.split(jax.random.key(seed), 10)
    return {
        "tokens_in": bell_draw(arg_keys[0], (MB, TOKENS, D), 1.0, 6.0, ((1, 64),)),
        "attn_proj": bell_draw(arg_keys[1], (LAYERS, D, 3 * D), D ** -0.5, 0.1875, ((0, 2), (1, 64))),
        "attn_out": bell_draw(arg_keys[2], (LAYERS, D, D), (D // 32) ** -0.5, 1.0, ((0, 2), (1, 64))),
        "mlp_in": bell_draw(arg_keys[3], (LAYERS, D, 2 * F), D ** -0.5, 0.1875, ((0, 2), (1, 64))),
        "mlp_out": bell_draw(arg_keys[4], (LAYERS, D, F), F ** -0.5, 0.125, ((0, 2), (1, 64))),
        "gain_attn": jnp.clip(1.0 + 0.15 * jax.random.normal(arg_keys[5], (LAYERS, D), jnp.float32), 0.25, 1.75).astype(jnp.bfloat16),
        "gain_mlp": jnp.clip(1.0 + 0.15 * jax.random.normal(arg_keys[6], (LAYERS, D), jnp.float32), 0.25, 1.75).astype(jnp.bfloat16),
        "lengths": jax.vmap(lambda own: uneven(own, SEQS, ROW, SEQ_MOST, 2))(jax.random.split(arg_keys[7], MB * SHARDS)).reshape((MB, SHARDS, SEQS)).astype(jnp.int32),
        "cotangent": bell_draw_with(arg_keys[8], (MB, TOKENS, D), 1.0, 16.0, ((1, 64),), (1, 2, 64, 4.0)),
    }


EPS = 1e-05
HIGHEST = lax.Precision.HIGHEST

@jax.custom_vjp
def low(v):
    return lax.optimization_barrier(v.astype(jnp.bfloat16)).astype(jnp.float32)

@jax.custom_vjp
def low_back(v):
    return v

def low_keep(v):
    return (low(v), None)

def low_pass(kept, grad):
    return (grad,)

def back_keep(v):
    return (v, None)

def back_low(kept, grad):
    return (low(grad),)
low.defvjp(low_keep, low_pass)
low_back.defvjp(back_keep, back_low)

def matmul(left, right):
    return jnp.dot(left, right, precision=HIGHEST, preferred_element_type=jnp.float32)

def layer_norm(values, gain):
    centre = lax.optimization_barrier(jnp.mean(values, -1, keepdims=True))
    centred = values - centre
    spread = lax.optimization_barrier(jnp.mean(centred * centred, -1, keepdims=True))
    return centred * lax.rsqrt(spread + EPS) * gain

def rotate(values, inner, base):
    half = values.shape[-1] // 2
    phases = jnp.arange(half, dtype=jnp.float32) * (2.0 / values.shape[-1])
    freqs = jnp.exp(-jnp.log(base) * phases)
    angles = inner.astype(jnp.float32)[..., None] * freqs
    cosine = jnp.concatenate([jnp.cos(angles), jnp.cos(angles)], -1)[..., None, :]
    sine = jnp.concatenate([jnp.sin(angles), jnp.sin(angles)], -1)[..., None, :]
    turned = jnp.concatenate([-values[..., half:], values[..., :half]], -1)
    return values * cosine + turned * sine

def segment_info(lens, count):
    ends = jnp.cumsum(lens, axis=-1)
    starts = ends - lens
    places = jnp.arange(count, dtype=jnp.int32)
    segment = lax.optimization_barrier(jnp.sum((places[:, None] >= ends[..., None, :]).astype(jnp.int32), axis=-1))
    picked = (segment[..., None] == jnp.arange(lens.shape[-1], dtype=jnp.int32)).astype(jnp.int32)
    inner = places - lax.optimization_barrier(jnp.sum(picked * starts[..., None, :], axis=-1))
    return (segment, inner)

def gated_unit(packed):
    half = packed.shape[-1] // 2
    return jax.nn.gelu(packed[..., :half], approximate=False) * packed[..., half:]

def attend_block(queries, keys, values_in, allowed):
    scores = jnp.einsum('qhd,khd->hqk', queries, keys, precision=HIGHEST) * HEAD_DIM ** (-0.5)
    scores = jnp.where(allowed[None], low_back(scores), -1e+30)
    peak = lax.optimization_barrier(jnp.max(scores, -1, keepdims=True))
    log_total = peak + jnp.log(lax.optimization_barrier(jnp.sum(jnp.exp(scores - peak), -1, keepdims=True)))
    probs = jnp.where(allowed[None], jnp.exp(scores - log_total), 0.0)
    return jnp.einsum('hqk,khd->qhd', low(probs), values_in, precision=HIGHEST)

def layer(inputs, proj, out_proj, up_proj, down_proj, gain_a, gain_m, allowed, inner, base):
    blocks, slots = (allowed.shape[0], allowed.shape[1])
    normed = low(layer_norm(inputs, gain_a))
    packed = low_back(matmul(normed, proj)).reshape(blocks, slots, 3, HEADS, HEAD_DIM)
    queries = low(rotate(packed[:, :, 0], inner, base))
    keys = low(rotate(packed[:, :, 1], inner, base))
    values_in = low(packed[:, :, 2])
    checked = jax.checkpoint(attend_block)
    attended = lax.map(lambda group: checked(*group), (queries, keys, values_in, allowed))
    attended = low(low_back(attended.reshape(blocks * slots, D)))
    hidden = inputs + low_back(matmul(attended, out_proj))
    normed_m = low(layer_norm(hidden, gain_m))
    gate_up = low_back(matmul(normed_m, up_proj))
    middle = low(gated_unit(gate_up))
    return hidden + matmul(middle, down_proj.T)

def reference(tokens_in, attn_proj, attn_out, mlp_in, mlp_out, gain_attn, gain_mlp, lengths, cotangent):
    blocks = MB * SHARDS
    lens = lengths.reshape(blocks, SEQS)
    segment, inner = segment_info(lens, ROW)
    same = segment[:, :, None] == segment[:, None, :]
    near = jnp.abs(inner[:, :, None] - inner[:, None, :]) <= WINDOW // 2
    masks = (same & near, same)
    bases = (10000.0, 160000.0)
    weights = tuple((w.astype(jnp.float32) for w in (attn_proj, attn_out, mlp_in, mlp_out, gain_attn, gain_mlp)))
    flat_in = tokens_in.astype(jnp.float32).reshape(blocks * ROW, D)

    def forward(start, offset, params):
        first = [w[0] for w in params]
        out_first = low(layer(start, *first, masks[0], inner, bases[0]))
        second_in = low_back(out_first + offset)
        second = [w[1] for w in params]
        return (layer(second_in, *second, masks[1], inner, bases[1]), out_first)
    out_last, grad_fn, out_first = jax.vjp(forward, flat_in, jnp.zeros_like(flat_in), weights, has_aux=True)
    grad_in, grad_mid, grad_weights = grad_fn(cotangent.astype(jnp.float32).reshape(blocks * ROW, D))
    section_outputs = jnp.stack([out_first, out_last]).astype(jnp.bfloat16).reshape(2, MB, TOKENS, D)
    section_input_grads = jnp.stack([grad_in, grad_mid]).astype(jnp.bfloat16).reshape(2, MB, TOKENS, D)
    return (section_outputs, section_input_grads, grad_weights[0], grad_weights[1], grad_weights[2], grad_weights[3], grad_weights[4], grad_weights[5])
```

```python
import jax
import jax.numpy as jnp
from jax import lax
from jax.sharding import PartitionSpec as P

HEADS = 16
HEAD_DIM = 64
WINDOW = 128
EPS = 1e-05
NY, NX, NZ, NC = 4, 4, 2, 2
SHARDS = NY * NX * NZ * NC
BF = jnp.bfloat16
F32 = jnp.float32


def split_index(i):
    return i // (NX * NZ * NC), (i // (NZ * NC)) % NX, (i // NC) % NZ, i % NC


def join_index(y, x, z, c):
    return ((y * NX + x) * NZ + z) * NC + c


def pairs(kind, step=1):
    out = []
    for i in range(SHARDS):
        y, x, z, c = split_index(i)
        if kind == "core":
            c = 1 - c
        elif kind == "z":
            z = 1 - z
        elif (kind == "first") == (c == 0):
            y = (y + step) % NY
        else:
            x = (x + step) % NX
        out.append((i, join_index(y, x, z, c)))
    return out


def send(value, kind, step=1):
    return lax.ppermute(value, "fsdp", pairs(kind, step))


def ring_gather(block, kind):
    half = block.shape[0] // 2
    after = send(block, kind, -1)
    before = send(block, kind, 1)
    far_a = send(after[:half], kind, -1)
    far_b = send(before[half:], kind, 1)
    return after, far_a, far_b, before


def gather(shard):
    block = jnp.concatenate([shard, send(shard, "z")], 0)
    block = jnp.concatenate([block, *ring_gather(block, "second")], 0)
    own = (block, *ring_gather(block, "first"))
    other = tuple(send(piece, "core") for piece in own)
    return jnp.concatenate([*own, *other], 0)


def ring_scatter(block, kind):
    rows = block.shape[0] // 4
    half = rows // 2
    here, after, far, before = (block[k * rows : (k + 1) * rows] for k in range(4))
    got_a = send(far[:half], kind, 1)
    got_b = send(far[half:], kind, -1)
    after = jnp.concatenate([add(after[:half], got_a).astype(BF), after[half:]], 0)
    before = jnp.concatenate([before[:half], add(before[half:], got_b).astype(BF)], 0)
    got_c = send(after, kind, 1)
    got_d = send(before, kind, -1)
    return here.astype(F32) + got_c.astype(F32) + got_d.astype(F32)


def add(left, right):
    return left.astype(F32) + right.astype(F32)


def scatter(lefts, rights):
    half = lefts[0].shape[1] // 2

    def product(rows):
        return jnp.concatenate([contract_first(l[:, rows], r) for l, r in zip(lefts, rights)], 1)

    got = send(product(slice(half, None)).astype(BF), "core")
    block = (product(slice(0, half)) + got.astype(F32)).astype(BF)
    block = ring_scatter(block, "first").astype(BF)
    block = ring_scatter(block, "second").astype(BF)
    mine = block.shape[0] // 2
    return add(block[:mine], send(block[mine:], "z"))


def relative_order(me):
    y, x, z, c = split_index(me)
    place = jnp.arange(SHARDS * 16, dtype=jnp.int32)
    block, inside = place // 16, place % 16
    core = c ^ (block // 32)
    first, second = (block // 8) % 4, (block // 2) % 4
    row_y = (y + jnp.where(core == 0, first, second)) % NY
    row_x = (x + jnp.where(core == 0, second, first)) % NX
    absolute = join_index(row_y, row_x, z ^ (block % 2), core) * 16 + inside
    return (place[:, None] == absolute[None, :]).astype(BF)


def dot(left, right):
    return jnp.dot(left, right, preferred_element_type=F32)


def contract_last(left, right):
    return lax.dot_general(left, right, (((1,), (1,)), ((), ())), preferred_element_type=F32)


def contract_first(left, right):
    return lax.dot_general(left, right, (((0,), (0,)), ((), ())), preferred_element_type=F32)


def to_absolute(values, order):
    high = lax.reduce_precision(values, 8, 7)
    low = (values - high).astype(BF)
    return contract_last(high.astype(BF), order) + contract_last(low, order)


def normal(values):
    centre = jnp.mean(values, -1, keepdims=True)
    centred = values - centre
    scale = lax.rsqrt(jnp.mean(centred * centred, -1, keepdims=True) + EPS)
    return centred * scale, scale


def normal_back(grad, unit, scale):
    return scale * (
        grad
        - jnp.mean(grad, -1, keepdims=True)
        - unit * jnp.mean(grad * unit, -1, keepdims=True)
    )


def angles_of(inner, base):
    half = HEAD_DIM // 2
    freqs = jnp.exp(-jnp.log(base) * (jnp.arange(half, dtype=F32) * (2.0 / HEAD_DIM)))
    angles = inner.astype(F32)[..., None] * freqs
    return jnp.cos(angles)[:, None, :], jnp.sin(angles)[:, None, :]


def rotate(values, turn):
    cosine, sine = turn
    half = HEAD_DIM // 2
    one, two = values[..., :half], values[..., half:]
    return jnp.concatenate([one * cosine - two * sine, two * cosine + one * sine], -1)


def rotate_back(values, turn):
    cosine, sine = turn
    half = HEAD_DIM // 2
    one, two = values[..., :half], values[..., half:]
    return jnp.concatenate([one * cosine + two * sine, two * cosine - one * sine], -1)


def segment_info(lens, count):
    ends = jnp.cumsum(lens, axis=-1)
    starts = ends - lens
    places = jnp.arange(count, dtype=jnp.int32)
    segment = jnp.sum((places[:, None] >= ends[..., None, :]).astype(jnp.int32), axis=-1)
    picked = (segment[..., None] == jnp.arange(lens.shape[-1], dtype=jnp.int32)).astype(jnp.int32)
    inner = places - jnp.sum(picked * starts[..., None, :], axis=-1)
    return segment, inner


def row_mask(lens, count, spanning):
    segment, inner = segment_info(lens, count)
    same = segment[:, :, None] == segment[:, None, :]
    near = jnp.abs(inner[:, :, None] - inner[:, None, :]) <= WINDOW // 2
    return same & (near | spanning), inner


def gated_unit(gate, up):
    return jax.nn.gelu(gate, approximate=False) * up


def layer_forward(layer_in, weights, allowed, turn, order):
    proj, out_proj, up_proj, down_proj, gain_a, gain_m = weights
    micro, slots = allowed.shape[:2]
    tokens, width = layer_in.shape
    unit_a, scale_a = normal(dot(layer_in, order))
    normed = (unit_a * gain_a).astype(BF)
    packed = dot(normed, proj).reshape(tokens, 3, HEADS, HEAD_DIM)
    queries = rotate(packed[:, 0], turn).astype(BF).reshape(micro, slots, HEADS, HEAD_DIM)
    keys = rotate(packed[:, 1], turn).astype(BF).reshape(micro, slots, HEADS, HEAD_DIM)
    values_in = packed[:, 2].astype(BF).reshape(micro, slots, HEADS, HEAD_DIM)
    scores = jnp.einsum("mqhd,mkhd->mhqk", queries, keys, preferred_element_type=F32) * HEAD_DIM**-0.5
    scores = jnp.where(allowed[:, None], scores, -1e30)
    peak = jnp.max(scores, -1, keepdims=True)
    log_total = peak + jnp.log(jnp.sum(jnp.exp(scores - peak), -1, keepdims=True))
    probs = jnp.where(allowed[:, None], jnp.exp(scores - log_total), 0.0)
    attended = jnp.einsum("mhqk,mkhd->mqhd", probs.astype(BF), values_in, preferred_element_type=F32)
    attended = dot(attended.reshape(tokens, width).astype(BF), order).astype(BF)
    hidden = layer_in.astype(F32) + dot(attended, out_proj)
    unit_m, scale_m = normal(hidden)
    normed_m = dot((unit_m * gain_m).astype(BF), order).astype(BF)
    gate_up = dot(normed_m, up_proj)
    middle = gated_unit(gate_up[:, : gate_up.shape[1] // 2], gate_up[:, gate_up.shape[1] // 2 :]).astype(BF)
    result = (hidden + to_absolute(contract_last(middle, down_proj), order)).astype(BF)
    saved = (unit_a, scale_a, normed, queries, keys, values_in, probs, attended, unit_m, scale_m, normed_m, gate_up, middle)
    return result, saved


def layer_backward(grad_out, saved, weights, turn, order):
    unit_a, scale_a, normed, queries, keys, values_in, probs, attended, unit_m, scale_m, normed_m, gate_up, middle = saved
    proj, out_proj, up_proj, down_proj, gain_a, gain_m = weights
    micro, slots = queries.shape[:2]
    tokens, width = grad_out.shape
    grad_out_rel = dot(grad_out, order).astype(BF)
    grad_middle = dot(grad_out_rel, down_proj)
    half = gate_up.shape[1] // 2
    grad_gate, grad_up = jax.vjp(gated_unit, gate_up[:, :half], gate_up[:, half:])[1](grad_middle)
    grad_gate_up = jnp.concatenate([grad_gate, grad_up], 1).astype(BF)
    grad_normed_m = to_absolute(contract_last(grad_gate_up, up_proj), order)
    term_m = (grad_normed_m * unit_m).astype(BF)
    grad_hidden = grad_out.astype(F32) + normal_back(grad_normed_m * gain_m, unit_m, scale_m)
    grad_branch = grad_hidden.astype(BF)
    grad_attended = contract_last(contract_last(grad_branch, out_proj).astype(BF), order)
    grad_attended = grad_attended.reshape(micro, slots, HEADS, HEAD_DIM).astype(BF)
    grad_values = jnp.einsum("mhqk,mqhd->mkhd", probs.astype(BF), grad_attended, preferred_element_type=F32)
    grad_probs = jnp.einsum("mqhd,mkhd->mhqk", grad_attended, values_in, preferred_element_type=F32)
    grad_scores = (probs * (grad_probs - jnp.sum(probs * grad_probs, -1, keepdims=True))).astype(BF)
    scale = HEAD_DIM**-0.5
    grad_queries = jnp.einsum("mhqk,mkhd->mqhd", grad_scores, keys, preferred_element_type=F32) * scale
    grad_keys = jnp.einsum("mhqk,mqhd->mkhd", grad_scores, queries, preferred_element_type=F32) * scale
    shape = (tokens, HEADS, HEAD_DIM)
    grad_packed = jnp.concatenate(
        [
            rotate_back(grad_queries.reshape(shape), turn).reshape(tokens, width),
            rotate_back(grad_keys.reshape(shape), turn).reshape(tokens, width),
            grad_values.reshape(tokens, width),
        ],
        1,
    ).astype(BF)
    grad_normed = contract_last(grad_packed, proj)
    term_a = (grad_normed * unit_a).astype(BF)
    grad_in = grad_hidden + to_absolute(normal_back(grad_normed * gain_a, unit_a, scale_a), order)
    return grad_in.astype(BF), (grad_out_rel, grad_gate_up, grad_branch, grad_packed, term_a, term_m)


def shards(tokens_in, attn_proj, attn_out, mlp_in, mlp_out, gain_attn, gain_mlp, lengths, cotangent):
    section = lax.axis_index("section")
    micro, slots, width = tokens_in.shape
    tokens = micro * slots
    three, hidden_two = attn_proj.shape[2], mlp_in.shape[2]
    edge = three + width
    gains = jnp.zeros((gain_attn.shape[1], 128), BF)
    gains = gains.at[:, 0].set(gain_attn[0]).at[:, 1].set(gain_mlp[0])
    whole_a = gather(jnp.concatenate([attn_proj[0], attn_out[0], gains], 1))
    whole_m = gather(jnp.concatenate([mlp_in[0], mlp_out[0]], 1))
    order = relative_order(lax.axis_index("fsdp"))
    gain_a = whole_a[:, edge].astype(F32)[None]
    gain_m = contract_last(whole_a[:, edge + 1][None], order)
    weights = (
        whole_a[:, :three],
        whole_a[:, three:edge],
        whole_m[:, :hidden_two],
        whole_m[:, hidden_two:],
        gain_a,
        gain_m,
    )
    base = jnp.where(section == 0, 10000.0, 160000.0).astype(F32)
    allowed, inner = row_mask(lengths[:, 0], slots, section > 0)
    turn = angles_of(inner.reshape(tokens), base)
    first_in = tokens_in.reshape(tokens, width)
    middle_out, _ = layer_forward(first_in, weights, allowed, turn, order)
    received = lax.ppermute(middle_out, "section", [(0, 1)])
    layer_in = jnp.where(section == 0, first_in, received)
    result, saved = layer_forward(layer_in, weights, allowed, turn, order)
    last_grad = cotangent.reshape(tokens, width)
    middle_grad, _ = layer_backward(last_grad, saved, weights, turn, order)
    received = lax.ppermute(middle_grad, "section", [(1, 0)])
    grad_out = jnp.where(section == 1, last_grad, received)
    grad_in, terms = layer_backward(grad_out, saved, weights, turn, order)
    grad_out_rel, grad_gate_up, grad_branch, grad_packed, term_a, term_m = terms
    normed, attended, normed_m, middle = saved[2], saved[7], saved[10], saved[12]
    sum_m = scatter((normed_m, grad_out_rel), (grad_gate_up, middle))
    lane = jnp.arange(128, dtype=jnp.int32)[None]
    pick_a = jnp.broadcast_to(lane == 0, (tokens, 128)).astype(BF)
    pick_m = jnp.broadcast_to(lane == 1, (tokens, 128)).astype(BF)
    term_m = dot(term_m, order).astype(BF)
    sum_a = scatter(
        (normed, attended, jnp.concatenate([term_a, term_m], 0)),
        (grad_packed, grad_branch, jnp.concatenate([pick_a, pick_m], 0)),
    )
    return (
        result.reshape(1, micro, slots, width),
        grad_in.reshape(1, micro, slots, width),
        sum_a[:, :three][None],
        sum_a[:, three:edge][None],
        sum_m[:, :hidden_two][None],
        sum_m[:, hidden_two:][None],
        sum_a[:, edge][None],
        sum_a[:, edge + 1][None],
    )


def solution(mesh):
    in_specs = (
        P(None, "fsdp", None),
        P("section", "fsdp", None),
        P("section", "fsdp", None),
        P("section", "fsdp", None),
        P("section", "fsdp", None),
        P("section", "fsdp"),
        P("section", "fsdp"),
        P(None, "fsdp", None),
        P(None, "fsdp", None),
    )
    out_specs = (
        P("section", None, "fsdp", None),
        P("section", None, "fsdp", None),
        P("section", "fsdp", None),
        P("section", "fsdp", None),
        P("section", "fsdp", None),
        P("section", "fsdp", None),
        P("section", "fsdp"),
        P("section", "fsdp"),
    )
    return jax.shard_map(shards, mesh=mesh, in_specs=in_specs, out_specs=out_specs, check_vma=False)
```

```python
import functools
import math
import jax
import jax.numpy as jnp
from jax import lax
from jax.experimental import pallas as pl
from jax.experimental.pallas import tpu as pltpu
from jax.sharding import PartitionSpec as P

HEADS = 16
HEAD_DIM = 64
WINDOW = 128
EPS = 1e-05
NY, NX, NZ, NC = 4, 4, 2, 2
SHARDS = NY * NX * NZ * NC
BF = jnp.bfloat16
F32 = jnp.float32
ATTN_TILE = 1024
MLP_TILE = 896
GAIN_TILE = 128
GROUP = 8
SCALE = HEAD_DIM**-0.5
PARAMS = pltpu.CompilerParams(vmem_limit_bytes=56 * 1024 * 1024)


def split_index(i):
    return i // (NX * NZ * NC), (i // (NZ * NC)) % NX, (i // NC) % NZ, i % NC


def join_index(y, x, z, c):
    return ((y * NX + x) * NZ + z) * NC + c


def pairs(kind, step=1):
    out = []
    for i in range(SHARDS):
        y, x, z, c = split_index(i)
        if kind == "core":
            c = 1 - c
        elif kind == "z":
            z = 1 - z
        elif (kind == "first") == (c == 0):
            y = (y + step) % NY
        else:
            x = (x + step) % NX
        out.append((i, join_index(y, x, z, c)))
    return out


def send(value, kind, step=1):
    return lax.ppermute(value, "fsdp", pairs(kind, step))


def tie(*values):
    return lax.optimization_barrier(values)


def rows(*blocks):
    return jnp.concatenate(blocks, 0)


def spread(block):
    return rows(block, send(block, "second", -1), send(block, "second", 2), send(block, "second", 1))


def near(block):
    return send(block, "first", -1), send(block, "first", 1)


def far(after, before):
    half = after.shape[0] // 2
    return send(after[:half], "first", -1), send(before[half:], "first", 1)


def core(*pieces):
    return tuple(send(piece, "core") for piece in pieces)


def gather(a, m, d):
    a_z = send(a, "z")
    a = rows(a, a_z)
    d = spread(d)
    a, m = tie(a, m)
    m_z = send(m, "z")
    a = spread(a)
    a, d = tie(a, d)
    a_after, a_before = near(a)
    d_after, d_before = near(d)
    a, m, m_z = tie(a, m, m_z)
    m = spread(rows(m, m_z))
    d_far, d_far2 = far(d_after, d_before)
    a_after, a_before, m, d_far, d_far2 = tie(a_after, a_before, m, d_far, d_far2)
    a_far, a_far2 = far(a_after, a_before)
    m_after, m_before = near(m)
    d = rows(d, d_after, d_far, d_far2, d_before)
    d = (d, send(d, "z"))
    a = (a, a_after, a_far, a_far2, a_before)
    a = a + core(*a)
    m_after, m_before, a = tie(m_after, m_before, a)
    m_far, m_far2 = far(m_after, m_before)
    m = (m, m_after, m_far, m_far2, m_before)
    return a, m + core(*m), d + core(*d)


def add(left, right):
    return left.astype(F32) + right.astype(F32)


def ring_scatter(here, after, far_a, far_b, before, kind):
    half = far_a.shape[0]
    got_a = send(far_a, kind, 1)
    got_b = send(far_b, kind, -1)
    after = rows(add(after[:half], got_a).astype(BF), after[half:])
    before = rows(before[:half], add(before[half:], got_b).astype(BF))
    got_c = send(after, kind, 1)
    got_d = send(before, kind, -1)
    return add(here, got_c) + got_d.astype(F32)


def direct_scatter(block, kind):
    size = block.shape[0] // 4
    here, after, far, before = (block[k * size : (k + 1) * size] for k in range(4))
    return add(here, send(after, kind, 1)) + add(send(far, kind, 2), send(before, kind, -1))


def cut(size):
    quarter = size // 4
    return quarter, quarter, quarter // 2, quarter // 2, quarter


def split(block, sizes):
    edges = [sum(sizes[:k]) for k in range(len(sizes) + 1)]
    return tuple(block[low:high] for low, high in zip(edges[:-1], edges[1:]))


def finish_z_first(mine, other):
    block = add(mine, send(other, "z")).astype(BF)
    block = ring_scatter(*split(block, cut(block.shape[0])), "first").astype(BF)
    return direct_scatter(block, "second")


def finish(*parts):
    block = ring_scatter(*parts, "first").astype(BF)
    block = direct_scatter(block, "second").astype(BF)
    mine = block.shape[0] // 2
    return add(block[:mine], send(block[mine:], "z"))


def relative_order(me, z_first):
    y, x, z, c = split_index(me)
    place = jnp.arange(SHARDS * 16, dtype=jnp.int32)
    block, inside = place // 16, place % 16
    core = c ^ (block // 32)
    if z_first:
        flip, first, second = (block // 16) % 2, (block // 4) % 4, block % 4
    else:
        flip, first, second = block % 2, (block // 8) % 4, (block // 2) % 4
    row_y = (y + jnp.where(core == 0, first, second)) % NY
    row_x = (x + jnp.where(core == 0, second, first)) % NX
    absolute = join_index(row_y, row_x, z ^ flip, core) * 16 + inside
    return (place[:, None] == absolute[None, :]).astype(BF)


def dot(left, right):
    return jnp.dot(left, right, preferred_element_type=F32)


def contract_last(left, right):
    return lax.dot_general(left, right, (((1,), (1,)), ((), ())), preferred_element_type=F32)


def contract_first(left, right):
    return lax.dot_general(left, right, (((0,), (0,)), ((), ())), preferred_element_type=F32)


def normal(values):
    centre = jnp.mean(values, -1, keepdims=True)
    centred = values - centre
    scale = lax.rsqrt(jnp.mean(centred * centred, -1, keepdims=True) + EPS)
    return centred * scale, scale


def normal_back(grad, unit, scale):
    return scale * (
        grad
        - jnp.mean(grad, -1, keepdims=True)
        - unit * jnp.mean(grad * unit, -1, keepdims=True)
    )


def segment_info(lens, count):
    ends = jnp.cumsum(lens, axis=-1)
    starts = ends - lens
    places = jnp.arange(count, dtype=jnp.int32)
    segment = jnp.sum((places[:, None] >= ends[..., None, :]).astype(jnp.int32), axis=-1)
    picked = (segment[..., None] == jnp.arange(lens.shape[-1], dtype=jnp.int32)).astype(jnp.int32)
    inner = places - jnp.sum(picked * starts[..., None, :], axis=-1)
    return segment, inner


def to_absolute(values, order):
    high = values.astype(BF)
    low = (values - high.astype(F32)).astype(BF)
    return contract_last(high, order) + contract_last(low, order)


def stack_rows(refs):
    return jnp.concatenate([ref[...] for ref in refs], 0)


def gain_rows(refs):
    row = lax.broadcasted_iota(jnp.int32, (16, 128), 0)
    lane = lax.broadcasted_iota(jnp.int32, (16, 128), 1)
    return contract_last((row == lane).astype(BF), stack_rows(refs))


def partner(values):
    width = values.shape[1]
    lane = lax.broadcasted_iota(jnp.int32, values.shape, 1)
    ahead = pltpu.roll(values, width - HEAD_DIM // 2, 1)
    behind = pltpu.roll(values, HEAD_DIM // 2, 1)
    return jnp.where(lane % HEAD_DIM < HEAD_DIM // 2, -ahead, behind)


def widen(table, width):
    return jnp.concatenate([table] * (width // table.shape[1]), 1)


def pair_bias(col, row):
    same = col[:, 0:1] == row[0:1]
    near = jnp.abs(col[:, 1:2] - row[1:2]) <= col[:, 2:3]
    return jnp.where(same & near, 0.0, -1e30)


def head_of(qkv, part, head, rows):
    return qkv[part, rows, head * HEAD_DIM : (head + 1) * HEAD_DIM]


def attn_forward_kernel(n, micro, steps, *refs):
    u, order, cos, sin, col, row = refs[:6]
    proj, out, gains = refs[6 : 6 + n], refs[6 + n : 6 + 2 * n], refs[6 + 2 * n : 6 + 3 * n]
    xn_out, qkv_out, lse_out, o_out, h_out, yn_out, qkv, xn = refs[6 + 3 * n :]
    step = pl.program_id(0)

    @pl.when(step == 0)
    def _():
        unit, _ = normal(dot(u[...], order[...]))
        xn[...] = (unit * gain_rows(gains)[0:1]).astype(BF)
        xn_out[...] = xn[...]

    packed = dot(xn[...], stack_rows(proj))

    @pl.when(step < steps * 2 // 3)
    def _():
        turned = packed * widen(cos[...], ATTN_TILE) + partner(packed) * widen(sin[...], ATTN_TILE)
        qkv[step] = turned.astype(BF)

    @pl.when(step >= steps * 2 // 3)
    def _():
        qkv[step] = packed.astype(BF)

    qkv_out[0] = qkv[step]

    @pl.when(step == steps - 1)
    def _():
        slots = u.shape[0] // micro
        lane = lax.broadcasted_iota(jnp.int32, (slots, 128), 1)
        blocks = []
        for m in range(micro):
            rows = slice(m * slots, (m + 1) * slots)
            bias = pair_bias(col[rows], row[m])
            log_all = jnp.zeros((slots, 128), F32)
            heads = []
            for low in range(0, HEADS, GROUP):
                group = range(low, low + GROUP)
                scores = [contract_last(head_of(qkv, 0, k, rows), head_of(qkv, 1, k, rows)) * SCALE + bias for k in group]
                peaks = [jnp.max(x, -1, keepdims=True) for x in scores]
                scores = [jnp.exp(x - p) for x, p in zip(scores, peaks)]
                totals = [jnp.sum(x, -1, keepdims=True) for x in scores]
                for k, p, t in zip(group, peaks, totals):
                    log_all = jnp.where(lane == k, p + jnp.log(t), log_all)
                probs = [(x * (1.0 / t)).astype(BF) for x, t in zip(scores, totals)]
                heads += [dot(x, head_of(qkv, 2, k, rows)).astype(BF) for k, x in zip(group, probs)]
            lse_out[rows] = log_all
            blocks.append(jnp.concatenate(heads, 1))
        attended = dot(jnp.concatenate(blocks, 0), order[...]).astype(BF)
        o_out[...] = attended
        hidden = u[...].astype(F32) + dot(attended, stack_rows(out))
        h_out[...] = hidden
        unit, _ = normal(hidden)
        gain = contract_last(gain_rows(gains).astype(BF), order[...])[1:2]
        yn_out[...] = dot((unit * gain).astype(BF), order[...]).astype(BF)


def mlp_forward_kernel(n, steps, *refs):
    yn, h, order = refs[:3]
    gate, up, down = refs[3 : 3 + n], refs[3 + n : 3 + 2 * n], refs[3 + 2 * n : -5]
    mid_out, one_out, two_out, z_out, total = refs[-5:]
    step = pl.program_id(0)
    g = dot(yn[...], stack_rows(gate))
    v = dot(yn[...], stack_rows(up))
    cdf = 0.5 * (1.0 + lax.erf(g * math.sqrt(0.5)))
    slope = cdf + g * jnp.exp(-0.5 * g * g) * (1.0 / math.sqrt(2.0 * math.pi))
    unit = g * cdf
    mid = (unit * v).astype(BF)
    mid_out[...] = mid
    one_out[...] = (v * slope).astype(BF)
    two_out[...] = unit.astype(BF)
    part = contract_last(mid, stack_rows(down))

    @pl.when(step == 0)
    def _():
        total[...] = part

    @pl.when(step > 0)
    def _():
        total[...] += part

    @pl.when(step == steps - 1)
    def _():
        z_out[...] = (h[...] + to_absolute(total[...], order[...])).astype(BF)


def mlp_backward_kernel(n, steps, *refs):
    dzr, dz, h, order, one, two = refs[:6]
    counts = (n[0], n[1], n[1], n[2])
    gains, gate, up, down = (refs[6 + sum(counts[:k]) : 6 + sum(counts[: k + 1])] for k in range(4))
    dg_out, dv_out, dh_out, da_out, term_out, total = refs[6 + sum(counts) :]
    step = pl.program_id(0)

    @pl.when(step == 0)
    def _():
        total[...] = jnp.zeros_like(total)

    dmid = dot(dzr[...], stack_rows(down))
    dg = (dmid * one[...].astype(F32)).astype(BF)
    dv = (dmid * two[...].astype(F32)).astype(BF)
    dg_out[...] = dg
    dv_out[...] = dv
    total[...] += contract_last(dg, stack_rows(gate)) + contract_last(dv, stack_rows(up))

    @pl.when(step == steps - 1)
    def _():
        dyn = to_absolute(total[...], order[...])
        unit, scale = normal(h[...])
        gain = contract_last(gain_rows(gains).astype(BF), order[...])[1:2]
        term_out[...] = dot((dyn * unit).astype(BF), order[...]).astype(BF)
        dh = dz[...].astype(F32) + normal_back(dyn * gain, unit, scale)
        dh_out[...] = dh
        da_out[...] = dh.astype(BF)


def attn_backward_kernel(n, micro, steps, *refs):
    da, dh, u, order, cos, sin, col, row, qkv, lse = refs[:10]
    out, gains, proj = (refs[10 + k * n : 10 + (k + 1) * n] for k in range(3))
    dqkv_out, du_out, term_out, dqkv, total = refs[10 + 3 * n :]
    step = pl.program_id(0)
    @pl.when(step == 0)
    def _():
        total[...] = jnp.zeros_like(total)
        rel = contract_last(da[...], stack_rows(out)).astype(BF)
        do_all = contract_last(rel, order[...]).astype(BF)
        slots = u.shape[0] // micro
        for m in range(micro):
            rows = slice(m * slots, (m + 1) * slots)
            bias = pair_bias(col[rows], row[m])
            log_all = lse[rows]
            cosine, sine = widen(cos[rows], ATTN_TILE), widen(sin[rows], ATTN_TILE)
            dqs, dks, dvs = [], [], []
            for low in range(0, HEADS, GROUP):
                group = range(low, low + GROUP)
                qs, ks, vs = ([head_of(qkv, part, k, rows) for k in group] for part in range(3))
                ds = [do_all[rows, k * HEAD_DIM : (k + 1) * HEAD_DIM] for k in group]
                probs = [contract_last(q, k) * SCALE + bias for q, k in zip(qs, ks)]
                probs = [jnp.exp(x - log_all[:, k : k + 1]) for x, k in zip(probs, group)]
                dps = [contract_last(d, v) for d, v in zip(ds, vs)]
                dss = [(p * (x - jnp.sum(p * x, -1, keepdims=True))).astype(BF) for p, x in zip(probs, dps)]
                dvs += [contract_first(p.astype(BF), d) for p, d in zip(probs, ds)]
                dqs += [dot(x, k) for x, k in zip(dss, ks)]
                dks += [contract_first(x, q) for x, q in zip(dss, qs)]
            dq, dk = (jnp.concatenate(x, 1) * SCALE for x in (dqs, dks))
            dqkv[0, rows] = (dq * cosine - partner(dq) * sine).astype(BF)
            dqkv[1, rows] = (dk * cosine - partner(dk) * sine).astype(BF)
            dqkv[2, rows] = jnp.concatenate(dvs, 1).astype(BF)

    dqkv_out[...] = dqkv[step]
    total[...] += contract_last(dqkv[step], stack_rows(proj))

    @pl.when(step == steps - 1)
    def _():
        unit, scale = normal(dot(u[...], order[...]))
        dxn = total[...]
        term_out[...] = (dxn * unit).astype(BF)
        back = normal_back(dxn * gain_rows(gains)[0:1], unit, scale)
        du_out[...] = (dh[...] + to_absolute(back, order[...])).astype(BF)


def columns(pieces, tile, place):
    return [pl.BlockSpec((p.shape[0], tile), lambda j: (0, place(j))) for p in pieces]


def whole(array):
    return pl.BlockSpec(array.shape, lambda j: (0,) * array.ndim)


def shape_of(rows, cols, kind=BF):
    return jax.ShapeDtypeStruct((rows, cols), kind)


def fixed(rows, cols):
    return pl.BlockSpec((rows, cols), lambda j: (0, 0))


def tiled(rows, cols, start=0, count=None):
    if count is None:
        return pl.BlockSpec((rows, cols), lambda j: (0, j))
    return pl.BlockSpec((rows, cols), lambda j: (0, jnp.clip(j - start, 0, count - 1)))


def cost(flops, weights):
    return pl.CostEstimate(flops=int(flops), bytes_accessed=int(weights * 2), transcendentals=0)


def attn_forward(u, pieces, common):
    order, cos, sin, col, row = common
    n, (tokens, width) = len(pieces), u.shape
    steps = 3 * width // ATTN_TILE
    args = (u, *common)
    return pl.pallas_call(
        functools.partial(attn_forward_kernel, n, row.shape[0], steps),
        grid=(steps,),
        in_specs=[whole(a) for a in args]
        + columns(pieces, ATTN_TILE, lambda j: j)
        + columns(pieces, width, lambda j: 3)
        + columns(pieces, 128, lambda j: 4 * width // 128),
        out_specs=[
            fixed(tokens, width),
            pl.BlockSpec((1, tokens, ATTN_TILE), lambda j: (j, 0, 0)),
            fixed(tokens, 128),
            fixed(tokens, width),
            fixed(tokens, width),
            fixed(tokens, width),
        ],
        out_shape=[
            shape_of(tokens, width),
            jax.ShapeDtypeStruct((steps, tokens, ATTN_TILE), BF),
            shape_of(tokens, 128, F32),
            shape_of(tokens, width),
            shape_of(tokens, width, F32),
            shape_of(tokens, width),
        ],
        scratch_shapes=[pltpu.VMEM((steps, tokens, ATTN_TILE), BF), pltpu.VMEM((tokens, width), BF)],
        compiler_params=PARAMS,
        cost_estimate=cost(2 * tokens * 6 * width * width, 5 * width * width),
    )(*args, *pieces, *pieces, *pieces)


def mlp_forward(yn, h, pieces, pieces_d, order):
    n, (tokens, width) = len(pieces), yn.shape
    hidden = pieces_d[0].shape[1]
    steps = hidden // MLP_TILE
    args = (yn, h, order)
    return pl.pallas_call(
        functools.partial(mlp_forward_kernel, n, steps),
        grid=(steps,),
        in_specs=[whole(a) for a in args]
        + columns(pieces, MLP_TILE, lambda j: j)
        + columns(pieces, MLP_TILE, lambda j: steps + j)
        + columns(pieces_d, MLP_TILE, lambda j: j),
        out_specs=[tiled(tokens, MLP_TILE)] * 3 + [fixed(tokens, width)],
        out_shape=[shape_of(tokens, hidden)] * 3 + [shape_of(tokens, width)],
        scratch_shapes=[pltpu.VMEM((tokens, width), F32)],
        compiler_params=PARAMS,
        cost_estimate=cost(6 * tokens * hidden * width, 4 * hidden * width),
    )(*args, *pieces, *pieces, *pieces_d)


def mlp_backward(dzr, dz, h, one, two, pieces_a, pieces, pieces_d, order):
    n, (tokens, width) = len(pieces), dz.shape
    hidden = pieces_d[0].shape[1]
    steps = hidden // MLP_TILE
    args = (dzr, dz, h, order)
    return pl.pallas_call(
        functools.partial(mlp_backward_kernel, (len(pieces_a), n, len(pieces_d)), steps),
        grid=(steps,),
        in_specs=[whole(a) for a in args]
        + [tiled(tokens, MLP_TILE)] * 2
        + columns(pieces_a, 128, lambda j: 4 * width // 128)
        + columns(pieces, MLP_TILE, lambda j: j)
        + columns(pieces, MLP_TILE, lambda j: steps + j)
        + columns(pieces_d, MLP_TILE, lambda j: j),
        out_specs=[tiled(tokens, MLP_TILE)] * 2 + [fixed(tokens, width)] * 3,
        out_shape=[shape_of(tokens, hidden)] * 2
        + [shape_of(tokens, width, F32), shape_of(tokens, width), shape_of(tokens, width)],
        scratch_shapes=[pltpu.VMEM((tokens, width), F32)],
        compiler_params=PARAMS,
        cost_estimate=cost(6 * tokens * hidden * width, 4 * hidden * width),
    )(*args, one, two, *pieces_a, *pieces, *pieces, *pieces_d)


def attn_backward(da, dh, u, common, qkv, lse, pieces):
    n, (tokens, width) = len(pieces), u.shape
    steps = qkv.shape[0]
    args = (da, dh, u, *common, qkv, lse)
    return pl.pallas_call(
        functools.partial(attn_backward_kernel, n, common[-1].shape[0], steps),
        grid=(steps,),
        in_specs=[whole(a) for a in args]
        + columns(pieces, width, lambda j: 3)
        + columns(pieces, 128, lambda j: 4 * width // 128)
        + columns(pieces, ATTN_TILE, lambda j: j),
        out_specs=[tiled(tokens, ATTN_TILE), fixed(tokens, width), fixed(tokens, width)],
        out_shape=[shape_of(tokens, 3 * width), shape_of(tokens, width), shape_of(tokens, width)],
        scratch_shapes=[pltpu.VMEM((steps, tokens, ATTN_TILE), BF), pltpu.VMEM((tokens, width), F32)],
        compiler_params=PARAMS,
        cost_estimate=cost(2 * tokens * 6 * width * width, 6 * width * width),
    )(*args, *pieces, *pieces, *pieces)


def product_kernel(counts, sides, add_got, *refs):
    count = len(counts)
    lefts, rights, rest = refs[: count + sides], refs[count + sides : 2 * (count + sides)], refs[2 * (count + sides) :]
    got, rest = (rest[0], rest[1:]) if add_got else (None, rest)
    outs, turned = rest[:-1], rest[-1]
    step = pl.program_id(0)

    @pl.when(step == 0)
    def _():
        for k, left in enumerate(lefts):
            turned[k] = left[...].T

    begin = 0
    for which in range(count):

        @pl.when((step >= begin) & (step < begin + counts[which]))
        def _(which=which):
            value = dot(turned[which], rights[which][...])
            if sides:
                beside = sum(dot(turned[k], rights[k][...]) for k in range(count, count + sides))
                value = jnp.concatenate([value, beside], 1)
            if add_got:
                value = value + got[...].astype(F32)
            low = 0
            for out in outs:
                out[...] = value[low : low + out.shape[0]].astype(BF)
                low += out.shape[0]

        begin += counts[which]


def make_product(lefts, rights, tile, side_lefts=(), side_rights=()):
    tokens, width = lefts[0].shape
    half = width // 2
    counts = [r.shape[1] // tile for r in rights]
    steps = sum(counts)
    starts = [sum(counts[:k]) for k in range(len(counts))]
    every = (*lefts, *side_lefts)
    side = side_rights[0].shape[1] // steps if side_rights else 0
    out_tile = tile + side

    def product(part, got, sizes):
        add_got = got is not None
        return pl.pallas_call(
            functools.partial(product_kernel, counts, len(side_lefts), add_got),
            grid=(steps,),
            in_specs=[pl.BlockSpec((tokens, half), lambda j: (0, part)) for _ in every]
            + [tiled(tokens, tile, s, c) for s, c in zip(starts, counts)]
            + [tiled(tokens, side) for _ in side_rights]
            + ([tiled(half, out_tile)] if add_got else []),
            out_specs=[tiled(r, out_tile) for r in sizes],
            out_shape=[shape_of(r, steps * out_tile) for r in sizes],
            scratch_shapes=[pltpu.VMEM((len(every), half, tokens), BF)],
            compiler_params=PARAMS,
            cost_estimate=cost(2 * tokens * half * steps * out_tile, half * steps * out_tile * (2 if add_got else 1)),
        )(*every, *rights, *side_rights, *([got] if add_got else []))

    return product


def shards(tokens_in, attn_proj, attn_out, mlp_in, mlp_out, gain_attn, gain_mlp, lengths, cotangent):
    section = lax.axis_index("section")
    micro, slots, width = tokens_in.shape
    tokens = micro * slots
    three, hidden = attn_proj.shape[2], mlp_out.shape[2]
    padded = -(-hidden // MLP_TILE) * MLP_TILE
    gains = jnp.zeros((gain_attn.shape[1], GAIN_TILE), BF)
    gains = gains.at[:, 0].set(gain_attn[0]).at[:, 1].set(gain_mlp[0])
    gap = jnp.zeros((gain_attn.shape[1], padded - hidden), BF)
    pieces_a, pieces_m, pieces_d = gather(
        jnp.concatenate([attn_proj[0], attn_out[0], gains], 1),
        jnp.concatenate([mlp_in[0, :, :hidden], gap, mlp_in[0, :, hidden:], gap], 1),
        jnp.concatenate([mlp_out[0], gap], 1),
    )
    order = relative_order(lax.axis_index("fsdp"), False)
    order_d = relative_order(lax.axis_index("fsdp"), True)
    base = jnp.where(section == 0, 10000.0, 160000.0).astype(F32)
    reach = jnp.where(section == 0, WINDOW / 2.0, 4.0 * slots).astype(F32)
    segment, inner = segment_info(lengths[:, 0], slots)
    half = HEAD_DIM // 2
    freqs = jnp.exp(-jnp.log(base) * (jnp.arange(half, dtype=F32) * (2.0 / HEAD_DIM)))
    angles = jnp.tile(inner.reshape(tokens, 1).astype(F32) * freqs, (1, 128 // half))
    col = jnp.stack([segment.reshape(tokens).astype(F32), inner.reshape(tokens).astype(F32)], 1)
    col = jnp.concatenate([col, jnp.broadcast_to(reach, (tokens, 126))], 1)
    row = jnp.stack([segment, inner] + [inner] * 6, 1).astype(F32)
    common = (order, jnp.cos(angles), jnp.sin(angles), col, row)

    first_in = tokens_in.reshape(tokens, width)
    _, _, _, _, hid, yn = attn_forward(first_in, pieces_a, common)
    middle_out = mlp_forward(yn, hid, pieces_m, pieces_d, order_d)[3]
    received = lax.ppermute(middle_out, "section", [(0, 1)])
    layer_in = jnp.where(section == 0, first_in, received)
    xn, qkv, lse, attended, hid, yn = attn_forward(layer_in, pieces_a, common)
    mid, one, two, result = mlp_forward(yn, hid, pieces_m, pieces_d, order_d)

    def backward_mlp(grad):
        rel = dot(grad, order_d).astype(BF)
        return rel, mlp_backward(rel, grad, hid, one, two, pieces_a, pieces_m, pieces_d, order)

    last_grad = cotangent.reshape(tokens, width)
    _, _, dh, da, _ = backward_mlp(last_grad)[1]
    middle_grad = attn_backward(da, dh, layer_in, common, qkv, lse, pieces_a)[1]
    received = lax.ppermute(middle_grad, "section", [(1, 0)])
    grad_out = jnp.where(section == 1, last_grad, received)
    half = width // 2
    dzr = dot(grad_out, order_d).astype(BF)
    product = make_product((dzr,), (mid,), MLP_TILE)
    sent_d, grad_out = tie(product(1, None, (half,))[0], grad_out)
    got_d = send(sent_d, "core")
    dg, dv, dh, da, term_m = mlp_backward(dzr, grad_out, hid, one, two, pieces_a, pieces_m, pieces_d, order)
    got_d, dg, dv, da = tie(got_d, dg, dv, da)
    parts_d = product(0, got_d, (half // 2, half // 2))
    *parts_d, da = tie(*parts_d, da)
    product = make_product((yn, yn), (dg, dv), padded, (attended,), (da,))
    sent_m, da = tie(product(1, None, (half,))[0], da)
    got_m = send(sent_m, "core")
    dqkv, grad_in, term_a = attn_backward(da, dh, layer_in, common, qkv, lse, pieces_a)
    got_m, dqkv, grad_in = tie(got_m, dqkv, grad_in)
    parts_m = product(0, got_m, cut(half))
    *parts_m, dqkv = tie(*parts_m, dqkv)
    lane = lax.broadcasted_iota(jnp.int32, (tokens, 2 * GAIN_TILE), 1)
    picks = ((lane == 0).astype(BF), (lane == 1).astype(BF))
    product = make_product((xn,), (dqkv,), three // 2, (term_a, term_m), picks)
    got_a = send(product(1, None, (half,))[0], "core")
    sum_d = finish_z_first(*parts_d)
    sum_m = finish(*parts_m)
    sum_a = finish(*product(0, got_a, cut(half)))
    part = three // 2
    edge = part + GAIN_TILE
    grad_proj = jnp.concatenate([sum_a[:, :part], sum_a[:, edge : edge + part]], 1)
    side = padded + width // 2
    grad_out_proj = jnp.concatenate([sum_m[:, padded:side], sum_m[:, side + padded :]], 1)
    grad_up = jnp.concatenate([sum_m[:, :hidden], sum_m[:, side : side + hidden]], 1)
    return (
        result.reshape(1, micro, slots, width),
        grad_in.reshape(1, micro, slots, width),
        grad_proj[None],
        grad_out_proj[None],
        grad_up[None],
        sum_d[:, :hidden][None],
        sum_a[:, part][None],
        sum_a[:, part + 1][None],
    )


def solution(mesh):
    in_specs = (
        P(None, "fsdp", None),
        P("section", "fsdp", None),
        P("section", "fsdp", None),
        P("section", "fsdp", None),
        P("section", "fsdp", None),
        P("section", "fsdp"),
        P("section", "fsdp"),
        P(None, "fsdp", None),
        P(None, "fsdp", None),
    )
    out_specs = (
        P("section", None, "fsdp", None),
        P("section", None, "fsdp", None),
        P("section", "fsdp", None),
        P("section", "fsdp", None),
        P("section", "fsdp", None),
        P("section", "fsdp", None),
        P("section", "fsdp"),
        P("section", "fsdp"),
    )
    return jax.shard_map(shards, mesh=mesh, in_specs=in_specs, out_specs=out_specs, check_vma=False)
```

```python
import functools
import math
import jax
import jax.numpy as jnp
from jax import lax
from jax.experimental import pallas as pl
from jax.experimental.pallas import tpu as pltpu
from jax.sharding import PartitionSpec as P

HEADS = 16
HEAD_DIM = 64
WINDOW = 128
EPS = 1e-05
NY, NX, NZ, NC = 4, 4, 2, 2
SHARDS = NY * NX * NZ * NC
BF = jnp.bfloat16
F32 = jnp.float32
ATTN_TILE = 1024
MLP_TILE = 896
GAIN_TILE = 128
GROUP = 8
SCALE = HEAD_DIM**-0.5
PARAMS = pltpu.CompilerParams(vmem_limit_bytes=56 * 1024 * 1024)


def split_index(i):
    return i // (NX * NZ * NC), (i // (NZ * NC)) % NX, (i // NC) % NZ, i % NC


def join_index(y, x, z, c):
    return ((y * NX + x) * NZ + z) * NC + c


def pairs(kind, step=1):
    out = []
    for i in range(SHARDS):
        y, x, z, c = split_index(i)
        if kind == "core":
            c = 1 - c
        elif kind == "z":
            z = 1 - z
        elif (kind == "first") == (c == 0):
            y = (y + step) % NY
        else:
            x = (x + step) % NX
        out.append((i, join_index(y, x, z, c)))
    return out


def send(value, kind, step=1):
    return lax.ppermute(value, "fsdp", pairs(kind, step))


def tie(*values):
    return lax.optimization_barrier(values)


def rows(*blocks):
    return jnp.concatenate(blocks, 0)


def spread(block):
    return rows(block, send(block, "second", -1), send(block, "second", 2), send(block, "second", 1))


def near(block):
    return send(block, "first", -1), send(block, "first", 1)


def far(after, before):
    half = after.shape[0] // 2
    return send(after[:half], "first", -1), send(before[half:], "first", 1)


def core(*pieces):
    return tuple(send(piece, "core") for piece in pieces)


def gather(a, m):
    a_z, m = tie(send(a, "z"), m)
    a, m_z = tie(spread(rows(a, a_z)), send(m, "z"))
    a_after, a_before = near(a)
    m = spread(rows(m, m_z))
    a_far, a_far2 = far(a_after, a_before)
    a_far, a_far2, m = tie(a_far, a_far2, m)
    a = (a, a_after, a_far, a_far2, a_before)
    return a + core(*a), (m, *near(m))


def add(left, right):
    return left.astype(F32) + right.astype(F32)


def cut(size):
    quarter = size // 4
    return quarter, quarter, quarter // 2, quarter // 2, quarter


def split(block, sizes):
    edges = [sum(sizes[:k]) for k in range(len(sizes) + 1)]
    return tuple(block[low:high] for low, high in zip(edges[:-1], edges[1:]))


def ring_start(parts, got):
    return tuple(add(part, other) for part, other in zip(parts, split(got, cut(got.shape[0]))))


def ring_mix(after, before, got_a, got_b):
    half = got_a.shape[0]
    after = rows(after[:half] + got_a.astype(F32), after[half:])
    before = rows(before[:half], before[half:] + got_b.astype(F32))
    return after.astype(BF), before.astype(BF)


def ring_close(here, got_c, got_d):
    return (here + got_c.astype(F32) + got_d.astype(F32)).astype(BF)


def direct(block):
    size = block.shape[0] // 4
    here, after, far, before = (block[k * size : (k + 1) * size] for k in range(4))
    return here, send(after, "second", 1), send(far, "second", 2), send(before, "second", -1)


def close_z(here, *got):
    block = (add(here, got[0]) + add(got[1], got[2])).astype(BF)
    mine = block.shape[0] // 2
    return add(block[:mine], send(block[mine:], "z"))


def relative_order(me):
    y, x, z, c = split_index(me)
    place = jnp.arange(SHARDS * 16, dtype=jnp.int32)
    block, inside = place // 16, place % 16
    core_at = c ^ (block // 32)
    first, second = (block // 8) % 4, (block // 2) % 4
    row_y = (y + jnp.where(core_at == 0, first, second)) % NY
    row_x = (x + jnp.where(core_at == 0, second, first)) % NX
    absolute = join_index(row_y, row_x, z ^ (block % 2), core_at) * 16 + inside
    return (place[:, None] == absolute[None, :]).astype(BF)


def dot(left, right):
    return jnp.dot(left, right, preferred_element_type=F32)


def contract_last(left, right):
    return lax.dot_general(left, right, (((1,), (1,)), ((), ())), preferred_element_type=F32)


def contract_first(left, right):
    return lax.dot_general(left, right, (((0,), (0,)), ((), ())), preferred_element_type=F32)


def normal(values):
    centre = jnp.mean(values, -1, keepdims=True)
    centred = values - centre
    scale = lax.rsqrt(jnp.mean(centred * centred, -1, keepdims=True) + EPS)
    return centred * scale, scale


def normal_back(grad, unit, scale):
    return scale * (
        grad
        - jnp.mean(grad, -1, keepdims=True)
        - unit * jnp.mean(grad * unit, -1, keepdims=True)
    )


def segment_info(lens, count):
    ends = jnp.cumsum(lens, axis=-1)
    starts = ends - lens
    places = jnp.arange(count, dtype=jnp.int32)
    segment = jnp.sum((places[:, None] >= ends[..., None, :]).astype(jnp.int32), axis=-1)
    picked = (segment[..., None] == jnp.arange(lens.shape[-1], dtype=jnp.int32)).astype(jnp.int32)
    inner = places - jnp.sum(picked * starts[..., None, :], axis=-1)
    return segment, inner


def to_absolute(values, order):
    high = values.astype(BF)
    low = (values - high.astype(F32)).astype(BF)
    return contract_last(high, order) + contract_last(low, order)


def stack_rows(refs):
    return jnp.concatenate([ref[...] for ref in refs], 0)


def gain_rows(refs):
    row = lax.broadcasted_iota(jnp.int32, (16, 128), 0)
    lane = lax.broadcasted_iota(jnp.int32, (16, 128), 1)
    return contract_last((row == lane).astype(BF), stack_rows(refs))


def partner(values):
    width = values.shape[1]
    lane = lax.broadcasted_iota(jnp.int32, values.shape, 1)
    ahead = pltpu.roll(values, width - HEAD_DIM // 2, 1)
    behind = pltpu.roll(values, HEAD_DIM // 2, 1)
    return jnp.where(lane % HEAD_DIM < HEAD_DIM // 2, -ahead, behind)


def widen(table, width):
    return jnp.concatenate([table] * (width // table.shape[1]), 1)


def pair_bias(col, row):
    same = col[:, 0:1] == row[0:1]
    near = jnp.abs(col[:, 1:2] - row[1:2]) <= col[:, 2:3]
    return jnp.where(same & near, 0.0, -1e30)


def head_of(qkv, part, head, rows):
    return qkv[part, rows, head * HEAD_DIM : (head + 1) * HEAD_DIM]


def attn_forward_kernel(n, micro, steps, *refs):
    u, order, cos, sin, col, row = refs[:6]
    proj, out, gains = refs[6 : 6 + n], refs[6 + n : 6 + 2 * n], refs[6 + 2 * n : 6 + 3 * n]
    xn_out, qkv_out, lse_out, o_out, h_out, yn_out, qkv, xn = refs[6 + 3 * n :]
    step = pl.program_id(0)

    @pl.when(step == 0)
    def _():
        unit, _ = normal(dot(u[...], order[...]))
        xn[...] = (unit * gain_rows(gains)[0:1]).astype(BF)
        xn_out[...] = xn[...]

    packed = dot(xn[...], stack_rows(proj))

    @pl.when(step < steps * 2 // 3)
    def _():
        turned = packed * widen(cos[...], ATTN_TILE) + partner(packed) * widen(sin[...], ATTN_TILE)
        qkv[step] = turned.astype(BF)

    @pl.when(step >= steps * 2 // 3)
    def _():
        qkv[step] = packed.astype(BF)

    qkv_out[0] = qkv[step]

    @pl.when(step == steps - 1)
    def _():
        slots = u.shape[0] // micro
        lane = lax.broadcasted_iota(jnp.int32, (slots, 128), 1)
        blocks = []
        for m in range(micro):
            rows = slice(m * slots, (m + 1) * slots)
            bias = pair_bias(col[rows], row[m])
            log_all = jnp.zeros((slots, 128), F32)
            heads = []
            for low in range(0, HEADS, GROUP):
                group = range(low, low + GROUP)
                scores = [contract_last(head_of(qkv, 0, k, rows), head_of(qkv, 1, k, rows)) * SCALE + bias for k in group]
                peaks = [jnp.max(x, -1, keepdims=True) for x in scores]
                scores = [jnp.exp(x - p) for x, p in zip(scores, peaks)]
                totals = [jnp.sum(x, -1, keepdims=True) for x in scores]
                for k, p, t in zip(group, peaks, totals):
                    log_all = jnp.where(lane == k, p + jnp.log(t), log_all)
                probs = [(x * (1.0 / t)).astype(BF) for x, t in zip(scores, totals)]
                heads += [dot(x, head_of(qkv, 2, k, rows)).astype(BF) for k, x in zip(group, probs)]
            lse_out[rows] = log_all
            blocks.append(jnp.concatenate(heads, 1))
        attended = dot(jnp.concatenate(blocks, 0), order[...]).astype(BF)
        o_out[...] = attended
        hidden = u[...].astype(F32) + dot(attended, stack_rows(out))
        h_out[...] = hidden
        unit, _ = normal(hidden)
        gain = contract_last(gain_rows(gains).astype(BF), order[...])[1:2]
        yn_out[...] = dot((unit * gain).astype(BF), order[...]).astype(BF)


def mlp_forward_kernel(n, steps, *refs):
    yn, h, order = refs[:3]
    gate, up, down = refs[3 : 3 + n], refs[3 + n : 3 + 2 * n], refs[3 + 2 * n : -5]
    mid_out, one_out, two_out, z_out, total = refs[-5:]
    step = pl.program_id(0)
    g = dot(yn[...], stack_rows(gate))
    v = dot(yn[...], stack_rows(up))
    cdf = 0.5 * (1.0 + lax.erf(g * math.sqrt(0.5)))
    slope = cdf + g * jnp.exp(-0.5 * g * g) * (1.0 / math.sqrt(2.0 * math.pi))
    unit = g * cdf
    mid = (unit * v).astype(BF)
    mid_out[...] = mid
    one_out[...] = (v * slope).astype(BF)
    two_out[...] = unit.astype(BF)
    part = contract_last(mid, stack_rows(down))

    @pl.when(step == 0)
    def _():
        total[...] = part

    @pl.when(step > 0)
    def _():
        total[...] += part

    @pl.when(step == steps - 1)
    def _():
        z_out[...] = (h[...] + to_absolute(total[...], order[...])).astype(BF)


def mlp_backward_kernel(n, steps, *refs):
    dzr, dz, h, order, one, two = refs[:6]
    gains, gate, up, down = (refs[6 + k * n : 6 + (k + 1) * n] for k in range(4))
    dg_out, dv_out, dh_out, da_out, term_out, total = refs[6 + 4 * n :]
    step = pl.program_id(0)

    @pl.when(step == 0)
    def _():
        total[...] = jnp.zeros_like(total)

    dmid = dot(dzr[...], stack_rows(down))
    dg = (dmid * one[...].astype(F32)).astype(BF)
    dv = (dmid * two[...].astype(F32)).astype(BF)
    dg_out[...] = dg
    dv_out[...] = dv
    total[...] += contract_last(dg, stack_rows(gate)) + contract_last(dv, stack_rows(up))

    @pl.when(step == steps - 1)
    def _():
        dyn = to_absolute(total[...], order[...])
        unit, scale = normal(h[...])
        gain = contract_last(gain_rows(gains).astype(BF), order[...])[1:2]
        term_out[...] = dot((dyn * unit).astype(BF), order[...]).astype(BF)
        dh = dz[...].astype(F32) + normal_back(dyn * gain, unit, scale)
        dh_out[...] = dh
        da_out[...] = dh.astype(BF)


def heads_backward_kernel(n, micro, *refs):
    da, order, cos, sin, col, row, qkv, lse = refs[:8]
    out, dqkv = refs[8 : 8 + n], refs[8 + n]
    tokens, width = da.shape
    rel = contract_last(da[...], stack_rows(out)).astype(BF)
    do_all = contract_last(rel, order[...]).astype(BF)
    slots = tokens // micro
    for m in range(micro):
        at = slice(m * slots, (m + 1) * slots)
        bias = pair_bias(col[at], row[m])
        log_all = lse[at]
        cosine, sine = widen(cos[at], width), widen(sin[at], width)
        dqs, dks, dvs = [], [], []
        for low in range(0, HEADS, GROUP):
            group = range(low, low + GROUP)
            qs, ks, vs = ([head_of(qkv, part, k, at) for k in group] for part in range(3))
            ds = [do_all[at, k * HEAD_DIM : (k + 1) * HEAD_DIM] for k in group]
            probs = [contract_last(q, k) * SCALE + bias for q, k in zip(qs, ks)]
            probs = [jnp.exp(x - log_all[:, k : k + 1]) for x, k in zip(probs, group)]
            dps = [contract_last(d, v) for d, v in zip(ds, vs)]
            dss = [(p * (x - jnp.sum(p * x, -1, keepdims=True))).astype(BF) for p, x in zip(probs, dps)]
            dvs += [contract_first(p.astype(BF), d) for p, d in zip(probs, ds)]
            dqs += [dot(x, k) for x, k in zip(dss, ks)]
            dks += [contract_first(x, q) for x, q in zip(dss, qs)]
        dq, dk = (jnp.concatenate(x, 1) * SCALE for x in (dqs, dks))
        dqkv[at, :width] = (dq * cosine - partner(dq) * sine).astype(BF)
        dqkv[at, width : 2 * width] = (dk * cosine - partner(dk) * sine).astype(BF)
        dqkv[at, 2 * width :] = jnp.concatenate(dvs, 1).astype(BF)


def qkv_backward_kernel(n, steps, *refs):
    dqkv, dh, u, order = refs[:4]
    gains, proj = refs[4 : 4 + n], refs[4 + n : 4 + 2 * n]
    du_out, term_out, total = refs[4 + 2 * n :]
    step = pl.program_id(0)

    @pl.when(step == 0)
    def _():
        total[...] = jnp.zeros_like(total)

    total[...] += contract_last(dqkv[...], stack_rows(proj))

    @pl.when(step == steps - 1)
    def _():
        unit, scale = normal(dot(u[...], order[...]))
        dxn = total[...]
        term_out[...] = (dxn * unit).astype(BF)
        back = normal_back(dxn * gain_rows(gains)[0:1], unit, scale)
        du_out[...] = (dh[...] + to_absolute(back, order[...])).astype(BF)


def columns(pieces, tile, place):
    return [pl.BlockSpec((p.shape[0], tile), lambda j: (0, place(j))) for p in pieces]


def whole(array):
    return pl.BlockSpec(array.shape, lambda j: (0,) * array.ndim)


def shape_of(rows, cols, kind=BF):
    return jax.ShapeDtypeStruct((rows, cols), kind)


def fixed(rows, cols):
    return pl.BlockSpec((rows, cols), lambda j: (0, 0))


def tiled(rows, cols, start=0, count=None):
    if count is None:
        return pl.BlockSpec((rows, cols), lambda j: (0, j))
    return pl.BlockSpec((rows, cols), lambda j: (0, jnp.clip(j - start, 0, count - 1)))


def cost(flops, weights):
    return pl.CostEstimate(flops=int(flops) // 64, bytes_accessed=int(weights * 2) // 64, transcendentals=0)


def attn_forward(u, pieces, common):
    order, cos, sin, col, row = common
    n, (tokens, width) = len(pieces), u.shape
    steps = 3 * width // ATTN_TILE
    args = (u, *common)
    return pl.pallas_call(
        functools.partial(attn_forward_kernel, n, row.shape[0], steps),
        grid=(steps,),
        in_specs=[whole(a) for a in args]
        + columns(pieces, ATTN_TILE, lambda j: j)
        + columns(pieces, width, lambda j: 3)
        + columns(pieces, 128, lambda j: 4 * width // 128),
        out_specs=[
            fixed(tokens, width),
            pl.BlockSpec((1, tokens, ATTN_TILE), lambda j: (j, 0, 0)),
            fixed(tokens, 128),
            fixed(tokens, width),
            fixed(tokens, width),
            fixed(tokens, width),
        ],
        out_shape=[
            shape_of(tokens, width),
            jax.ShapeDtypeStruct((steps, tokens, ATTN_TILE), BF),
            shape_of(tokens, 128, F32),
            shape_of(tokens, width),
            shape_of(tokens, width, F32),
            shape_of(tokens, width),
        ],
        scratch_shapes=[pltpu.VMEM((steps, tokens, ATTN_TILE), BF), pltpu.VMEM((tokens, width), BF)],
        compiler_params=PARAMS,
        cost_estimate=cost(2 * tokens * 6 * width * width, 5 * width * width),
    )(*args, *pieces, *pieces, *pieces)


def mlp_forward(yn, h, pieces, order):
    n, (tokens, width) = len(pieces), yn.shape
    hidden = pieces[0].shape[1] // 3
    steps = hidden // MLP_TILE
    args = (yn, h, order)
    return pl.pallas_call(
        functools.partial(mlp_forward_kernel, n, steps),
        grid=(steps,),
        in_specs=[whole(a) for a in args]
        + columns(pieces, MLP_TILE, lambda j: j)
        + columns(pieces, MLP_TILE, lambda j: steps + j)
        + columns(pieces, MLP_TILE, lambda j: 2 * steps + j),
        out_specs=[tiled(tokens, MLP_TILE)] * 3 + [fixed(tokens, width)],
        out_shape=[shape_of(tokens, hidden)] * 3 + [shape_of(tokens, width)],
        scratch_shapes=[pltpu.VMEM((tokens, width), F32)],
        compiler_params=PARAMS,
        cost_estimate=cost(6 * tokens * hidden * width, 4 * hidden * width),
    )(*args, *pieces, *pieces, *pieces)


def mlp_backward(dzr, dz, h, one, two, pieces_a, pieces, order):
    n, (tokens, width) = len(pieces), dz.shape
    hidden = pieces[0].shape[1] // 3
    steps = hidden // MLP_TILE
    args = (dzr, dz, h, order)
    return pl.pallas_call(
        functools.partial(mlp_backward_kernel, n, steps),
        grid=(steps,),
        in_specs=[whole(a) for a in args]
        + [tiled(tokens, MLP_TILE)] * 2
        + columns(pieces_a, 128, lambda j: 4 * width // 128)
        + columns(pieces, MLP_TILE, lambda j: j)
        + columns(pieces, MLP_TILE, lambda j: steps + j)
        + columns(pieces, MLP_TILE, lambda j: 2 * steps + j),
        out_specs=[tiled(tokens, MLP_TILE)] * 2 + [fixed(tokens, width)] * 3,
        out_shape=[shape_of(tokens, hidden)] * 2
        + [shape_of(tokens, width, F32), shape_of(tokens, width), shape_of(tokens, width)],
        scratch_shapes=[pltpu.VMEM((tokens, width), F32)],
        compiler_params=PARAMS,
        cost_estimate=cost(6 * tokens * hidden * width, 4 * hidden * width),
    )(*args, one, two, *pieces_a, *pieces, *pieces, *pieces)


def heads_backward(da, common, qkv, lse, pieces):
    n, (tokens, width) = len(pieces), da.shape
    args = (da, *common, qkv, lse)
    return pl.pallas_call(
        functools.partial(heads_backward_kernel, n, common[-1].shape[0]),
        grid=(1,),
        in_specs=[whole(a) for a in args] + columns(pieces, width, lambda j: 3),
        out_specs=fixed(tokens, 3 * width),
        out_shape=shape_of(tokens, 3 * width),
        compiler_params=PARAMS,
        cost_estimate=cost(2 * tokens * width * width, width * width),
    )(*args, *pieces)


def qkv_backward(dqkv, dh, u, order, pieces):
    n, (tokens, width) = len(pieces), u.shape
    steps = 3 * width // ATTN_TILE
    args = (dh, u, order)
    return pl.pallas_call(
        functools.partial(qkv_backward_kernel, n, steps),
        grid=(steps,),
        in_specs=[tiled(tokens, ATTN_TILE)]
        + [whole(a) for a in args]
        + columns(pieces, 128, lambda j: 4 * width // 128)
        + columns(pieces, ATTN_TILE, lambda j: j),
        out_specs=[fixed(tokens, width), fixed(tokens, width)],
        out_shape=[shape_of(tokens, width), shape_of(tokens, width)],
        scratch_shapes=[pltpu.VMEM((tokens, width), F32)],
        compiler_params=PARAMS,
        cost_estimate=cost(2 * tokens * 3 * width * width, 3 * width * width),
    )(dqkv, *args, *pieces, *pieces)


def product_kernel(counts, sides, *refs):
    count = len(counts)
    lefts, rights, rest = refs[: count + sides], refs[count + sides : 2 * (count + sides)], refs[2 * (count + sides) :]
    outs, turned = rest[:-1], rest[-1]
    step = pl.program_id(0)

    @pl.when(step == 0)
    def _():
        for k, left in enumerate(lefts):
            turned[k] = left[...].T

    begin = 0
    for which in range(count):

        @pl.when((step >= begin) & (step < begin + counts[which]))
        def _(which=which):
            value = dot(turned[which], rights[which][...])
            if sides:
                beside = sum(dot(turned[k], rights[k][...]) for k in range(count, count + sides))
                value = jnp.concatenate([value, beside], 1)
            low = 0
            for out in outs:
                out[...] = value[low : low + out.shape[0]].astype(BF)
                low += out.shape[0]

        begin += counts[which]


def make_product(lefts, rights, tile, side_lefts=(), side_rights=()):
    tokens, width = lefts[0].shape
    counts = [r.shape[1] // tile for r in rights]
    steps = sum(counts)
    starts = [sum(counts[:k]) for k in range(len(counts))]
    every = (*lefts, *side_lefts)
    side = side_rights[0].shape[1] // steps if side_rights else 0
    out_tile = tile + side

    def product(part, sizes):
        span = sum(sizes)
        return pl.pallas_call(
            functools.partial(product_kernel, counts, len(side_lefts)),
            grid=(steps,),
            in_specs=[pl.BlockSpec((tokens, span), lambda j: (0, part)) for _ in every]
            + [tiled(tokens, tile, s, c) for s, c in zip(starts, counts)]
            + [tiled(tokens, side) for _ in side_rights],
            out_specs=[tiled(r, out_tile) for r in sizes],
            out_shape=[shape_of(r, steps * out_tile) for r in sizes],
            scratch_shapes=[pltpu.VMEM((len(every), span, tokens), BF)],
            compiler_params=PARAMS,
            cost_estimate=cost(2 * tokens * span * steps * out_tile, span * steps * out_tile),
        )(*every, *rights, *side_rights)

    return product


def shards(tokens_in, attn_proj, attn_out, mlp_in, mlp_out, gain_attn, gain_mlp, lengths, cotangent):
    section = lax.axis_index("section")
    micro, slots, width = tokens_in.shape
    tokens = micro * slots
    three, hidden = attn_proj.shape[2], mlp_out.shape[2]
    padded = -(-hidden // MLP_TILE) * MLP_TILE
    gains = jnp.zeros((gain_attn.shape[1], GAIN_TILE), BF)
    gains = gains.at[:, 0].set(gain_attn[0]).at[:, 1].set(gain_mlp[0])
    gap = jnp.zeros((gain_attn.shape[1], padded - hidden), BF)
    pieces_a, pieces_m = gather(
        jnp.concatenate([attn_proj[0], attn_out[0], gains], 1),
        jnp.concatenate([mlp_in[0, :, :hidden], gap, mlp_in[0, :, hidden:], gap, mlp_out[0], gap], 1),
    )
    order = relative_order(lax.axis_index("fsdp"))
    base = jnp.where(section == 0, 10000.0, 160000.0).astype(F32)
    reach = jnp.where(section == 0, WINDOW / 2.0, 4.0 * slots).astype(F32)
    segment, inner = segment_info(lengths[:, 0], slots)
    half = HEAD_DIM // 2
    freqs = jnp.exp(-jnp.log(base) * (jnp.arange(half, dtype=F32) * (2.0 / HEAD_DIM)))
    angles = jnp.tile(inner.reshape(tokens, 1).astype(F32) * freqs, (1, 128 // half))
    col = jnp.stack([segment.reshape(tokens).astype(F32), inner.reshape(tokens).astype(F32)], 1)
    col = jnp.concatenate([col, jnp.broadcast_to(reach, (tokens, 126))], 1)
    row = jnp.stack([segment, inner] + [inner] * 6, 1).astype(F32)
    common = (order, jnp.cos(angles), jnp.sin(angles), col, row)

    first_in = tokens_in.reshape(tokens, width)
    _, _, _, _, hid, yn = attn_forward(first_in, pieces_a, common)
    m_block, m_near, m_near2 = pieces_m
    m_near, m_near2, yn = tie(m_near, m_near2, yn)
    m_far, m_far2 = far(m_near, m_near2)
    near_core = core(m_block, m_near, m_near2)
    far_core = core(m_far, m_far2)
    pieces_m = (m_block, m_near, m_far, m_far2, m_near2, *near_core[:2], *far_core, near_core[2])
    middle_out = mlp_forward(yn, hid, pieces_m, order)[3]
    received = lax.ppermute(middle_out, "section", [(0, 1)])
    layer_in = jnp.where(section == 0, first_in, received)
    xn, qkv, lse, attended, hid, yn = attn_forward(layer_in, pieces_a, common)
    mid, one, two, result = mlp_forward(yn, hid, pieces_m, order)

    def backward_mlp(grad):
        rel = dot(grad, order).astype(BF)
        return mlp_backward(rel, grad, hid, one, two, pieces_a, pieces_m, order)

    last_grad = cotangent.reshape(tokens, width)
    _, _, dh, da, _ = backward_mlp(last_grad)
    dqkv = heads_backward(da, common, qkv, lse, pieces_a)
    middle_grad = qkv_backward(dqkv, dh, layer_in, order, pieces_a)[0]
    received = lax.ppermute(middle_grad, "section", [(1, 0)])
    grad_out = jnp.where(section == 1, last_grad, received)
    half = width // 2
    dzr = dot(grad_out, order).astype(BF)
    dg, dv, dh, da, term_m = mlp_backward(dzr, grad_out, hid, one, two, pieces_a, pieces_m, order)
    product = make_product((yn, yn, dzr), (dg, dv, mid), MLP_TILE)
    sent_m, yn = tie(product(1, (half,))[0], yn)
    got_m = send(sent_m, "core")
    product = make_product((yn, yn, dzr), (dg, dv, mid), MLP_TILE)
    own_m = product(0, cut(half))
    here_m, after_m, far_m, far_m2, before_m = ring_start(own_m, got_m)
    far_m, far_m2 = send(far_m.astype(BF), "first", 1), send(far_m2.astype(BF), "first", -1)
    dqkv = heads_backward(da, common, qkv, lse, pieces_a)
    far_m, far_m2, dqkv = tie(far_m, far_m2, dqkv)
    *mix_m, dqkv = tie(*ring_mix(after_m, before_m, far_m, far_m2), dqkv)
    near_m = send(mix_m[0], "first", 1), send(mix_m[1], "first", -1)
    grad_in, term_a = qkv_backward(dqkv, dh, layer_in, order, pieces_a)
    lane = lax.broadcasted_iota(jnp.int32, (tokens, 4 * GAIN_TILE), 1)
    picks = ((lane == 0).astype(BF), (lane == 1).astype(BF))
    product = make_product((xn, attended), (dqkv, da), width, (term_a, term_m), picks)
    *own_a, sent_a = product(0, (*cut(half), half))
    got_a = send(sent_a, "core")
    here_a, after_a, far_a, far_a2, before_a = ring_start(own_a, got_a)
    ends_m = direct(ring_close(here_m, *near_m))
    far_a, far_a2 = send(far_a.astype(BF), "first", 1), send(far_a2.astype(BF), "first", -1)
    mix_a = ring_mix(after_a, before_a, far_a, far_a2)
    *ends_m, mix_a, mix_a2 = tie(*ends_m, *mix_a)
    near_a = send(mix_a, "first", 1), send(mix_a2, "first", -1)
    sum_m = close_z(*ends_m)
    sum_a = close_z(*direct(ring_close(here_a, *near_a)))
    edge = width + GAIN_TILE
    grad_proj = jnp.concatenate([sum_a[:, k * edge : k * edge + width] for k in range(3)], 1)
    grad_up = jnp.concatenate([sum_m[:, :hidden], sum_m[:, padded : padded + hidden]], 1)
    return (
        result.reshape(1, micro, slots, width),
        grad_in.reshape(1, micro, slots, width),
        grad_proj[None],
        sum_a[:, 3 * edge : 3 * edge + width][None],
        grad_up[None],
        sum_m[:, 2 * padded : 2 * padded + hidden][None],
        sum_a[:, width][None],
        sum_a[:, width + 1][None],
    )


def solution(mesh):
    in_specs = (
        P(None, "fsdp", None),
        P("section", "fsdp", None),
        P("section", "fsdp", None),
        P("section", "fsdp", None),
        P("section", "fsdp", None),
        P("section", "fsdp"),
        P("section", "fsdp"),
        P(None, "fsdp", None),
        P(None, "fsdp", None),
    )
    out_specs = (
        P("section", None, "fsdp", None),
        P("section", None, "fsdp", None),
        P("section", "fsdp", None),
        P("section", "fsdp", None),
        P("section", "fsdp", None),
        P("section", "fsdp", None),
        P("section", "fsdp"),
        P("section", "fsdp"),
    )
    return jax.shard_map(shards, mesh=mesh, in_specs=in_specs, out_specs=out_specs, check_vma=False)
```

```python
import functools
import math
import jax
import jax.numpy as jnp
from jax import lax
from jax.experimental import pallas as pl
from jax.experimental.pallas import tpu as pltpu
from jax.sharding import PartitionSpec as P

HEADS = 16
HEAD_DIM = 64
WINDOW = 128
EPS = 1e-05
NY, NX, NZ, NC = 4, 4, 2, 2
SHARDS = NY * NX * NZ * NC
BF = jnp.bfloat16
F32 = jnp.float32
ATTN_TILE = 1024
MLP_TILE = 896
GAIN_TILE = 128
GROUP = 8
SCALE = HEAD_DIM**-0.5
PARAMS = pltpu.CompilerParams(vmem_limit_bytes=56 * 1024 * 1024)


def split_index(i):
    return i // (NX * NZ * NC), (i // (NZ * NC)) % NX, (i // NC) % NZ, i % NC


def join_index(y, x, z, c):
    return ((y * NX + x) * NZ + z) * NC + c


def pairs(kind, step=1):
    out = []
    for i in range(SHARDS):
        y, x, z, c = split_index(i)
        if kind == "core":
            c = 1 - c
        elif kind == "z":
            z = 1 - z
        elif (kind == "first") == (c == 0):
            y = (y + step) % NY
        else:
            x = (x + step) % NX
        out.append((i, join_index(y, x, z, c)))
    return out


def send(value, kind, step=1):
    return lax.ppermute(value, "fsdp", pairs(kind, step))


def tie(*values):
    return lax.optimization_barrier(values)


def rows(*blocks):
    return jnp.concatenate(blocks, 0)


def spread(block):
    return rows(block, send(block, "second", -1), send(block, "second", 2), send(block, "second", 1))


def near(block):
    return send(block, "first", -1), send(block, "first", 1)


def far(after, before):
    half = after.shape[0] // 2
    return send(after[:half], "first", -1), send(before[half:], "first", 1)


def core(*pieces):
    return tuple(send(piece, "core") for piece in pieces)


def gather(a, m, order):
    a_z, m = tie(send(a, "z"), m)
    a, m_z, order = tie(spread(rows(a, a_z)), send(m, "z"), order)
    a_after, a_before = near(a)
    m = spread(rows(m, m_z))
    a_far, a_far2 = far(a_after, a_before)
    a_far, a_far2, m = tie(a_far, a_far2, m)
    a = (a, a_after, a_far, a_far2, a_before)
    return a + core(*a), (m, *near(m)), order


def add(left, right):
    return left.astype(F32) + right.astype(F32)


def cut(size):
    quarter = size // 4
    return quarter, quarter, quarter // 2, quarter // 2, quarter


def split(block, sizes):
    edges = [sum(sizes[:k]) for k in range(len(sizes) + 1)]
    return tuple(block[low:high] for low, high in zip(edges[:-1], edges[1:]))


def ring_start(parts, got):
    return tuple(add(part, other) for part, other in zip(parts, split(got, cut(got.shape[0]))))


def ring_mix(after, before, got_a, got_b):
    half = got_a.shape[0]
    after = rows(after[:half] + got_a.astype(F32), after[half:])
    before = rows(before[:half], before[half:] + got_b.astype(F32))
    return after.astype(BF), before.astype(BF)


def ring_close(here, got_c, got_d):
    return (here + got_c.astype(F32) + got_d.astype(F32)).astype(BF)


def direct(block):
    size = block.shape[0] // 4
    here, after, far, before = (block[k * size : (k + 1) * size] for k in range(4))
    return here, send(after, "second", 1), send(far, "second", 2), send(before, "second", -1)


def close_z(here, *got):
    block = (add(here, got[0]) + add(got[1], got[2])).astype(BF)
    mine = block.shape[0] // 2
    return add(block[:mine], send(block[mine:], "z"))


def relative_order(me):
    y, x, z, c = split_index(me)
    place = jnp.arange(SHARDS * 16, dtype=jnp.int32)
    block, inside = place // 16, place % 16
    core_at = c ^ (block // 32)
    first, second = (block // 8) % 4, (block // 2) % 4
    row_y = (y + jnp.where(core_at == 0, first, second)) % NY
    row_x = (x + jnp.where(core_at == 0, second, first)) % NX
    absolute = join_index(row_y, row_x, z ^ (block % 2), core_at) * 16 + inside
    return (place[:, None] == absolute[None, :]).astype(BF)


def dot(left, right):
    return jnp.dot(left, right, preferred_element_type=F32)


def contract_last(left, right):
    return lax.dot_general(left, right, (((1,), (1,)), ((), ())), preferred_element_type=F32)


def contract_first(left, right):
    return lax.dot_general(left, right, (((0,), (0,)), ((), ())), preferred_element_type=F32)


def normal(values):
    centre = jnp.mean(values, -1, keepdims=True)
    centred = values - centre
    scale = lax.rsqrt(jnp.mean(centred * centred, -1, keepdims=True) + EPS)
    return centred * scale, scale


def normal_back(grad, unit, scale):
    return scale * (
        grad
        - jnp.mean(grad, -1, keepdims=True)
        - unit * jnp.mean(grad * unit, -1, keepdims=True)
    )


def segment_info(lens, count):
    ends = jnp.cumsum(lens, axis=-1)
    starts = ends - lens
    places = jnp.arange(count, dtype=jnp.int32)
    segment = jnp.sum((places[:, None] >= ends[..., None, :]).astype(jnp.int32), axis=-1)
    picked = (segment[..., None] == jnp.arange(lens.shape[-1], dtype=jnp.int32)).astype(jnp.int32)
    inner = places - jnp.sum(picked * starts[..., None, :], axis=-1)
    return segment, inner


def to_absolute(values, order):
    high = values.astype(BF)
    low = (values - high.astype(F32)).astype(BF)
    return contract_last(high, order) + contract_last(low, order)


def stack_rows(refs):
    return jnp.concatenate([ref[...] for ref in refs], 0)


def gain_rows(refs):
    row = lax.broadcasted_iota(jnp.int32, (16, 128), 0)
    lane = lax.broadcasted_iota(jnp.int32, (16, 128), 1)
    return contract_last((row == lane).astype(BF), stack_rows(refs))


def partner(values):
    width = values.shape[1]
    lane = lax.broadcasted_iota(jnp.int32, values.shape, 1)
    ahead = pltpu.roll(values, width - HEAD_DIM // 2, 1)
    behind = pltpu.roll(values, HEAD_DIM // 2, 1)
    return jnp.where(lane % HEAD_DIM < HEAD_DIM // 2, -ahead, behind)


def widen(table, width):
    return jnp.concatenate([table] * (width // table.shape[1]), 1)


def pair_bias(col, row):
    same = col[:, 0:1] == row[0:1]
    near = jnp.abs(col[:, 1:2] - row[1:2]) <= col[:, 2:3]
    return jnp.where(same & near, 0.0, -1e30)


def head_of(qkv, part, head, rows):
    return qkv[part, rows, head * HEAD_DIM : (head + 1) * HEAD_DIM]


def attn_forward_step(step, steps, micro, u, order, cos, sin, col, row, proj, out, gains, xn, qkv, h, yn, saves=None):
    @pl.when(step == 0)
    def _():
        unit, _ = normal(dot(u[...], order[...]))
        xn[...] = (unit * gain_rows(gains)[0:1]).astype(BF)

    packed = dot(xn[...], stack_rows(proj))

    @pl.when(step < 2)
    def _():
        turned = packed * widen(cos[...], ATTN_TILE) + partner(packed) * widen(sin[...], ATTN_TILE)
        qkv[step] = turned.astype(BF)

    @pl.when(step == 2)
    def _():
        qkv[step] = packed.astype(BF)
        slots = u.shape[0] // micro
        lane = lax.broadcasted_iota(jnp.int32, (slots, 128), 1)
        blocks = []
        for m in range(micro):
            at = slice(m * slots, (m + 1) * slots)
            bias = pair_bias(col[at], row[m])
            log_all = jnp.zeros((slots, 128), F32)
            heads = []
            for low in range(0, HEADS, GROUP):
                group = range(low, low + GROUP)
                scores = [contract_last(head_of(qkv, 0, k, at), head_of(qkv, 1, k, at)) * SCALE + bias for k in group]
                peaks = [jnp.max(x, -1, keepdims=True) for x in scores]
                scores = [jnp.exp(x - p) for x, p in zip(scores, peaks)]
                totals = [jnp.sum(x, -1, keepdims=True) for x in scores]
                for k, p, t in zip(group, peaks, totals):
                    log_all = jnp.where(lane == k, p + jnp.log(t), log_all)
                probs = [(x * (1.0 / t)).astype(BF) for x, t in zip(scores, totals)]
                heads += [dot(x, head_of(qkv, 2, k, at)).astype(BF) for k, x in zip(group, probs)]
            if saves:
                saves[0][at] = log_all
            blocks.append(jnp.concatenate(heads, 1))
        attended = dot(jnp.concatenate(blocks, 0), order[...]).astype(BF)
        if saves:
            saves[1][...] = attended
        hidden = u[...].astype(F32) + dot(attended, stack_rows(out))
        h[...] = hidden
        unit, _ = normal(hidden)
        gain = contract_last(gain_rows(gains).astype(BF), order[...])[1:2]
        yn[...] = dot((unit * gain).astype(BF), order[...]).astype(BF)


def mlp_forward_step(step, steps, yn, h, order, gate, up, down, z, total, saves=None):
    g = dot(yn[...], stack_rows(gate))
    v = dot(yn[...], stack_rows(up))
    cdf = 0.5 * (1.0 + lax.erf(g * math.sqrt(0.5)))
    unit = g * cdf
    mid = (unit * v).astype(BF)
    if saves:
        slope = cdf + g * jnp.exp(-0.5 * g * g) * (1.0 / math.sqrt(2.0 * math.pi))
        at = pl.ds(pl.multiple_of(step * MLP_TILE, 128), MLP_TILE)
        for ref, value in zip(saves, (mid, (v * slope).astype(BF), unit.astype(BF))):
            ref[:, at] = value
    part = contract_last(mid, stack_rows(down))

    @pl.when(step == 0)
    def _():
        total[...] = part

    @pl.when(step > 0)
    def _():
        total[...] += part

    @pl.when(step == steps - 1)
    def _():
        z[...] = (h[...] + to_absolute(total[...], order[...])).astype(BF)


def mlp_backward_step(step, steps, dzr, dz, h, order, one, two, gains, gate, up, down, dh, da, total, saves=None):
    @pl.when(step == 0)
    def _():
        total[...] = jnp.zeros_like(total)

    dmid = dot(dzr[...], stack_rows(down))
    dg = (dmid * one.astype(F32)).astype(BF)
    dv = (dmid * two.astype(F32)).astype(BF)
    if saves:
        saves[0][...] = dg
        saves[1][...] = dv
    total[...] += contract_last(dg, stack_rows(gate)) + contract_last(dv, stack_rows(up))

    @pl.when(step == steps - 1)
    def _():
        dyn = to_absolute(total[...], order[...])
        unit, scale = normal(h[...])
        gain = contract_last(gain_rows(gains).astype(BF), order[...])[1:2]
        if saves:
            saves[2][...] = dot((dyn * unit).astype(BF), order[...]).astype(BF)
        grad = dz[...].astype(F32) + normal_back(dyn * gain, unit, scale)
        dh[...] = grad
        da[...] = grad.astype(BF)


def heads_backward_step(micro, da, order, cos, sin, col, row, qkv, lse, out, put):
    tokens, width = da.shape
    rel = contract_last(da[...], stack_rows(out)).astype(BF)
    do_all = contract_last(rel, order[...]).astype(BF)
    slots = tokens // micro
    for m in range(micro):
        at = slice(m * slots, (m + 1) * slots)
        bias = pair_bias(col[at], row[m])
        log_all = lse[at]
        cosine, sine = widen(cos[at], width), widen(sin[at], width)
        dqs, dks, dvs = [], [], []
        for low in range(0, HEADS, GROUP):
            group = range(low, low + GROUP)
            qs, ks, vs = ([head_of(qkv, part, k, at) for k in group] for part in range(3))
            ds = [do_all[at, k * HEAD_DIM : (k + 1) * HEAD_DIM] for k in group]
            probs = [contract_last(q, k) * SCALE + bias for q, k in zip(qs, ks)]
            probs = [jnp.exp(x - log_all[:, k : k + 1]) for x, k in zip(probs, group)]
            dps = [contract_last(d, v) for d, v in zip(ds, vs)]
            dss = [(p * (x - jnp.sum(p * x, -1, keepdims=True))).astype(BF) for p, x in zip(probs, dps)]
            dvs += [contract_first(p.astype(BF), d) for p, d in zip(probs, ds)]
            dqs += [dot(x, k) for x, k in zip(dss, ks)]
            dks += [contract_first(x, q) for x, q in zip(dss, qs)]
        dq, dk = (jnp.concatenate(x, 1) * SCALE for x in (dqs, dks))
        put(0, at, (dq * cosine - partner(dq) * sine).astype(BF))
        put(1, at, (dk * cosine - partner(dk) * sine).astype(BF))
        put(2, at, jnp.concatenate(dvs, 1).astype(BF))


def qkv_backward_step(step, steps, dqkv, dh, u, order, gains, proj, du, total, term=None):
    @pl.when(step == 0)
    def _():
        total[...] = jnp.zeros_like(total)

    total[...] += contract_last(dqkv, stack_rows(proj))

    @pl.when(step == steps - 1)
    def _():
        unit, scale = normal(dot(u[...], order[...]))
        dxn = total[...]
        if term is not None:
            term[...] = (dxn * unit).astype(BF)
        back = normal_back(dxn * gain_rows(gains)[0:1], unit, scale)
        du[...] = (dh[...] + to_absolute(back, order[...])).astype(BF)


def parted(refs, *sizes):
    out, low = [], 0
    for size in sizes:
        out.append(refs[low : low + size])
        low += size
    return *out, refs[low:]


def attn_forward_kernel(n, micro, steps, *refs):
    args, proj, out, gains, rest = parted(refs, 6, n, n, n)
    h, yn, qkv, xn = rest
    attn_forward_step(pl.program_id(0), steps, micro, *args, proj, out, gains, xn, qkv, h, yn)


def mlp_forward_kernel(n, steps, *refs):
    args, gate, up, down, rest = parted(refs, 3, n, n, n)
    mlp_forward_step(pl.program_id(0), steps, *args, gate, up, down, *rest)


def mlp_backward_kernel(n, steps, *refs):
    args, (one, two), gains, gate, up, down, rest = parted(refs, 4, 2, n, n, n, n)
    dg, dv, dh, da, term, total = rest
    weights = (gains, gate, up, down)
    mlp_backward_step(pl.program_id(0), steps, *args, one[...], two[...], *weights, dh, da, total, (dg, dv, term))


def heads_backward_kernel(n, micro, *refs):
    args, out, (dqkv,) = parted(refs, 8, n)
    width = refs[0].shape[1]

    def put(part, at, value):
        dqkv[at, part * width : (part + 1) * width] = value

    heads_backward_step(micro, *args, out, put)


def middle_kernel(n, micro, *refs):
    args, proj, out, gains, gate, up, down, outs, scratch = parted(refs, 7, n, n, n, n, n, n, 11)
    u, dz, order, cos, sin, col, row = args
    xn, qkv, lse, attended, h, yn, mid, one, two, z, du = outs
    total, dzr, dh, da, dqkv = scratch
    step = pl.program_id(0)
    turns = (cos, sin, col, row)

    @pl.when(step < 3)
    def _():
        attn_forward_step(step, 3, micro, u, order, *turns, proj, out, gains, xn, qkv, h, yn, (lse, attended))

    @pl.when((step >= 3) & (step < 6))
    def _():
        mlp_forward_step(step - 3, 3, yn, h, order, gate, up, down, z, total, (mid, one, two))

    @pl.when(step == 6)
    def _():
        dzr[...] = dot(dz[...], order[...]).astype(BF)

    @pl.when((step >= 6) & (step < 9))
    def _():
        at = pl.ds(pl.multiple_of((8 - step) * MLP_TILE, 128), MLP_TILE)
        weights = (gains, gate, up, down)
        mlp_backward_step(step - 6, 3, dzr, dz, h, order, one[:, at], two[:, at], *weights, dh, da, total)

    @pl.when(step == 9)
    def _():
        def put(part, at, value):
            dqkv[part, at] = value

        heads_backward_step(micro, da, order, *turns, qkv, lse, out, put)

    @pl.when(step >= 9)
    def _():
        qkv_backward_step(step - 9, 3, dqkv[11 - step], dh, u, order, gains, proj, du, total)


def qkv_backward_kernel(n, steps, *refs):
    (dqkv, *args), gains, proj, (du, term, total) = parted(refs, 4, n, n)
    qkv_backward_step(pl.program_id(0), steps, dqkv[...], *args, gains, proj, du, total, term)


def columns(pieces, tile, place):
    return [pl.BlockSpec((p.shape[0], tile), lambda j: (0, place(j))) for p in pieces]


def whole(array):
    return pl.BlockSpec(array.shape, lambda j: (0,) * array.ndim)


def shape_of(rows, cols, kind=BF):
    return jax.ShapeDtypeStruct((rows, cols), kind)


def fixed(rows, cols):
    return pl.BlockSpec((rows, cols), lambda j: (0, 0))


def tiled(rows, cols, start=0, count=None):
    if count is None:
        return pl.BlockSpec((rows, cols), lambda j: (0, j))
    return pl.BlockSpec((rows, cols), lambda j: (0, jnp.clip(j - start, 0, count - 1)))


def cost(flops, weights):
    return pl.CostEstimate(flops=int(flops) // 64, bytes_accessed=int(weights * 2) // 64, transcendentals=0)


def attn_forward(u, pieces, common):
    n, (tokens, width) = len(pieces), u.shape
    steps = 3 * width // ATTN_TILE
    args = (u, *common)
    return pl.pallas_call(
        functools.partial(attn_forward_kernel, n, common[-1].shape[0], steps),
        grid=(steps,),
        in_specs=[whole(a) for a in args]
        + columns(pieces, ATTN_TILE, lambda j: j)
        + columns(pieces, width, lambda j: 3)
        + columns(pieces, 128, lambda j: 4 * width // 128),
        out_specs=[fixed(tokens, width), fixed(tokens, width)],
        out_shape=[shape_of(tokens, width, F32), shape_of(tokens, width)],
        scratch_shapes=[pltpu.VMEM((steps, tokens, ATTN_TILE), BF), pltpu.VMEM((tokens, width), BF)],
        compiler_params=PARAMS,
        cost_estimate=cost(2 * tokens * 6 * width * width, 5 * width * width),
    )(*args, *pieces, *pieces, *pieces)


def mlp_forward(yn, h, pieces, order):
    n, (tokens, width) = len(pieces), yn.shape
    hidden = pieces[0].shape[1] // 3
    steps = hidden // MLP_TILE
    args = (yn, h, order)
    return pl.pallas_call(
        functools.partial(mlp_forward_kernel, n, steps),
        grid=(steps,),
        in_specs=[whole(a) for a in args]
        + columns(pieces, MLP_TILE, lambda j: j)
        + columns(pieces, MLP_TILE, lambda j: steps + j)
        + columns(pieces, MLP_TILE, lambda j: 2 * steps + j),
        out_specs=fixed(tokens, width),
        out_shape=shape_of(tokens, width),
        scratch_shapes=[pltpu.VMEM((tokens, width), F32)],
        compiler_params=PARAMS,
        cost_estimate=cost(6 * tokens * hidden * width, 4 * hidden * width),
    )(*args, *pieces, *pieces, *pieces)


def middle(u, dz, common, pieces_a, pieces_m):
    n, (tokens, width) = len(pieces_a), u.shape
    hidden = pieces_m[0].shape[1] // 3
    args = (u, dz, *common)

    def proj_at(j):
        return jnp.where(j < 3, j, jnp.where(j < 9, 2, 11 - j))

    def mlp_at(j):
        return jnp.where(j < 6, jnp.maximum(j - 3, 0), jnp.maximum(8 - j, 0))

    kinds = [(width, BF), None, (128, F32), (width, BF), (width, F32), (width, BF)]
    kinds += [(hidden, BF)] * 3 + [(width, BF)] * 2
    cube = (3, tokens, width)
    return pl.pallas_call(
        functools.partial(middle_kernel, n, common[-1].shape[0]),
        grid=(12,),
        in_specs=[whole(a) for a in args]
        + columns(pieces_a, ATTN_TILE, proj_at)
        + columns(pieces_a, width, lambda j: 3)
        + columns(pieces_a, 128, lambda j: 4 * width // 128)
        + columns(pieces_m, MLP_TILE, mlp_at)
        + columns(pieces_m, MLP_TILE, lambda j: 3 + mlp_at(j))
        + columns(pieces_m, MLP_TILE, lambda j: 6 + mlp_at(j)),
        out_specs=[fixed(tokens, k[0]) if k else pl.BlockSpec(cube, lambda j: (0, 0, 0)) for k in kinds],
        out_shape=[shape_of(tokens, *k) if k else jax.ShapeDtypeStruct(cube, BF) for k in kinds],
        scratch_shapes=[
            pltpu.VMEM((tokens, width), F32),
            pltpu.VMEM((tokens, width), BF),
            pltpu.VMEM((tokens, width), F32),
            pltpu.VMEM((tokens, width), BF),
            pltpu.VMEM(cube, BF),
        ],
        compiler_params=PARAMS,
        cost_estimate=cost(12 * tokens * (hidden + width) * width, 12 * hidden * width),
    )(*args, *pieces_a, *pieces_a, *pieces_a, *pieces_m, *pieces_m, *pieces_m)


def mlp_backward(dzr, dz, h, one, two, pieces_a, pieces, order):
    n, (tokens, width) = len(pieces), dz.shape
    hidden = pieces[0].shape[1] // 3
    steps = hidden // MLP_TILE
    args = (dzr, dz, h, order)
    return pl.pallas_call(
        functools.partial(mlp_backward_kernel, n, steps),
        grid=(steps,),
        in_specs=[whole(a) for a in args]
        + [tiled(tokens, MLP_TILE)] * 2
        + columns(pieces_a, 128, lambda j: 4 * width // 128)
        + columns(pieces, MLP_TILE, lambda j: j)
        + columns(pieces, MLP_TILE, lambda j: steps + j)
        + columns(pieces, MLP_TILE, lambda j: 2 * steps + j),
        out_specs=[tiled(tokens, MLP_TILE)] * 2 + [fixed(tokens, width)] * 3,
        out_shape=[shape_of(tokens, hidden)] * 2
        + [shape_of(tokens, width, F32), shape_of(tokens, width), shape_of(tokens, width)],
        scratch_shapes=[pltpu.VMEM((tokens, width), F32)],
        compiler_params=PARAMS,
        cost_estimate=cost(6 * tokens * hidden * width, 4 * hidden * width),
    )(*args, one, two, *pieces_a, *pieces, *pieces, *pieces)


def heads_backward(da, common, qkv, lse, pieces):
    n, (tokens, width) = len(pieces), da.shape
    args = (da, *common, qkv, lse)
    return pl.pallas_call(
        functools.partial(heads_backward_kernel, n, common[-1].shape[0]),
        grid=(1,),
        in_specs=[whole(a) for a in args] + columns(pieces, width, lambda j: 3),
        out_specs=fixed(tokens, 3 * width),
        out_shape=shape_of(tokens, 3 * width),
        compiler_params=PARAMS,
        cost_estimate=cost(2 * tokens * width * width, width * width),
    )(*args, *pieces)


def qkv_backward(dqkv, dh, u, order, pieces):
    n, (tokens, width) = len(pieces), u.shape
    steps = 3 * width // ATTN_TILE
    args = (dh, u, order)
    return pl.pallas_call(
        functools.partial(qkv_backward_kernel, n, steps),
        grid=(steps,),
        in_specs=[tiled(tokens, ATTN_TILE)]
        + [whole(a) for a in args]
        + columns(pieces, 128, lambda j: 4 * width // 128)
        + columns(pieces, ATTN_TILE, lambda j: j),
        out_specs=[fixed(tokens, width), fixed(tokens, width)],
        out_shape=[shape_of(tokens, width), shape_of(tokens, width)],
        scratch_shapes=[pltpu.VMEM((tokens, width), F32)],
        compiler_params=PARAMS,
        cost_estimate=cost(2 * tokens * 3 * width * width, 3 * width * width),
    )(dqkv, *args, *pieces, *pieces)


def product_kernel(counts, sides, *refs):
    count = len(counts)
    lefts, rights, rest = refs[: count + sides], refs[count + sides : 2 * (count + sides)], refs[2 * (count + sides) :]
    outs, turned = rest[:-1], rest[-1]
    step = pl.program_id(0)

    @pl.when(step == 0)
    def _():
        for k, left in enumerate(lefts):
            turned[k] = left[...].T

    begin = 0
    for which in range(count):

        @pl.when((step >= begin) & (step < begin + counts[which]))
        def _(which=which):
            value = dot(turned[which], rights[which][...])
            if sides:
                beside = sum(dot(turned[k], rights[k][...]) for k in range(count, count + sides))
                value = jnp.concatenate([value, beside], 1)
            low = 0
            for out in outs:
                out[...] = value[low : low + out.shape[0]].astype(BF)
                low += out.shape[0]

        begin += counts[which]


def make_product(lefts, rights, tile, side_lefts=(), side_rights=()):
    tokens, width = lefts[0].shape
    counts = [r.shape[1] // tile for r in rights]
    steps = sum(counts)
    starts = [sum(counts[:k]) for k in range(len(counts))]
    every = (*lefts, *side_lefts)
    side = side_rights[0].shape[1] // steps if side_rights else 0
    out_tile = tile + side

    def product(part, sizes):
        span = sum(sizes)
        return pl.pallas_call(
            functools.partial(product_kernel, counts, len(side_lefts)),
            grid=(steps,),
            in_specs=[pl.BlockSpec((tokens, span), lambda j: (0, part)) for _ in every]
            + [tiled(tokens, tile, s, c) for s, c in zip(starts, counts)]
            + [tiled(tokens, side) for _ in side_rights],
            out_specs=[tiled(r, out_tile) for r in sizes],
            out_shape=[shape_of(r, steps * out_tile) for r in sizes],
            scratch_shapes=[pltpu.VMEM((len(every), span, tokens), BF)],
            compiler_params=PARAMS,
            cost_estimate=cost(2 * tokens * span * steps * out_tile, span * steps * out_tile),
        )(*every, *rights, *side_rights)

    return product


def shards(tokens_in, attn_proj, attn_out, mlp_in, mlp_out, gain_attn, gain_mlp, lengths, cotangent):
    section = lax.axis_index("section")
    micro, slots, width = tokens_in.shape
    tokens = micro * slots
    three, hidden = attn_proj.shape[2], mlp_out.shape[2]
    padded = -(-hidden // MLP_TILE) * MLP_TILE
    gains = jnp.zeros((gain_attn.shape[1], GAIN_TILE), BF)
    gains = gains.at[:, 0].set(gain_attn[0]).at[:, 1].set(gain_mlp[0])
    gap = jnp.zeros((gain_attn.shape[1], padded - hidden), BF)
    order = relative_order(lax.axis_index("fsdp"))
    pieces_a, pieces_m, order = gather(
        jnp.concatenate([attn_proj[0], attn_out[0], gains], 1),
        jnp.concatenate([mlp_in[0, :, :hidden], gap, mlp_in[0, :, hidden:], gap, mlp_out[0], gap], 1),
        order,
    )
    base = jnp.where(section == 0, 10000.0, 160000.0).astype(F32)
    reach = jnp.where(section == 0, WINDOW / 2.0, 4.0 * slots).astype(F32)
    segment, inner = segment_info(lengths[:, 0], slots)
    half = HEAD_DIM // 2
    freqs = jnp.exp(-jnp.log(base) * (jnp.arange(half, dtype=F32) * (2.0 / HEAD_DIM)))
    angles = jnp.tile(inner.reshape(tokens, 1).astype(F32) * freqs, (1, 128 // half))
    col = jnp.stack([segment.reshape(tokens).astype(F32), inner.reshape(tokens).astype(F32)], 1)
    col = jnp.concatenate([col, jnp.broadcast_to(reach, (tokens, 126))], 1)
    row = jnp.stack([segment, inner] + [inner] * 6, 1).astype(F32)
    common = (order, jnp.cos(angles), jnp.sin(angles), col, row)

    first_in = tokens_in.reshape(tokens, width)
    hid, yn = attn_forward(first_in, pieces_a, common)
    m_block, m_near, m_near2 = pieces_m
    m_near, m_near2, yn = tie(m_near, m_near2, yn)
    m_far, m_far2 = far(m_near, m_near2)
    near_core = core(m_block, m_near, m_near2)
    far_core = core(m_far, m_far2)
    pieces_m = (m_block, m_near, m_far, m_far2, m_near2, *near_core[:2], *far_core, near_core[2])
    middle_out = mlp_forward(yn, hid, pieces_m, order)
    received = lax.ppermute(middle_out, "section", [(0, 1)])
    layer_in = jnp.where(section == 0, first_in, received)
    last_grad = cotangent.reshape(tokens, width)
    xn, qkv, lse, attended, hid, yn, mid, one, two, result, middle_grad = middle(
        layer_in, last_grad, common, pieces_a, pieces_m
    )
    received = lax.ppermute(middle_grad, "section", [(1, 0)])
    grad_out = jnp.where(section == 1, last_grad, received)
    half = width // 2
    dzr = dot(grad_out, order).astype(BF)
    dg, dv, dh, da, term_m = mlp_backward(dzr, grad_out, hid, one, two, pieces_a, pieces_m, order)
    product = make_product((yn, yn, dzr), (dg, dv, mid), MLP_TILE)
    sent_m, yn = tie(product(1, (half,))[0], yn)
    got_m = send(sent_m, "core")
    product = make_product((yn, yn, dzr), (dg, dv, mid), MLP_TILE)
    own_m = product(0, cut(half))
    got_m, da = tie(got_m, da)
    here_m, after_m, far_m, far_m2, before_m = ring_start(own_m, got_m)
    far_m, far_m2 = send(far_m.astype(BF), "first", 1), send(far_m2.astype(BF), "first", -1)
    dqkv = heads_backward(da, common, qkv, lse, pieces_a)
    far_m, far_m2, dqkv = tie(far_m, far_m2, dqkv)
    *mix_m, dqkv = tie(*ring_mix(after_m, before_m, far_m, far_m2), dqkv)
    near_m = send(mix_m[0], "first", 1), send(mix_m[1], "first", -1)
    grad_in, term_a = qkv_backward(dqkv, dh, layer_in, order, pieces_a)
    lane = lax.broadcasted_iota(jnp.int32, (tokens, 4 * GAIN_TILE), 1)
    picks = ((lane == 0).astype(BF), (lane == 1).astype(BF))
    product = make_product((xn, attended), (dqkv, da), width, (term_a, term_m), picks)
    *own_a, sent_a = product(0, (*cut(half), half))
    got_a = send(sent_a, "core")
    here_a, after_a, far_a, far_a2, before_a = ring_start(own_a, got_a)
    ends_m = direct(ring_close(here_m, *near_m))
    far_a, far_a2 = send(far_a.astype(BF), "first", 1), send(far_a2.astype(BF), "first", -1)
    mix_a = ring_mix(after_a, before_a, far_a, far_a2)
    *ends_m, mix_a, mix_a2 = tie(*ends_m, *mix_a)
    near_a = send(mix_a, "first", 1), send(mix_a2, "first", -1)
    sum_m = close_z(*ends_m)
    sum_a = close_z(*direct(ring_close(here_a, *near_a)))
    edge = width + GAIN_TILE
    grad_proj = jnp.concatenate([sum_a[:, k * edge : k * edge + width] for k in range(3)], 1)
    grad_up = jnp.concatenate([sum_m[:, :hidden], sum_m[:, padded : padded + hidden]], 1)
    return (
        result.reshape(1, micro, slots, width),
        grad_in.reshape(1, micro, slots, width),
        grad_proj[None],
        sum_a[:, 3 * edge : 3 * edge + width][None],
        grad_up[None],
        sum_m[:, 2 * padded : 2 * padded + hidden][None],
        sum_a[:, width][None],
        sum_a[:, width + 1][None],
    )


def solution(mesh):
    in_specs = (
        P(None, "fsdp", None),
        P("section", "fsdp", None),
        P("section", "fsdp", None),
        P("section", "fsdp", None),
        P("section", "fsdp", None),
        P("section", "fsdp"),
        P("section", "fsdp"),
        P(None, "fsdp", None),
        P(None, "fsdp", None),
    )
    out_specs = (
        P("section", None, "fsdp", None),
        P("section", None, "fsdp", None),
        P("section", "fsdp", None),
        P("section", "fsdp", None),
        P("section", "fsdp", None),
        P("section", "fsdp", None),
        P("section", "fsdp"),
        P("section", "fsdp"),
    )
    return jax.shard_map(shards, mesh=mesh, in_specs=in_specs, out_specs=out_specs, check_vma=False)
```

```python
import functools
import math
import jax
import jax.numpy as jnp
from jax import lax
from jax.experimental import pallas as pl
from jax.experimental.pallas import tpu as pltpu
from jax.sharding import PartitionSpec as P

HEADS = 16
HEAD_DIM = 64
WINDOW = 128
EPS = 1e-05
NY, NX, NZ, NC = 4, 4, 2, 2
SHARDS = NY * NX * NZ * NC
BF = jnp.bfloat16
F32 = jnp.float32
ATTN_TILE = 1024
MLP_TILE = 896
GAIN_TILE = 128
GROUP = 8
SCALE = HEAD_DIM**-0.5
PARAMS = pltpu.CompilerParams(vmem_limit_bytes=56 * 1024 * 1024)


def split_index(i):
    return i // (NX * NZ * NC), (i // (NZ * NC)) % NX, (i // NC) % NZ, i % NC


def join_index(y, x, z, c):
    return ((y * NX + x) * NZ + z) * NC + c


def pairs(kind, step=1):
    out = []
    for i in range(SHARDS):
        y, x, z, c = split_index(i)
        if kind == "core":
            c = 1 - c
        elif kind == "z":
            z = 1 - z
        elif (kind == "first") == (c == 0):
            y = (y + step) % NY
        else:
            x = (x + step) % NX
        out.append((i, join_index(y, x, z, c)))
    return out


def send(value, kind, step=1):
    return lax.ppermute(value, "fsdp", pairs(kind, step))


def tie(*values):
    return lax.optimization_barrier(values)


def rows(*blocks):
    return jnp.concatenate(blocks, 0)


def spread(block):
    return rows(block, send(block, "second", -1), send(block, "second", 2), send(block, "second", 1))


def near(block):
    return send(block, "first", -1), send(block, "first", 1)


def far(after, before):
    half = after.shape[0] // 2
    return send(after[:half], "first", -1), send(before[half:], "first", 1)


def core(*pieces):
    return tuple(send(piece, "core") for piece in pieces)


def gather(a, m, order):
    a_z, m = tie(send(a, "z"), m)
    a, m_z, order = tie(spread(rows(a, a_z)), send(m, "z"), order)
    a_after, a_before = near(a)
    m = spread(rows(m, m_z))
    a_far, a_far2 = far(a_after, a_before)
    a_far, a_far2, m = tie(a_far, a_far2, m)
    a = (a, a_after, a_far, a_far2, a_before)
    return a + core(*a), (m, *near(m)), order


def add(left, right):
    return left.astype(F32) + right.astype(F32)


def cut(size):
    quarter = size // 4
    return quarter, quarter, quarter // 2, quarter // 2, quarter


def split(block, sizes):
    edges = [sum(sizes[:k]) for k in range(len(sizes) + 1)]
    return tuple(block[low:high] for low, high in zip(edges[:-1], edges[1:]))


def ring_start(parts, got):
    return tuple(add(part, other) for part, other in zip(parts, split(got, cut(got.shape[0]))))


def ring_mix(after, before, got_a, got_b):
    half = got_a.shape[0]
    after = rows(after[:half] + got_a.astype(F32), after[half:])
    before = rows(before[:half], before[half:] + got_b.astype(F32))
    return after.astype(BF), before.astype(BF)


def ring_close(here, got_c, got_d):
    return (here + got_c.astype(F32) + got_d.astype(F32)).astype(BF)


def direct(block):
    size = block.shape[0] // 4
    here, after, far, before = (block[k * size : (k + 1) * size] for k in range(4))
    return here, send(after, "second", 1), send(far, "second", 2), send(before, "second", -1)


def close_z(here, *got):
    block = (add(here, got[0]) + add(got[1], got[2])).astype(BF)
    mine = block.shape[0] // 2
    return add(block[:mine], send(block[mine:], "z"))


def relative_order(me):
    y, x, z, c = split_index(me)
    place = jnp.arange(SHARDS * 16, dtype=jnp.int32)
    block, inside = place // 16, place % 16
    core_at = c ^ (block // 32)
    first, second = (block // 8) % 4, (block // 2) % 4
    row_y = (y + jnp.where(core_at == 0, first, second)) % NY
    row_x = (x + jnp.where(core_at == 0, second, first)) % NX
    absolute = join_index(row_y, row_x, z ^ (block % 2), core_at) * 16 + inside
    return (place[:, None] == absolute[None, :]).astype(BF)


def dot(left, right):
    return jnp.dot(left, right, preferred_element_type=F32)


def contract_last(left, right):
    return lax.dot_general(left, right, (((1,), (1,)), ((), ())), preferred_element_type=F32)


def contract_first(left, right):
    return lax.dot_general(left, right, (((0,), (0,)), ((), ())), preferred_element_type=F32)


def normal(values):
    centre = jnp.mean(values, -1, keepdims=True)
    centred = values - centre
    scale = lax.rsqrt(jnp.mean(centred * centred, -1, keepdims=True) + EPS)
    return centred * scale, scale


def normal_back(grad, unit, scale):
    return scale * (
        grad
        - jnp.mean(grad, -1, keepdims=True)
        - unit * jnp.mean(grad * unit, -1, keepdims=True)
    )


def segment_info(lens, count):
    ends = jnp.cumsum(lens, axis=-1)
    starts = ends - lens
    places = jnp.arange(count, dtype=jnp.int32)
    segment = jnp.sum((places[:, None] >= ends[..., None, :]).astype(jnp.int32), axis=-1)
    picked = (segment[..., None] == jnp.arange(lens.shape[-1], dtype=jnp.int32)).astype(jnp.int32)
    inner = places - jnp.sum(picked * starts[..., None, :], axis=-1)
    return segment, inner


def to_absolute(values, order):
    high = values.astype(BF)
    low = (values - high.astype(F32)).astype(BF)
    return contract_last(high, order) + contract_last(low, order)


def stack_rows(refs):
    return jnp.concatenate([ref[...] for ref in refs], 0)


def gain_rows(refs):
    row = lax.broadcasted_iota(jnp.int32, (16, 128), 0)
    lane = lax.broadcasted_iota(jnp.int32, (16, 128), 1)
    return contract_last((row == lane).astype(BF), stack_rows(refs))


def partner(values):
    width = values.shape[1]
    lane = lax.broadcasted_iota(jnp.int32, values.shape, 1)
    ahead = pltpu.roll(values, width - HEAD_DIM // 2, 1)
    behind = pltpu.roll(values, HEAD_DIM // 2, 1)
    return jnp.where(lane % HEAD_DIM < HEAD_DIM // 2, -ahead, behind)


def widen(table, width):
    return jnp.concatenate([table] * (width // table.shape[1]), 1)


def pair_bias(col, row):
    same = col[:, 0:1] == row[0:1]
    near = jnp.abs(col[:, 1:2] - row[1:2]) <= col[:, 2:3]
    return jnp.where(same & near, 0.0, -1e30)


def head_of(qkv, part, head, rows):
    return qkv[part, rows, head * HEAD_DIM : (head + 1) * HEAD_DIM]


def attn_forward_step(step, steps, micro, u, order, cos, sin, col, row, proj, out, gains, xn, qkv, h, yn, saves=None):
    @pl.when(step == 0)
    def _():
        unit, _ = normal(dot(u[...], order[...]))
        xn[...] = (unit * gain_rows(gains)[0:1]).astype(BF)

    packed = dot(xn[...], stack_rows(proj))

    @pl.when(step < 2)
    def _():
        turned = packed * widen(cos[...], ATTN_TILE) + partner(packed) * widen(sin[...], ATTN_TILE)
        qkv[step] = turned.astype(BF)

    @pl.when(step == 2)
    def _():
        qkv[step] = packed.astype(BF)
        slots = u.shape[0] // micro
        lane = lax.broadcasted_iota(jnp.int32, (slots, 128), 1)
        blocks = []
        for m in range(micro):
            at = slice(m * slots, (m + 1) * slots)
            bias = pair_bias(col[at], row[m])
            log_all = jnp.zeros((slots, 128), F32)
            heads = []
            for low in range(0, HEADS, GROUP):
                group = range(low, low + GROUP)
                scores = [contract_last(head_of(qkv, 0, k, at), head_of(qkv, 1, k, at)) * SCALE + bias for k in group]
                peaks = [jnp.max(x, -1, keepdims=True) for x in scores]
                scores = [jnp.exp(x - p) for x, p in zip(scores, peaks)]
                totals = [jnp.sum(x, -1, keepdims=True) for x in scores]
                for k, p, t in zip(group, peaks, totals):
                    log_all = jnp.where(lane == k, p + jnp.log(t), log_all)
                probs = [(x * (1.0 / t)).astype(BF) for x, t in zip(scores, totals)]
                heads += [dot(x, head_of(qkv, 2, k, at)).astype(BF) for k, x in zip(group, probs)]
            if saves:
                saves[0][at] = log_all
            blocks.append(jnp.concatenate(heads, 1))
        attended = dot(jnp.concatenate(blocks, 0), order[...]).astype(BF)
        if saves:
            saves[1][...] = attended
        hidden = u[...].astype(F32) + dot(attended, stack_rows(out))
        h[...] = hidden
        unit, _ = normal(hidden)
        gain = contract_last(gain_rows(gains).astype(BF), order[...])[1:2]
        yn[...] = dot((unit * gain).astype(BF), order[...]).astype(BF)


def mlp_forward_step(step, steps, yn, h, order, gate, up, down, z, total, saves=None):
    g = dot(yn[...], stack_rows(gate))
    v = dot(yn[...], stack_rows(up))
    cdf = 0.5 * (1.0 + lax.erf(g * math.sqrt(0.5)))
    unit = g * cdf
    mid = (unit * v).astype(BF)
    if saves:
        slope = cdf + g * jnp.exp(-0.5 * g * g) * (1.0 / math.sqrt(2.0 * math.pi))
        at = pl.ds(pl.multiple_of(step * MLP_TILE, 128), MLP_TILE)
        for ref, value in zip(saves, (mid, (v * slope).astype(BF), unit.astype(BF))):
            ref[:, at] = value
    part = contract_last(mid, stack_rows(down))

    @pl.when(step == 0)
    def _():
        total[...] = part

    @pl.when(step > 0)
    def _():
        total[...] += part

    @pl.when(step == steps - 1)
    def _():
        z[...] = (h[...] + to_absolute(total[...], order[...])).astype(BF)


def mlp_backward_step(step, steps, dzr, dz, h, order, one, two, gains, gate, up, down, dh, da, total, saves=None):
    @pl.when(step == 0)
    def _():
        total[...] = jnp.zeros_like(total)

    dmid = dot(dzr[...], stack_rows(down))
    dg = (dmid * one.astype(F32)).astype(BF)
    dv = (dmid * two.astype(F32)).astype(BF)
    if saves:
        saves[0][...] = dg
        saves[1][...] = dv
    total[...] += contract_last(dg, stack_rows(gate)) + contract_last(dv, stack_rows(up))

    @pl.when(step == steps - 1)
    def _():
        dyn = to_absolute(total[...], order[...])
        unit, scale = normal(h[...])
        gain = contract_last(gain_rows(gains).astype(BF), order[...])[1:2]
        grad = dz[...].astype(F32) + normal_back(dyn * gain, unit, scale)
        dh[...] = grad
        da[...] = grad.astype(BF)


def heads_backward_step(micro, da, order, cos, sin, col, row, qkv, lse, out, put):
    tokens, width = da.shape
    rel = contract_last(da[...], stack_rows(out)).astype(BF)
    do_all = contract_last(rel, order[...]).astype(BF)
    slots = tokens // micro
    for m in range(micro):
        at = slice(m * slots, (m + 1) * slots)
        bias = pair_bias(col[at], row[m])
        log_all = lse[at]
        cosine, sine = widen(cos[at], width), widen(sin[at], width)
        dqs, dks, dvs = [], [], []
        for low in range(0, HEADS, GROUP):
            group = range(low, low + GROUP)
            qs, ks, vs = ([head_of(qkv, part, k, at) for k in group] for part in range(3))
            ds = [do_all[at, k * HEAD_DIM : (k + 1) * HEAD_DIM] for k in group]
            probs = [contract_last(q, k) * SCALE + bias for q, k in zip(qs, ks)]
            probs = [jnp.exp(x - log_all[:, k : k + 1]) for x, k in zip(probs, group)]
            dps = [contract_last(d, v) for d, v in zip(ds, vs)]
            dss = [(p * (x - jnp.sum(p * x, -1, keepdims=True))).astype(BF) for p, x in zip(probs, dps)]
            dvs += [contract_first(p.astype(BF), d) for p, d in zip(probs, ds)]
            dqs += [dot(x, k) for x, k in zip(dss, ks)]
            dks += [contract_first(x, q) for x, q in zip(dss, qs)]
        dq, dk = (jnp.concatenate(x, 1) * SCALE for x in (dqs, dks))
        put(0, at, (dq * cosine - partner(dq) * sine).astype(BF))
        put(1, at, (dk * cosine - partner(dk) * sine).astype(BF))
        put(2, at, jnp.concatenate(dvs, 1).astype(BF))


def qkv_backward_step(step, steps, dqkv, dh, u, order, gains, proj, du, total):
    @pl.when(step == 0)
    def _():
        total[...] = jnp.zeros_like(total)

    total[...] += contract_last(dqkv, stack_rows(proj))

    @pl.when(step == steps - 1)
    def _():
        unit, scale = normal(dot(u[...], order[...]))
        dxn = total[...]
        back = normal_back(dxn * gain_rows(gains)[0:1], unit, scale)
        du[...] = (dh[...] + to_absolute(back, order[...])).astype(BF)


def parted(refs, *sizes):
    out, low = [], 0
    for size in sizes:
        out.append(refs[low : low + size])
        low += size
    return *out, refs[low:]


def attn_forward_kernel(n, micro, steps, *refs):
    args, proj, out, gains, rest = parted(refs, 6, n, n, n)
    h, yn, qkv, xn = rest
    attn_forward_step(pl.program_id(0), steps, micro, *args, proj, out, gains, xn, qkv, h, yn)


def mlp_forward_kernel(n, steps, *refs):
    args, gate, up, down, rest = parted(refs, 3, n, n, n)
    mlp_forward_step(pl.program_id(0), steps, *args, gate, up, down, *rest)


def mlp_backward_kernel(n, steps, *refs):
    args, (one, two), gains, gate, up, down, rest = parted(refs, 4, 2, n, n, n, n)
    dg, dv, dh, da, total = rest
    weights = (gains, gate, up, down)
    mlp_backward_step(pl.program_id(0), steps, *args, one[...], two[...], *weights, dh, da, total, (dg, dv))


def heads_backward_kernel(n, micro, *refs):
    args, out, (dqkv,) = parted(refs, 8, n)
    width = refs[0].shape[1]

    def put(part, at, value):
        dqkv[at, part * width : (part + 1) * width] = value

    heads_backward_step(micro, *args, out, put)


def middle_kernel(n, micro, *refs):
    args, proj, out, gains, gate, up, down, outs, scratch = parted(refs, 7, n, n, n, n, n, n, 11)
    u, dz, order, cos, sin, col, row = args
    xn, qkv, lse, attended, h, yn, mid, one, two, z, du = outs
    total, dzr, dh, da, dqkv = scratch
    step = pl.program_id(0)
    turns = (cos, sin, col, row)

    @pl.when(step < 3)
    def _():
        attn_forward_step(step, 3, micro, u, order, *turns, proj, out, gains, xn, qkv, h, yn, (lse, attended))

    @pl.when((step >= 3) & (step < 6))
    def _():
        mlp_forward_step(step - 3, 3, yn, h, order, gate, up, down, z, total, (mid, one, two))

    @pl.when(step == 6)
    def _():
        dzr[...] = dot(dz[...], order[...]).astype(BF)

    @pl.when((step >= 6) & (step < 9))
    def _():
        at = pl.ds(pl.multiple_of((8 - step) * MLP_TILE, 128), MLP_TILE)
        weights = (gains, gate, up, down)
        mlp_backward_step(step - 6, 3, dzr, dz, h, order, one[:, at], two[:, at], *weights, dh, da, total)

    @pl.when(step == 9)
    def _():
        def put(part, at, value):
            dqkv[part, at] = value

        heads_backward_step(micro, da, order, *turns, qkv, lse, out, put)

    @pl.when(step >= 9)
    def _():
        qkv_backward_step(step - 9, 3, dqkv[11 - step], dh, u, order, gains, proj, du, total)


def qkv_backward_kernel(n, steps, *refs):
    (dqkv, *args), gains, proj, (du, total) = parted(refs, 4, n, n)
    qkv_backward_step(pl.program_id(0), steps, dqkv[...], *args, gains, proj, du, total)


def gain_grad(weight, grad, gain):
    return jnp.sum(weight.astype(F32) * grad, 1) / gain.astype(F32)


def columns(pieces, tile, place):
    return [pl.BlockSpec((p.shape[0], tile), lambda j: (0, place(j))) for p in pieces]


def whole(array):
    return pl.BlockSpec(array.shape, lambda j: (0,) * array.ndim)


def shape_of(rows, cols, kind=BF):
    return jax.ShapeDtypeStruct((rows, cols), kind)


def fixed(rows, cols):
    return pl.BlockSpec((rows, cols), lambda j: (0, 0))


def tiled(rows, cols, start=0, count=None):
    if count is None:
        return pl.BlockSpec((rows, cols), lambda j: (0, j))
    return pl.BlockSpec((rows, cols), lambda j: (0, jnp.clip(j - start, 0, count - 1)))


def cost(flops, weights):
    return pl.CostEstimate(flops=int(flops) // 64, bytes_accessed=int(weights * 2) // 64, transcendentals=0)


def attn_forward(u, pieces, common):
    n, (tokens, width) = len(pieces), u.shape
    steps = 3 * width // ATTN_TILE
    args = (u, *common)
    return pl.pallas_call(
        functools.partial(attn_forward_kernel, n, common[-1].shape[0], steps),
        grid=(steps,),
        in_specs=[whole(a) for a in args]
        + columns(pieces, ATTN_TILE, lambda j: j)
        + columns(pieces, width, lambda j: 3)
        + columns(pieces, 128, lambda j: 4 * width // 128),
        out_specs=[fixed(tokens, width), fixed(tokens, width)],
        out_shape=[shape_of(tokens, width, F32), shape_of(tokens, width)],
        scratch_shapes=[pltpu.VMEM((steps, tokens, ATTN_TILE), BF), pltpu.VMEM((tokens, width), BF)],
        compiler_params=PARAMS,
        cost_estimate=cost(2 * tokens * 6 * width * width, 5 * width * width),
    )(*args, *pieces, *pieces, *pieces)


def mlp_forward(yn, h, pieces, order):
    n, (tokens, width) = len(pieces), yn.shape
    hidden = pieces[0].shape[1] // 3
    steps = hidden // MLP_TILE
    args = (yn, h, order)
    return pl.pallas_call(
        functools.partial(mlp_forward_kernel, n, steps),
        grid=(steps,),
        in_specs=[whole(a) for a in args]
        + columns(pieces, MLP_TILE, lambda j: j)
        + columns(pieces, MLP_TILE, lambda j: steps + j)
        + columns(pieces, MLP_TILE, lambda j: 2 * steps + j),
        out_specs=fixed(tokens, width),
        out_shape=shape_of(tokens, width),
        scratch_shapes=[pltpu.VMEM((tokens, width), F32)],
        compiler_params=PARAMS,
        cost_estimate=cost(6 * tokens * hidden * width, 4 * hidden * width),
    )(*args, *pieces, *pieces, *pieces)


def middle(u, dz, common, pieces_a, pieces_m):
    n, (tokens, width) = len(pieces_a), u.shape
    hidden = pieces_m[0].shape[1] // 3
    args = (u, dz, *common)

    def proj_at(j):
        return jnp.where(j < 3, j, jnp.where(j < 9, 2, 11 - j))

    def mlp_at(j):
        return jnp.where(j < 6, jnp.maximum(j - 3, 0), jnp.maximum(8 - j, 0))

    kinds = [(width, BF), None, (128, F32), (width, BF), (width, F32), (width, BF)]
    kinds += [(hidden, BF)] * 3 + [(width, BF)] * 2
    cube = (3, tokens, width)
    return pl.pallas_call(
        functools.partial(middle_kernel, n, common[-1].shape[0]),
        grid=(12,),
        in_specs=[whole(a) for a in args]
        + columns(pieces_a, ATTN_TILE, proj_at)
        + columns(pieces_a, width, lambda j: 3)
        + columns(pieces_a, 128, lambda j: 4 * width // 128)
        + columns(pieces_m, MLP_TILE, mlp_at)
        + columns(pieces_m, MLP_TILE, lambda j: 3 + mlp_at(j))
        + columns(pieces_m, MLP_TILE, lambda j: 6 + mlp_at(j)),
        out_specs=[fixed(tokens, k[0]) if k else pl.BlockSpec(cube, lambda j: (0, 0, 0)) for k in kinds],
        out_shape=[shape_of(tokens, *k) if k else jax.ShapeDtypeStruct(cube, BF) for k in kinds],
        scratch_shapes=[
            pltpu.VMEM((tokens, width), F32),
            pltpu.VMEM((tokens, width), BF),
            pltpu.VMEM((tokens, width), F32),
            pltpu.VMEM((tokens, width), BF),
            pltpu.VMEM(cube, BF),
        ],
        compiler_params=PARAMS,
        cost_estimate=cost(12 * tokens * (hidden + width) * width, 12 * hidden * width),
    )(*args, *pieces_a, *pieces_a, *pieces_a, *pieces_m, *pieces_m, *pieces_m)


def mlp_backward(dzr, dz, h, one, two, pieces_a, pieces, order):
    n, (tokens, width) = len(pieces), dz.shape
    hidden = pieces[0].shape[1] // 3
    steps = hidden // MLP_TILE
    args = (dzr, dz, h, order)
    return pl.pallas_call(
        functools.partial(mlp_backward_kernel, n, steps),
        grid=(steps,),
        in_specs=[whole(a) for a in args]
        + [tiled(tokens, MLP_TILE)] * 2
        + columns(pieces_a, 128, lambda j: 4 * width // 128)
        + columns(pieces, MLP_TILE, lambda j: j)
        + columns(pieces, MLP_TILE, lambda j: steps + j)
        + columns(pieces, MLP_TILE, lambda j: 2 * steps + j),
        out_specs=[tiled(tokens, MLP_TILE)] * 2 + [fixed(tokens, width)] * 2,
        out_shape=[shape_of(tokens, hidden)] * 2
        + [shape_of(tokens, width, F32), shape_of(tokens, width)],
        scratch_shapes=[pltpu.VMEM((tokens, width), F32)],
        compiler_params=PARAMS,
        cost_estimate=cost(6 * tokens * hidden * width, 4 * hidden * width),
    )(*args, one, two, *pieces_a, *pieces, *pieces, *pieces)


def heads_backward(da, common, qkv, lse, pieces):
    n, (tokens, width) = len(pieces), da.shape
    args = (da, *common, qkv, lse)
    return pl.pallas_call(
        functools.partial(heads_backward_kernel, n, common[-1].shape[0]),
        grid=(1,),
        in_specs=[whole(a) for a in args] + columns(pieces, width, lambda j: 3),
        out_specs=fixed(tokens, 3 * width),
        out_shape=shape_of(tokens, 3 * width),
        compiler_params=PARAMS,
        cost_estimate=cost(2 * tokens * width * width, width * width),
    )(*args, *pieces)


def qkv_backward(dqkv, dh, u, order, pieces):
    n, (tokens, width) = len(pieces), u.shape
    steps = 3 * width // ATTN_TILE
    args = (dh, u, order)
    return pl.pallas_call(
        functools.partial(qkv_backward_kernel, n, steps),
        grid=(steps,),
        in_specs=[tiled(tokens, ATTN_TILE)]
        + [whole(a) for a in args]
        + columns(pieces, 128, lambda j: 4 * width // 128)
        + columns(pieces, ATTN_TILE, lambda j: j),
        out_specs=fixed(tokens, width),
        out_shape=shape_of(tokens, width),
        scratch_shapes=[pltpu.VMEM((tokens, width), F32)],
        compiler_params=PARAMS,
        cost_estimate=cost(2 * tokens * 3 * width * width, 3 * width * width),
    )(dqkv, *args, *pieces, *pieces)


def product_kernel(counts, *refs):
    count = len(counts)
    lefts, rights, rest = parted(refs, count, count)
    outs, turned = rest[:-1], rest[-1]
    step = pl.program_id(0)

    @pl.when(step == 0)
    def _():
        for k, left in enumerate(lefts):
            turned[k] = left[...].T

    begin = 0
    for which in range(count):

        @pl.when((step >= begin) & (step < begin + counts[which]))
        def _(which=which):
            value = dot(turned[which], rights[which][...])
            low = 0
            for out in outs:
                out[...] = value[low : low + out.shape[0]].astype(BF)
                low += out.shape[0]

        begin += counts[which]


def make_product(lefts, rights, tile):
    tokens = lefts[0].shape[0]
    counts = [r.shape[1] // tile for r in rights]
    steps = sum(counts)
    starts = [sum(counts[:k]) for k in range(len(counts))]

    def product(part, sizes):
        span = sum(sizes)
        return pl.pallas_call(
            functools.partial(product_kernel, counts),
            grid=(steps,),
            in_specs=[pl.BlockSpec((tokens, span), lambda j: (0, part)) for _ in lefts]
            + [tiled(tokens, tile, s, c) for s, c in zip(starts, counts)],
            out_specs=[tiled(r, tile) for r in sizes],
            out_shape=[shape_of(r, steps * tile) for r in sizes],
            scratch_shapes=[pltpu.VMEM((len(lefts), span, tokens), BF)],
            compiler_params=PARAMS,
            cost_estimate=cost(2 * tokens * span * steps * tile, span * steps * tile),
        )(*lefts, *rights)

    return product


def shards(tokens_in, attn_proj, attn_out, mlp_in, mlp_out, gain_attn, gain_mlp, lengths, cotangent):
    section = lax.axis_index("section")
    micro, slots, width = tokens_in.shape
    tokens = micro * slots
    three, hidden = attn_proj.shape[2], mlp_out.shape[2]
    padded = -(-hidden // MLP_TILE) * MLP_TILE
    gains = jnp.zeros((gain_attn.shape[1], GAIN_TILE), BF)
    gains = gains.at[:, 0].set(gain_attn[0]).at[:, 1].set(gain_mlp[0])
    gap = jnp.zeros((gain_attn.shape[1], padded - hidden), BF)
    order = relative_order(lax.axis_index("fsdp"))
    pieces_a, pieces_m, order = gather(
        jnp.concatenate([attn_proj[0], attn_out[0], gains], 1),
        jnp.concatenate([mlp_in[0, :, :hidden], gap, mlp_in[0, :, hidden:], gap, mlp_out[0], gap], 1),
        order,
    )
    base = jnp.where(section == 0, 10000.0, 160000.0).astype(F32)
    reach = jnp.where(section == 0, WINDOW / 2.0, 4.0 * slots).astype(F32)
    segment, inner = segment_info(lengths[:, 0], slots)
    half = HEAD_DIM // 2
    freqs = jnp.exp(-jnp.log(base) * (jnp.arange(half, dtype=F32) * (2.0 / HEAD_DIM)))
    angles = jnp.tile(inner.reshape(tokens, 1).astype(F32) * freqs, (1, 128 // half))
    col = jnp.stack([segment.reshape(tokens).astype(F32), inner.reshape(tokens).astype(F32)], 1)
    col = jnp.concatenate([col, jnp.broadcast_to(reach, (tokens, 126))], 1)
    row = jnp.stack([segment, inner] + [inner] * 6, 1).astype(F32)
    common = (order, jnp.cos(angles), jnp.sin(angles), col, row)

    first_in = tokens_in.reshape(tokens, width)
    hid, yn = attn_forward(first_in, pieces_a, common)
    m_block, m_near, m_near2 = pieces_m
    m_near, m_near2, yn = tie(m_near, m_near2, yn)
    m_far, m_far2 = far(m_near, m_near2)
    near_core = core(m_block, m_near, m_near2)
    far_core = core(m_far, m_far2)
    pieces_m = (m_block, m_near, m_far, m_far2, m_near2, *near_core[:2], *far_core, near_core[2])
    middle_out = mlp_forward(yn, hid, pieces_m, order)
    received = lax.ppermute(middle_out, "section", [(0, 1)])
    layer_in = jnp.where(section == 0, first_in, received)
    last_grad = cotangent.reshape(tokens, width)
    xn, qkv, lse, attended, hid, yn, mid, one, two, result, middle_grad = middle(
        layer_in, last_grad, common, pieces_a, pieces_m
    )
    received = lax.ppermute(middle_grad, "section", [(1, 0)])
    grad_out = jnp.where(section == 1, last_grad, received)
    half = width // 2
    dzr = dot(grad_out, order).astype(BF)
    dg, dv, dh, da = mlp_backward(dzr, grad_out, hid, one, two, pieces_a, pieces_m, order)
    product = make_product((yn, yn, dzr), (dg, dv, mid), MLP_TILE)
    sent_m, yn = tie(product(1, (half,))[0], yn)
    got_m = send(sent_m, "core")
    product = make_product((yn, yn, dzr), (dg, dv, mid), MLP_TILE)
    own_m = product(0, cut(half))
    got_m, da = tie(got_m, da)
    here_m, after_m, far_m, far_m2, before_m = ring_start(own_m, got_m)
    far_m, far_m2 = send(far_m.astype(BF), "first", 1), send(far_m2.astype(BF), "first", -1)
    dqkv = heads_backward(da, common, qkv, lse, pieces_a)
    far_m, far_m2, dqkv = tie(far_m, far_m2, dqkv)
    *mix_m, dqkv = tie(*ring_mix(after_m, before_m, far_m, far_m2), dqkv)
    near_m = send(mix_m[0], "first", 1), send(mix_m[1], "first", -1)
    grad_in = qkv_backward(dqkv, dh, layer_in, order, pieces_a)
    dqkv, grad_in = tie(dqkv, grad_in)
    *own_a, sent_a = make_product((xn, attended), (dqkv, da), width)(0, (*cut(half), half))
    got_a = send(sent_a, "core")
    here_a, after_a, far_a, far_a2, before_a = ring_start(own_a, got_a)
    far_a, far_a2 = send(far_a.astype(BF), "first", 1), send(far_a2.astype(BF), "first", -1)
    ends_m = direct(ring_close(here_m, *near_m))
    mix_a = ring_mix(after_a, before_a, far_a, far_a2)
    *ends_m, mix_a, mix_a2 = tie(*ends_m, *mix_a)
    near_a = send(mix_a, "first", 1), send(mix_a2, "first", -1)
    sum_m = close_z(*ends_m)
    sum_a = close_z(*direct(ring_close(here_a, *near_a)))
    grad_proj, grad_out_proj = sum_a[:, :three], sum_a[:, three:]
    grad_up = jnp.concatenate([sum_m[:, :hidden], sum_m[:, padded : padded + hidden]], 1)
    return (
        result.reshape(1, micro, slots, width),
        grad_in.reshape(1, micro, slots, width),
        grad_proj[None],
        grad_out_proj[None],
        grad_up[None],
        sum_m[:, 2 * padded : 2 * padded + hidden][None],
        gain_grad(attn_proj[0], grad_proj, gain_attn[0])[None],
        gain_grad(mlp_in[0], grad_up, gain_mlp[0])[None],
    )


def solution(mesh):
    in_specs = (
        P(None, "fsdp", None),
        P("section", "fsdp", None),
        P("section", "fsdp", None),
        P("section", "fsdp", None),
        P("section", "fsdp", None),
        P("section", "fsdp"),
        P("section", "fsdp"),
        P(None, "fsdp", None),
        P(None, "fsdp", None),
    )
    out_specs = (
        P("section", None, "fsdp", None),
        P("section", None, "fsdp", None),
        P("section", "fsdp", None),
        P("section", "fsdp", None),
        P("section", "fsdp", None),
        P("section", "fsdp", None),
        P("section", "fsdp"),
        P("section", "fsdp"),
    )
    return jax.shard_map(shards, mesh=mesh, in_specs=in_specs, out_specs=out_specs, check_vma=False)
```

```python
import functools
import math
import jax
import jax.numpy as jnp
from jax import lax
from jax.experimental import pallas as pl
from jax.experimental.pallas import tpu as pltpu
from jax.sharding import PartitionSpec as P

HEADS = 16
HEAD_DIM = 64
WINDOW = 128
EPS = 1e-05
NY, NX, NZ, NC = 4, 4, 2, 2
SHARDS = NY * NX * NZ * NC
BF = jnp.bfloat16
F32 = jnp.float32
ATTN_TILE = 1024
MLP_TILE = 896
GAIN_TILE = 128
GROUP = 8
SCALE = HEAD_DIM**-0.5
PARAMS = pltpu.CompilerParams(vmem_limit_bytes=56 * 1024 * 1024)


def split_index(i):
    return i // (NX * NZ * NC), (i // (NZ * NC)) % NX, (i // NC) % NZ, i % NC


def join_index(y, x, z, c):
    return ((y * NX + x) * NZ + z) * NC + c


def pairs(kind, step=1):
    out = []
    for i in range(SHARDS):
        y, x, z, c = split_index(i)
        if kind == "core":
            c = 1 - c
        elif kind == "z":
            z = 1 - z
        elif (kind == "first") == (c == 0):
            y = (y + step) % NY
        else:
            x = (x + step) % NX
        out.append((i, join_index(y, x, z, c)))
    return out


def send(value, kind, step=1):
    return lax.ppermute(value, "fsdp", pairs(kind, step))


def tie(*values):
    return lax.optimization_barrier(values)


def rows(*blocks):
    return jnp.concatenate(blocks, 0)


def spread(block):
    return rows(block, send(block, "second", -1), send(block, "second", 2), send(block, "second", 1))


def near(block):
    return send(block, "first", -1), send(block, "first", 1)


def far(after, before):
    half = after.shape[0] // 2
    return send(after[:half], "first", -1), send(before[half:], "first", 1)


def core(*pieces):
    return tuple(send(piece, "core") for piece in pieces)


def gather(a, m, order):
    a_z, m = tie(send(a, "z"), m)
    a, m_z, order = tie(spread(rows(a, a_z)), send(m, "z"), order)
    a_after, a_before = near(a)
    m = spread(rows(m, m_z))
    a_far, a_far2 = far(a_after, a_before)
    a_far, a_far2, m = tie(a_far, a_far2, m)
    a = (a, a_after, a_far, a_far2, a_before)
    return a + core(*a), (m, *near(m)), order


def add(left, right):
    return left.astype(F32) + right.astype(F32)


def cut(size):
    quarter = size // 4
    return quarter, quarter, quarter // 2, quarter // 2, quarter


def split(block, sizes):
    edges = [sum(sizes[:k]) for k in range(len(sizes) + 1)]
    return tuple(block[low:high] for low, high in zip(edges[:-1], edges[1:]))


def ring_start(parts, got):
    return tuple(add(part, other) for part, other in zip(parts, split(got, cut(got.shape[0]))))


def ring_mix(after, before, got_a, got_b):
    half = got_a.shape[0]
    after = rows(after[:half] + got_a.astype(F32), after[half:])
    before = rows(before[:half], before[half:] + got_b.astype(F32))
    return after.astype(BF), before.astype(BF)


def ring_close(here, got_c, got_d):
    return (here + got_c.astype(F32) + got_d.astype(F32)).astype(BF)


def direct(block):
    size = block.shape[0] // 4
    here, after, far, before = (block[k * size : (k + 1) * size] for k in range(4))
    return here, send(after, "second", 1), send(far, "second", 2), send(before, "second", -1)


def close_z(here, *got):
    block = (add(here, got[0]) + add(got[1], got[2])).astype(BF)
    mine = block.shape[0] // 2
    return add(block[:mine], send(block[mine:], "z"))


def relative_order(me):
    y, x, z, c = split_index(me)
    place = jnp.arange(SHARDS * 16, dtype=jnp.int32)
    block, inside = place // 16, place % 16
    core_at = c ^ (block // 32)
    first, second = (block // 8) % 4, (block // 2) % 4
    row_y = (y + jnp.where(core_at == 0, first, second)) % NY
    row_x = (x + jnp.where(core_at == 0, second, first)) % NX
    absolute = join_index(row_y, row_x, z ^ (block % 2), core_at) * 16 + inside
    return (place[:, None] == absolute[None, :]).astype(BF)


def dot(left, right):
    return jnp.dot(left, right, preferred_element_type=F32)


def contract_last(left, right):
    return lax.dot_general(left, right, (((1,), (1,)), ((), ())), preferred_element_type=F32)


def contract_first(left, right):
    return lax.dot_general(left, right, (((0,), (0,)), ((), ())), preferred_element_type=F32)


def normal(values):
    centre = jnp.mean(values, -1, keepdims=True)
    centred = values - centre
    scale = lax.rsqrt(jnp.mean(centred * centred, -1, keepdims=True) + EPS)
    return centred * scale, scale


def normal_back(grad, unit, scale):
    return scale * (
        grad
        - jnp.mean(grad, -1, keepdims=True)
        - unit * jnp.mean(grad * unit, -1, keepdims=True)
    )


def segment_info(lens, count):
    ends = jnp.cumsum(lens, axis=-1)
    starts = ends - lens
    places = jnp.arange(count, dtype=jnp.int32)
    segment = jnp.sum((places[:, None] >= ends[..., None, :]).astype(jnp.int32), axis=-1)
    picked = (segment[..., None] == jnp.arange(lens.shape[-1], dtype=jnp.int32)).astype(jnp.int32)
    inner = places - jnp.sum(picked * starts[..., None, :], axis=-1)
    return segment, inner


def to_absolute(values, order):
    high = values.astype(BF)
    low = (values - high.astype(F32)).astype(BF)
    return contract_last(high, order) + contract_last(low, order)


def stack_rows(refs):
    return jnp.concatenate([ref[...] for ref in refs], 0)


def gain_rows(refs):
    row = lax.broadcasted_iota(jnp.int32, (16, 128), 0)
    lane = lax.broadcasted_iota(jnp.int32, (16, 128), 1)
    return contract_last((row == lane).astype(BF), stack_rows(refs))


def partner(values):
    width = values.shape[1]
    lane = lax.broadcasted_iota(jnp.int32, values.shape, 1)
    ahead = pltpu.roll(values, width - HEAD_DIM // 2, 1)
    behind = pltpu.roll(values, HEAD_DIM // 2, 1)
    return jnp.where(lane % HEAD_DIM < HEAD_DIM // 2, -ahead, behind)


def widen(table, width):
    return jnp.concatenate([table] * (width // table.shape[1]), 1)


def pair_bias(col, row):
    same = col[:, 0:1] == row[0:1]
    near = jnp.abs(col[:, 1:2] - row[1:2]) <= col[:, 2:3]
    return jnp.where(same & near, 0.0, -1e30)


def head_of(qkv, part, head, rows):
    return qkv[part, rows, head * HEAD_DIM : (head + 1) * HEAD_DIM]


def attn_forward_step(step, steps, micro, u, order, cos, sin, col, row, proj, out, gains, xn, qkv, h, yn, saves=None):
    @pl.when(step == 0)
    def _():
        unit, _ = normal(dot(u[...], order[...]))
        xn[...] = (unit * gain_rows(gains)[0:1]).astype(BF)

    packed = dot(xn[...], stack_rows(proj))

    @pl.when(step < 2)
    def _():
        turned = packed * widen(cos[...], ATTN_TILE) + partner(packed) * widen(sin[...], ATTN_TILE)
        qkv[step] = turned.astype(BF)

    @pl.when(step == 2)
    def _():
        qkv[step] = packed.astype(BF)
        slots = u.shape[0] // micro
        lane = lax.broadcasted_iota(jnp.int32, (slots, 128), 1)
        blocks = []
        for m in range(micro):
            at = slice(m * slots, (m + 1) * slots)
            bias = pair_bias(col[at], row[m])
            log_all = jnp.zeros((slots, 128), F32)
            heads = []
            for low in range(0, HEADS, GROUP):
                group = range(low, low + GROUP)
                scores = [contract_last(head_of(qkv, 0, k, at), head_of(qkv, 1, k, at)) * SCALE + bias for k in group]
                peaks = [jnp.max(x, -1, keepdims=True) for x in scores]
                scores = [jnp.exp(x - p) for x, p in zip(scores, peaks)]
                totals = [jnp.sum(x, -1, keepdims=True) for x in scores]
                for k, p, t in zip(group, peaks, totals):
                    log_all = jnp.where(lane == k, p + jnp.log(t), log_all)
                probs = [(x * (1.0 / t)).astype(BF) for x, t in zip(scores, totals)]
                heads += [dot(x, head_of(qkv, 2, k, at)).astype(BF) for k, x in zip(group, probs)]
            if saves:
                saves[0][at] = log_all
            blocks.append(jnp.concatenate(heads, 1))
        attended = dot(jnp.concatenate(blocks, 0), order[...]).astype(BF)
        if saves:
            saves[1][...] = attended
        hidden = u[...].astype(F32) + dot(attended, stack_rows(out))
        h[...] = hidden
        unit, _ = normal(hidden)
        gain = contract_last(gain_rows(gains).astype(BF), order[...])[1:2]
        yn[...] = dot((unit * gain).astype(BF), order[...]).astype(BF)


def mlp_forward_step(step, steps, yn, h, order, gate, up, down, z, total, saves=None):
    g = dot(yn[...], stack_rows(gate))
    v = dot(yn[...], stack_rows(up))
    cdf = 0.5 * (1.0 + lax.erf(g * math.sqrt(0.5)))
    unit = g * cdf
    mid = (unit * v).astype(BF)
    if saves:
        slope = cdf + g * jnp.exp(-0.5 * g * g) * (1.0 / math.sqrt(2.0 * math.pi))
        at = pl.ds(pl.multiple_of(step * MLP_TILE, 128), MLP_TILE)
        for ref, value in zip(saves, (mid, (v * slope).astype(BF), unit.astype(BF))):
            ref[:, at] = value
    part = contract_last(mid, stack_rows(down))

    @pl.when(step == 0)
    def _():
        total[...] = part

    @pl.when(step > 0)
    def _():
        total[...] += part

    @pl.when(step == steps - 1)
    def _():
        z[...] = (h[...] + to_absolute(total[...], order[...])).astype(BF)


def mlp_backward_step(step, steps, dzr, dz, h, order, one, two, gains, gate, up, down, dh, da, total, saves=None):
    @pl.when(step == 0)
    def _():
        total[...] = jnp.zeros_like(total)

    dmid = dot(dzr[...], stack_rows(down))
    dg = (dmid * one.astype(F32)).astype(BF)
    dv = (dmid * two.astype(F32)).astype(BF)
    if saves:
        saves[0][...] = dg
        saves[1][...] = dv
    total[...] += contract_last(dg, stack_rows(gate)) + contract_last(dv, stack_rows(up))

    @pl.when(step == steps - 1)
    def _():
        dyn = to_absolute(total[...], order[...])
        unit, scale = normal(h[...])
        gain = contract_last(gain_rows(gains).astype(BF), order[...])[1:2]
        grad = dz[...].astype(F32) + normal_back(dyn * gain, unit, scale)
        dh[...] = grad
        da[...] = grad.astype(BF)


def heads_backward_step(micro, da, order, cos, sin, col, row, qkv, lse, out, put):
    tokens, width = da.shape
    rel = contract_last(da[...], stack_rows(out)).astype(BF)
    do_all = contract_last(rel, order[...]).astype(BF)
    slots = tokens // micro
    for m in range(micro):
        at = slice(m * slots, (m + 1) * slots)
        bias = pair_bias(col[at], row[m])
        log_all = lse[at]
        cosine, sine = widen(cos[at], width), widen(sin[at], width)
        dqs, dks, dvs = [], [], []
        for low in range(0, HEADS, GROUP):
            group = range(low, low + GROUP)
            qs, ks, vs = ([head_of(qkv, part, k, at) for k in group] for part in range(3))
            ds = [do_all[at, k * HEAD_DIM : (k + 1) * HEAD_DIM] for k in group]
            probs = [contract_last(q, k) * SCALE + bias for q, k in zip(qs, ks)]
            probs = [jnp.exp(x - log_all[:, k : k + 1]) for x, k in zip(probs, group)]
            dps = [contract_last(d, v) for d, v in zip(ds, vs)]
            dss = [(p * (x - jnp.sum(p * x, -1, keepdims=True))).astype(BF) for p, x in zip(probs, dps)]
            dvs += [contract_first(p.astype(BF), d) for p, d in zip(probs, ds)]
            dqs += [dot(x, k) for x, k in zip(dss, ks)]
            dks += [contract_first(x, q) for x, q in zip(dss, qs)]
        dq, dk = (jnp.concatenate(x, 1) * SCALE for x in (dqs, dks))
        put(0, at, (dq * cosine - partner(dq) * sine).astype(BF))
        put(1, at, (dk * cosine - partner(dk) * sine).astype(BF))
        put(2, at, jnp.concatenate(dvs, 1).astype(BF))


def qkv_backward_step(step, steps, dqkv, dh, u, order, gains, proj, du, total):
    @pl.when(step == 0)
    def _():
        total[...] = jnp.zeros_like(total)

    total[...] += contract_last(dqkv, stack_rows(proj))

    @pl.when(step == steps - 1)
    def _():
        unit, scale = normal(dot(u[...], order[...]))
        dxn = total[...]
        back = normal_back(dxn * gain_rows(gains)[0:1], unit, scale)
        du[...] = (dh[...] + to_absolute(back, order[...])).astype(BF)


def parted(refs, *sizes):
    out, low = [], 0
    for size in sizes:
        out.append(refs[low : low + size])
        low += size
    return *out, refs[low:]


def attn_forward_kernel(n, micro, steps, *refs):
    args, proj, out, gains, rest = parted(refs, 6, n, n, n)
    h, yn, qkv, xn = rest
    attn_forward_step(pl.program_id(0), steps, micro, *args, proj, out, gains, xn, qkv, h, yn)


def mlp_forward_kernel(n, steps, *refs):
    args, gate, up, down, rest = parted(refs, 3, n, n, n)
    mlp_forward_step(pl.program_id(0), steps, *args, gate, up, down, *rest)


def mlp_backward_kernel(n, steps, *refs):
    args, (one, two), gains, gate, up, down, rest = parted(refs, 3, 2, n, n, n, n)
    dzr, dg, dv, dh, da, total = rest
    weights = (gains, gate, up, down)
    step = pl.program_id(0)

    @pl.when(step == 0)
    def _():
        dzr[...] = dot(args[0][...], args[2][...]).astype(BF)

    mlp_backward_step(step, steps, dzr, *args, one[...], two[...], *weights, dh, da, total, (dg, dv))


def heads_backward_kernel(n, micro, *refs):
    args, out, (dqkv,) = parted(refs, 8, n)
    width = refs[0].shape[1]

    def put(part, at, value):
        dqkv[at, part * width : (part + 1) * width] = value

    heads_backward_step(micro, *args, out, put)


def middle_kernel(n, micro, *refs):
    args, proj, out, gains, gate, up, down, outs, scratch = parted(refs, 7, n, n, n, n, n, n, 11)
    u, dz, order, cos, sin, col, row = args
    xn, qkv, lse, attended, h, yn, mid, one, two, z, du = outs
    total, dzr, dh, da, dqkv = scratch
    step = pl.program_id(0)
    turns = (cos, sin, col, row)

    @pl.when(step < 3)
    def _():
        attn_forward_step(step, 3, micro, u, order, *turns, proj, out, gains, xn, qkv, h, yn, (lse, attended))

    @pl.when((step >= 3) & (step < 6))
    def _():
        mlp_forward_step(step - 3, 3, yn, h, order, gate, up, down, z, total, (mid, one, two))

    @pl.when(step == 6)
    def _():
        dzr[...] = dot(dz[...], order[...]).astype(BF)

    @pl.when((step >= 6) & (step < 9))
    def _():
        at = pl.ds(pl.multiple_of((8 - step) * MLP_TILE, 128), MLP_TILE)
        weights = (gains, gate, up, down)
        mlp_backward_step(step - 6, 3, dzr, dz, h, order, one[:, at], two[:, at], *weights, dh, da, total)

    @pl.when(step == 9)
    def _():
        def put(part, at, value):
            dqkv[part, at] = value

        heads_backward_step(micro, da, order, *turns, qkv, lse, out, put)

    @pl.when(step >= 9)
    def _():
        qkv_backward_step(step - 9, 3, dqkv[11 - step], dh, u, order, gains, proj, du, total)


def qkv_backward_kernel(n, steps, *refs):
    (dqkv, *args), gains, proj, (du, total) = parted(refs, 4, n, n)
    qkv_backward_step(pl.program_id(0), steps, dqkv[...], *args, gains, proj, du, total)


def gain_grad(weight, grad, gain):
    return jnp.sum(weight.astype(F32) * grad, 1) / gain.astype(F32)


def columns(pieces, tile, place):
    return [pl.BlockSpec((p.shape[0], tile), lambda j: (0, place(j))) for p in pieces]


def whole(array):
    return pl.BlockSpec(array.shape, lambda j: (0,) * array.ndim)


def shape_of(rows, cols, kind=BF):
    return jax.ShapeDtypeStruct((rows, cols), kind)


def fixed(rows, cols):
    return pl.BlockSpec((rows, cols), lambda j: (0, 0))


def tiled(rows, cols, start=0, count=None):
    if count is None:
        return pl.BlockSpec((rows, cols), lambda j: (0, j))
    return pl.BlockSpec((rows, cols), lambda j: (0, jnp.clip(j - start, 0, count - 1)))


def cost(flops, weights):
    return pl.CostEstimate(flops=int(flops) // 64, bytes_accessed=int(weights * 2) // 64, transcendentals=0)


def attn_forward(u, pieces, common):
    n, (tokens, width) = len(pieces), u.shape
    steps = 3 * width // ATTN_TILE
    args = (u, *common)
    return pl.pallas_call(
        functools.partial(attn_forward_kernel, n, common[-1].shape[0], steps),
        grid=(steps,),
        in_specs=[whole(a) for a in args]
        + columns(pieces, ATTN_TILE, lambda j: j)
        + columns(pieces, width, lambda j: 3)
        + columns(pieces, 128, lambda j: 4 * width // 128),
        out_specs=[fixed(tokens, width), fixed(tokens, width)],
        out_shape=[shape_of(tokens, width, F32), shape_of(tokens, width)],
        scratch_shapes=[pltpu.VMEM((steps, tokens, ATTN_TILE), BF), pltpu.VMEM((tokens, width), BF)],
        compiler_params=PARAMS,
        cost_estimate=cost(2 * tokens * 6 * width * width, 5 * width * width),
    )(*args, *pieces, *pieces, *pieces)


def mlp_forward(yn, h, pieces, order):
    n, (tokens, width) = len(pieces), yn.shape
    hidden = pieces[0].shape[1] // 3
    steps = hidden // MLP_TILE
    args = (yn, h, order)
    return pl.pallas_call(
        functools.partial(mlp_forward_kernel, n, steps),
        grid=(steps,),
        in_specs=[whole(a) for a in args]
        + columns(pieces, MLP_TILE, lambda j: j)
        + columns(pieces, MLP_TILE, lambda j: steps + j)
        + columns(pieces, MLP_TILE, lambda j: 2 * steps + j),
        out_specs=fixed(tokens, width),
        out_shape=shape_of(tokens, width),
        scratch_shapes=[pltpu.VMEM((tokens, width), F32)],
        compiler_params=PARAMS,
        cost_estimate=cost(6 * tokens * hidden * width, 4 * hidden * width),
    )(*args, *pieces, *pieces, *pieces)


def middle(u, dz, common, pieces_a, pieces_m):
    n, (tokens, width) = len(pieces_a), u.shape
    hidden = pieces_m[0].shape[1] // 3
    args = (u, dz, *common)

    def proj_at(j):
        return jnp.where(j < 3, j, jnp.where(j < 9, 2, 11 - j))

    def mlp_at(j):
        return jnp.where(j < 6, jnp.maximum(j - 3, 0), jnp.maximum(8 - j, 0))

    kinds = [(width, BF), None, (128, F32), (width, BF), (width, F32), (width, BF)]
    kinds += [(hidden, BF)] * 3 + [(width, BF)] * 2
    cube = (3, tokens, width)
    return pl.pallas_call(
        functools.partial(middle_kernel, n, common[-1].shape[0]),
        grid=(12,),
        in_specs=[whole(a) for a in args]
        + columns(pieces_a, ATTN_TILE, proj_at)
        + columns(pieces_a, width, lambda j: 3)
        + columns(pieces_a, 128, lambda j: 4 * width // 128)
        + columns(pieces_m, MLP_TILE, mlp_at)
        + columns(pieces_m, MLP_TILE, lambda j: 3 + mlp_at(j))
        + columns(pieces_m, MLP_TILE, lambda j: 6 + mlp_at(j)),
        out_specs=[fixed(tokens, k[0]) if k else pl.BlockSpec(cube, lambda j: (0, 0, 0)) for k in kinds],
        out_shape=[shape_of(tokens, *k) if k else jax.ShapeDtypeStruct(cube, BF) for k in kinds],
        scratch_shapes=[
            pltpu.VMEM((tokens, width), F32),
            pltpu.VMEM((tokens, width), BF),
            pltpu.VMEM((tokens, width), F32),
            pltpu.VMEM((tokens, width), BF),
            pltpu.VMEM(cube, BF),
        ],
        compiler_params=PARAMS,
        cost_estimate=cost(12 * tokens * (hidden + width) * width, 12 * hidden * width),
    )(*args, *pieces_a, *pieces_a, *pieces_a, *pieces_m, *pieces_m, *pieces_m)


def mlp_backward(dz, h, one, two, pieces_a, pieces, order):
    n, (tokens, width) = len(pieces), dz.shape
    hidden = pieces[0].shape[1] // 3
    steps = hidden // MLP_TILE
    args = (dz, h, order)
    return pl.pallas_call(
        functools.partial(mlp_backward_kernel, n, steps),
        grid=(steps,),
        in_specs=[whole(a) for a in args]
        + [tiled(tokens, MLP_TILE)] * 2
        + columns(pieces_a, 128, lambda j: 4 * width // 128)
        + columns(pieces, MLP_TILE, lambda j: j)
        + columns(pieces, MLP_TILE, lambda j: steps + j)
        + columns(pieces, MLP_TILE, lambda j: 2 * steps + j),
        out_specs=[fixed(tokens, width)] + [tiled(tokens, MLP_TILE)] * 2 + [fixed(tokens, width)] * 2,
        out_shape=[shape_of(tokens, width)]
        + [shape_of(tokens, hidden)] * 2
        + [shape_of(tokens, width, F32), shape_of(tokens, width)],
        scratch_shapes=[pltpu.VMEM((tokens, width), F32)],
        compiler_params=PARAMS,
        cost_estimate=cost(6 * tokens * hidden * width, 4 * hidden * width),
    )(*args, one, two, *pieces_a, *pieces, *pieces, *pieces)


def heads_backward(da, common, qkv, lse, pieces):
    n, (tokens, width) = len(pieces), da.shape
    args = (da, *common, qkv, lse)
    return pl.pallas_call(
        functools.partial(heads_backward_kernel, n, common[-1].shape[0]),
        grid=(1,),
        in_specs=[whole(a) for a in args] + columns(pieces, width, lambda j: 3),
        out_specs=fixed(tokens, 3 * width),
        out_shape=shape_of(tokens, 3 * width),
        compiler_params=PARAMS,
        cost_estimate=cost(2 * tokens * width * width, width * width),
    )(*args, *pieces)


def qkv_backward(dqkv, dh, u, order, pieces):
    n, (tokens, width) = len(pieces), u.shape
    steps = 3 * width // ATTN_TILE
    args = (dh, u, order)
    return pl.pallas_call(
        functools.partial(qkv_backward_kernel, n, steps),
        grid=(steps,),
        in_specs=[tiled(tokens, ATTN_TILE)]
        + [whole(a) for a in args]
        + columns(pieces, 128, lambda j: 4 * width // 128)
        + columns(pieces, ATTN_TILE, lambda j: j),
        out_specs=fixed(tokens, width),
        out_shape=shape_of(tokens, width),
        scratch_shapes=[pltpu.VMEM((tokens, width), F32)],
        compiler_params=PARAMS,
        cost_estimate=cost(2 * tokens * 3 * width * width, 3 * width * width),
    )(dqkv, *args, *pieces, *pieces)


def product_kernel(counts, *refs):
    count = len(counts)
    lefts, rights, rest = parted(refs, count, count)
    outs, turned = rest[:-1], rest[-1]
    step = pl.program_id(0)

    @pl.when(step == 0)
    def _():
        for k, left in enumerate(lefts):
            turned[k] = left[...].T

    begin = 0
    for which in range(count):

        @pl.when((step >= begin) & (step < begin + counts[which]))
        def _(which=which):
            value = dot(turned[which], rights[which][...])
            low = 0
            for out in outs:
                out[...] = value[low : low + out.shape[0]].astype(BF)
                low += out.shape[0]

        begin += counts[which]


def make_product(lefts, rights, tile):
    tokens = lefts[0].shape[0]
    counts = [r.shape[1] // tile for r in rights]
    steps = sum(counts)
    starts = [sum(counts[:k]) for k in range(len(counts))]

    def product(part, sizes):
        span = sum(sizes)
        return pl.pallas_call(
            functools.partial(product_kernel, counts),
            grid=(steps,),
            in_specs=[pl.BlockSpec((tokens, span), lambda j: (0, part)) for _ in lefts]
            + [tiled(tokens, tile, s, c) for s, c in zip(starts, counts)],
            out_specs=[tiled(r, tile) for r in sizes],
            out_shape=[shape_of(r, steps * tile) for r in sizes],
            scratch_shapes=[pltpu.VMEM((len(lefts), span, tokens), BF)],
            compiler_params=PARAMS,
            cost_estimate=cost(2 * tokens * span * steps * tile, span * steps * tile),
        )(*lefts, *rights)

    return product


def shards(tokens_in, attn_proj, attn_out, mlp_in, mlp_out, gain_attn, gain_mlp, lengths, cotangent):
    section = lax.axis_index("section")
    micro, slots, width = tokens_in.shape
    tokens = micro * slots
    three, hidden = attn_proj.shape[2], mlp_out.shape[2]
    padded = -(-hidden // MLP_TILE) * MLP_TILE
    gains = jnp.zeros((gain_attn.shape[1], GAIN_TILE), BF)
    gains = gains.at[:, 0].set(gain_attn[0]).at[:, 1].set(gain_mlp[0])
    gap = jnp.zeros((gain_attn.shape[1], padded - hidden), BF)
    order = relative_order(lax.axis_index("fsdp"))
    pieces_a, pieces_m, order = gather(
        jnp.concatenate([attn_proj[0], attn_out[0], gains], 1),
        jnp.concatenate([mlp_in[0, :, :hidden], gap, mlp_in[0, :, hidden:], gap, mlp_out[0], gap], 1),
        order,
    )
    base = jnp.where(section == 0, 10000.0, 160000.0).astype(F32)
    reach = jnp.where(section == 0, WINDOW / 2.0, 4.0 * slots).astype(F32)
    segment, inner = segment_info(lengths[:, 0], slots)
    half = HEAD_DIM // 2
    freqs = jnp.exp(-jnp.log(base) * (jnp.arange(half, dtype=F32) * (2.0 / HEAD_DIM)))
    angles = jnp.tile(inner.reshape(tokens, 1).astype(F32) * freqs, (1, 128 // half))
    col = jnp.stack([segment.reshape(tokens).astype(F32), inner.reshape(tokens).astype(F32)], 1)
    col = jnp.concatenate([col, jnp.broadcast_to(reach, (tokens, 126))], 1)
    row = jnp.stack([segment, inner] + [inner] * 6, 1).astype(F32)
    common = (order, jnp.cos(angles), jnp.sin(angles), col, row)

    first_in = tokens_in.reshape(tokens, width)
    hid, yn = attn_forward(first_in, pieces_a, common)
    m_block, m_near, m_near2 = pieces_m
    m_near, m_near2, yn = tie(m_near, m_near2, yn)
    m_far, m_far2 = far(m_near, m_near2)
    near_core = core(m_block, m_near, m_near2)
    far_core = core(m_far, m_far2)
    pieces_m = (m_block, m_near, m_far, m_far2, m_near2, *near_core[:2], *far_core, near_core[2])
    middle_out = mlp_forward(yn, hid, pieces_m, order)
    received = lax.ppermute(middle_out, "section", [(0, 1)])
    layer_in = jnp.where(section == 0, first_in, received)
    last_grad = cotangent.reshape(tokens, width)
    xn, qkv, lse, attended, hid, yn, mid, one, two, result, middle_grad = middle(
        layer_in, last_grad, common, pieces_a, pieces_m
    )
    received = lax.ppermute(middle_grad, "section", [(1, 0)])
    grad_out = jnp.where(section == 1, last_grad, received)
    half = width // 2
    dzr, dg, dv, dh, da = mlp_backward(grad_out, hid, one, two, pieces_a, pieces_m, order)
    product = make_product((yn, yn, dzr), (dg, dv, mid), MLP_TILE)
    sent_m, yn = tie(product(1, (half,))[0], yn)
    got_m = send(sent_m, "core")
    product = make_product((yn, yn, dzr), (dg, dv, mid), MLP_TILE)
    own_m = product(0, cut(half))
    got_m, da = tie(got_m, da)
    here_m, after_m, far_m, far_m2, before_m = ring_start(own_m, got_m)
    far_m, far_m2 = send(far_m.astype(BF), "first", 1), send(far_m2.astype(BF), "first", -1)
    dqkv = heads_backward(da, common, qkv, lse, pieces_a)
    far_m, far_m2, dqkv = tie(far_m, far_m2, dqkv)
    *mix_m, dqkv = tie(*ring_mix(after_m, before_m, far_m, far_m2), dqkv)
    near_m = send(mix_m[0], "first", 1), send(mix_m[1], "first", -1)
    *own_a, sent_a = make_product((xn, attended), (dqkv, da), width)(0, (*cut(half), half))
    sent_a, dh = tie(sent_a, dh)
    grad_in = qkv_backward(dqkv, dh, layer_in, order, pieces_a)
    got_a = send(sent_a, "core")
    here_a, after_a, far_a, far_a2, before_a = ring_start(own_a, got_a)
    far_a, far_a2 = send(far_a.astype(BF), "first", 1), send(far_a2.astype(BF), "first", -1)
    *near_m, grad_in = tie(*near_m, grad_in)
    ends_m = direct(ring_close(here_m, *near_m))
    mix_a = ring_mix(after_a, before_a, far_a, far_a2)
    *ends_m, mix_a, mix_a2 = tie(*ends_m, *mix_a)
    near_a = send(mix_a, "first", 1), send(mix_a2, "first", -1)
    sum_m = close_z(*ends_m)
    sum_a = close_z(*direct(ring_close(here_a, *near_a)))
    grad_proj, grad_out_proj = sum_a[:, :three], sum_a[:, three:]
    grad_up = jnp.concatenate([sum_m[:, :hidden], sum_m[:, padded : padded + hidden]], 1)
    return (
        result.reshape(1, micro, slots, width),
        grad_in.reshape(1, micro, slots, width),
        grad_proj[None],
        grad_out_proj[None],
        grad_up[None],
        sum_m[:, 2 * padded : 2 * padded + hidden][None],
        gain_grad(attn_proj[0], grad_proj, gain_attn[0])[None],
        gain_grad(mlp_in[0], grad_up, gain_mlp[0])[None],
    )


def solution(mesh):
    in_specs = (
        P(None, "fsdp", None),
        P("section", "fsdp", None),
        P("section", "fsdp", None),
        P("section", "fsdp", None),
        P("section", "fsdp", None),
        P("section", "fsdp"),
        P("section", "fsdp"),
        P(None, "fsdp", None),
        P(None, "fsdp", None),
    )
    out_specs = (
        P("section", None, "fsdp", None),
        P("section", None, "fsdp", None),
        P("section", "fsdp", None),
        P("section", "fsdp", None),
        P("section", "fsdp", None),
        P("section", "fsdp", None),
        P("section", "fsdp"),
        P("section", "fsdp"),
    )
    return jax.shard_map(shards, mesh=mesh, in_specs=in_specs, out_specs=out_specs, check_vma=False)
```

```python
import functools
import math
import jax
import jax.numpy as jnp
from jax import lax
from jax.experimental import pallas as pl
from jax.experimental.pallas import tpu as pltpu
from jax.sharding import PartitionSpec as P

HEADS = 16
HEAD_DIM = 64
WINDOW = 128
EPS = 1e-05
NY, NX, NZ, NC = 4, 4, 2, 2
SHARDS = NY * NX * NZ * NC
BF = jnp.bfloat16
F32 = jnp.float32
ATTN_TILE = 1024
MLP_TILE = 896
GAIN_TILE = 128
GROUP = 8
SCALE = HEAD_DIM**-0.5
PARAMS = pltpu.CompilerParams(vmem_limit_bytes=56 * 1024 * 1024)


def split_index(i):
    return i // (NX * NZ * NC), (i // (NZ * NC)) % NX, (i // NC) % NZ, i % NC


def join_index(y, x, z, c):
    return ((y * NX + x) * NZ + z) * NC + c


def pairs(kind, step=1):
    out = []
    for i in range(SHARDS):
        y, x, z, c = split_index(i)
        if kind == "core":
            c = 1 - c
        elif kind == "z":
            z = 1 - z
        elif (kind == "first") == (c == 0):
            y = (y + step) % NY
        else:
            x = (x + step) % NX
        out.append((i, join_index(y, x, z, c)))
    return out


def send(value, kind, step=1):
    return lax.ppermute(value, "fsdp", pairs(kind, step))


def tie(*values):
    return lax.optimization_barrier(values)


def rows(*blocks):
    return jnp.concatenate(blocks, 0)


def spread(block):
    return rows(block, send(block, "second", -1), send(block, "second", 2), send(block, "second", 1))


def near(block):
    return send(block, "first", -1), send(block, "first", 1)


def far(after, before):
    half = after.shape[0] // 2
    return send(after[:half], "first", -1), send(before[half:], "first", 1)


def core(*pieces):
    return tuple(send(piece, "core") for piece in pieces)


def gather(a, m, order):
    a_z, m = tie(send(a, "z"), m)
    a, m_z, order = tie(spread(rows(a, a_z)), send(m, "z"), order)
    a_after, a_before = near(a)
    m = spread(rows(m, m_z))
    a_far, a_far2 = far(a_after, a_before)
    a_far, a_far2, m = tie(a_far, a_far2, m)
    a = (a, a_after, a_far, a_far2, a_before)
    return a + core(*a), (m, *near(m)), order


def add(left, right):
    return left.astype(F32) + right.astype(F32)


def cut(size):
    quarter = size // 4
    return quarter, quarter, quarter // 2, quarter // 2, quarter


def split(block, sizes):
    edges = [sum(sizes[:k]) for k in range(len(sizes) + 1)]
    return tuple(block[low:high] for low, high in zip(edges[:-1], edges[1:]))


def ring_start(parts, got):
    return tuple(add(part, other) for part, other in zip(parts, split(got, cut(got.shape[0]))))


def ring_mix(after, before, got_a, got_b):
    half = got_a.shape[0]
    after = rows(after[:half] + got_a.astype(F32), after[half:])
    before = rows(before[:half], before[half:] + got_b.astype(F32))
    return after.astype(BF), before.astype(BF)


def ring_close(here, got_c, got_d):
    return (here + got_c.astype(F32) + got_d.astype(F32)).astype(BF)


def direct(block):
    size = block.shape[0] // 4
    here, after, far, before = (block[k * size : (k + 1) * size] for k in range(4))
    return here, send(after, "second", 1), send(far, "second", 2), send(before, "second", -1)


def close_z(here, *got):
    block = (add(here, got[0]) + add(got[1], got[2])).astype(BF)
    mine = block.shape[0] // 2
    return add(block[:mine], send(block[mine:], "z"))


def relative_order(me):
    y, x, z, c = split_index(me)
    place = jnp.arange(SHARDS * 16, dtype=jnp.int32)
    block, inside = place // 16, place % 16
    core_at = c ^ (block // 32)
    first, second = (block // 8) % 4, (block // 2) % 4
    row_y = (y + jnp.where(core_at == 0, first, second)) % NY
    row_x = (x + jnp.where(core_at == 0, second, first)) % NX
    absolute = join_index(row_y, row_x, z ^ (block % 2), core_at) * 16 + inside
    return (place[:, None] == absolute[None, :]).astype(BF)


def dot(left, right):
    return jnp.dot(left, right, preferred_element_type=F32)


def contract_last(left, right):
    return lax.dot_general(left, right, (((1,), (1,)), ((), ())), preferred_element_type=F32)


def contract_first(left, right):
    return lax.dot_general(left, right, (((0,), (0,)), ((), ())), preferred_element_type=F32)


def normal(values):
    centre = jnp.mean(values, -1, keepdims=True)
    centred = values - centre
    scale = lax.rsqrt(jnp.mean(centred * centred, -1, keepdims=True) + EPS)
    return centred * scale, scale


def normal_back(grad, unit, scale):
    return scale * (
        grad
        - jnp.mean(grad, -1, keepdims=True)
        - unit * jnp.mean(grad * unit, -1, keepdims=True)
    )


def segment_info(lens, count):
    ends = jnp.cumsum(lens, axis=-1)
    starts = ends - lens
    places = jnp.arange(count, dtype=jnp.int32)
    segment = jnp.sum((places[:, None] >= ends[..., None, :]).astype(jnp.int32), axis=-1)
    picked = (segment[..., None] == jnp.arange(lens.shape[-1], dtype=jnp.int32)).astype(jnp.int32)
    inner = places - jnp.sum(picked * starts[..., None, :], axis=-1)
    return segment, inner


def to_absolute(values, order):
    high = values.astype(BF)
    low = (values - high.astype(F32)).astype(BF)
    return contract_last(high, order) + contract_last(low, order)


def stack_rows(refs):
    return jnp.concatenate([ref[...] for ref in refs], 0)


def gain_rows(refs):
    row = lax.broadcasted_iota(jnp.int32, (16, 128), 0)
    lane = lax.broadcasted_iota(jnp.int32, (16, 128), 1)
    return contract_last((row == lane).astype(BF), stack_rows(refs))


def partner(values):
    width = values.shape[1]
    lane = lax.broadcasted_iota(jnp.int32, values.shape, 1)
    ahead = pltpu.roll(values, width - HEAD_DIM // 2, 1)
    behind = pltpu.roll(values, HEAD_DIM // 2, 1)
    return jnp.where(lane % HEAD_DIM < HEAD_DIM // 2, -ahead, behind)


def widen(table, width):
    return jnp.concatenate([table] * (width // table.shape[1]), 1)


def pair_bias(col, row):
    same = col[:, 0:1] == row[0:1]
    near = jnp.abs(col[:, 1:2] - row[1:2]) <= col[:, 2:3]
    return jnp.where(same & near, 0.0, -1e30)


def head_of(qkv, part, head, rows):
    return qkv[part, rows, head * HEAD_DIM : (head + 1) * HEAD_DIM]


def attn_forward_step(step, steps, micro, u, order, cos, sin, col, row, proj, out, gains, xn, qkv, h, yn, saves=None):
    @pl.when(step == 0)
    def _():
        unit, _ = normal(dot(u[...], order[...]))
        xn[...] = (unit * gain_rows(gains)[0:1]).astype(BF)

    packed = dot(xn[...], stack_rows(proj))

    @pl.when(step < 2)
    def _():
        turned = packed * widen(cos[...], ATTN_TILE) + partner(packed) * widen(sin[...], ATTN_TILE)
        qkv[step] = turned.astype(BF)

    @pl.when(step == 2)
    def _():
        qkv[step] = packed.astype(BF)
        slots = u.shape[0] // micro
        lane = lax.broadcasted_iota(jnp.int32, (slots, 128), 1)
        blocks = []
        for m in range(micro):
            at = slice(m * slots, (m + 1) * slots)
            bias = pair_bias(col[at], row[m])
            log_all = jnp.zeros((slots, 128), F32)
            heads = []
            for low in range(0, HEADS, GROUP):
                group = range(low, low + GROUP)
                scores = [contract_last(head_of(qkv, 0, k, at), head_of(qkv, 1, k, at)) * SCALE + bias for k in group]
                peaks = [jnp.max(x, -1, keepdims=True) for x in scores]
                scores = [jnp.exp(x - p) for x, p in zip(scores, peaks)]
                totals = [jnp.sum(x, -1, keepdims=True) for x in scores]
                for k, p, t in zip(group, peaks, totals):
                    log_all = jnp.where(lane == k, p + jnp.log(t), log_all)
                probs = [(x * (1.0 / t)).astype(BF) for x, t in zip(scores, totals)]
                heads += [dot(x, head_of(qkv, 2, k, at)).astype(BF) for k, x in zip(group, probs)]
            if saves:
                saves[0][at] = log_all
            blocks.append(jnp.concatenate(heads, 1))
        attended = dot(jnp.concatenate(blocks, 0), order[...]).astype(BF)
        if saves:
            saves[1][...] = attended
        hidden = u[...].astype(F32) + dot(attended, stack_rows(out))
        h[...] = hidden
        unit, _ = normal(hidden)
        gain = contract_last(gain_rows(gains).astype(BF), order[...])[1:2]
        yn[...] = dot((unit * gain).astype(BF), order[...]).astype(BF)


def mlp_forward_step(step, steps, yn, h, order, gate, up, down, z, total, saves=None):
    g = dot(yn[...], stack_rows(gate))
    v = dot(yn[...], stack_rows(up))
    cdf = 0.5 * (1.0 + lax.erf(g * math.sqrt(0.5)))
    unit = g * cdf
    mid = (unit * v).astype(BF)
    if saves:
        slope = cdf + g * jnp.exp(-0.5 * g * g) * (1.0 / math.sqrt(2.0 * math.pi))
        at = pl.ds(pl.multiple_of(step * MLP_TILE, 128), MLP_TILE)
        for ref, value in zip(saves, (mid, (v * slope).astype(BF), unit.astype(BF))):
            ref[:, at] = value
    part = contract_last(mid, stack_rows(down))

    @pl.when(step == 0)
    def _():
        total[...] = part

    @pl.when(step > 0)
    def _():
        total[...] += part

    @pl.when(step == steps - 1)
    def _():
        z[...] = (h[...] + to_absolute(total[...], order[...])).astype(BF)


def mlp_backward_step(step, steps, dzr, dz, h, order, one, two, gains, gate, up, down, dh, da, total, saves=None):
    @pl.when(step == 0)
    def _():
        total[...] = jnp.zeros_like(total)

    dmid = dot(dzr[...], stack_rows(down))
    dg = (dmid * one.astype(F32)).astype(BF)
    dv = (dmid * two.astype(F32)).astype(BF)
    if saves:
        saves[0][...] = dg
        saves[1][...] = dv
    total[...] += contract_last(dg, stack_rows(gate)) + contract_last(dv, stack_rows(up))

    @pl.when(step == steps - 1)
    def _():
        dyn = to_absolute(total[...], order[...])
        unit, scale = normal(h[...])
        gain = contract_last(gain_rows(gains).astype(BF), order[...])[1:2]
        grad = dz[...].astype(F32) + normal_back(dyn * gain, unit, scale)
        dh[...] = grad
        da[...] = grad.astype(BF)


def heads_backward_step(micro, da, order, cos, sin, col, row, qkv, lse, out, put):
    tokens, width = da.shape
    rel = contract_last(da[...], stack_rows(out)).astype(BF)
    do_all = contract_last(rel, order[...]).astype(BF)
    slots = tokens // micro
    for m in range(micro):
        at = slice(m * slots, (m + 1) * slots)
        bias = pair_bias(col[at], row[m])
        log_all = lse[at]
        cosine, sine = widen(cos[at], width), widen(sin[at], width)
        dqs, dks, dvs = [], [], []
        for low in range(0, HEADS, GROUP):
            group = range(low, low + GROUP)
            qs, ks, vs = ([head_of(qkv, part, k, at) for k in group] for part in range(3))
            ds = [do_all[at, k * HEAD_DIM : (k + 1) * HEAD_DIM] for k in group]
            probs = [contract_last(q, k) * SCALE + bias for q, k in zip(qs, ks)]
            probs = [jnp.exp(x - log_all[:, k : k + 1]) for x, k in zip(probs, group)]
            dps = [contract_last(d, v) for d, v in zip(ds, vs)]
            dss = [(p * (x - jnp.sum(p * x, -1, keepdims=True))).astype(BF) for p, x in zip(probs, dps)]
            dvs += [contract_first(p.astype(BF), d) for p, d in zip(probs, ds)]
            dqs += [dot(x, k) for x, k in zip(dss, ks)]
            dks += [contract_first(x, q) for x, q in zip(dss, qs)]
        dq, dk = (jnp.concatenate(x, 1) * SCALE for x in (dqs, dks))
        put(0, at, (dq * cosine - partner(dq) * sine).astype(BF))
        put(1, at, (dk * cosine - partner(dk) * sine).astype(BF))
        put(2, at, jnp.concatenate(dvs, 1).astype(BF))


def qkv_backward_step(step, steps, dqkv, dh, u, order, gains, proj, du, total):
    @pl.when(step == 0)
    def _():
        total[...] = jnp.zeros_like(total)

    total[...] += contract_last(dqkv, stack_rows(proj))

    @pl.when(step == steps - 1)
    def _():
        unit, scale = normal(dot(u[...], order[...]))
        dxn = total[...]
        back = normal_back(dxn * gain_rows(gains)[0:1], unit, scale)
        du[...] = (dh[...] + to_absolute(back, order[...])).astype(BF)


def parted(refs, *sizes):
    out, low = [], 0
    for size in sizes:
        out.append(refs[low : low + size])
        low += size
    return *out, refs[low:]


def attn_forward_kernel(n, micro, steps, *refs):
    args, proj, out, gains, rest = parted(refs, 6, n, n, n)
    h, yn, qkv, xn = rest
    attn_forward_step(pl.program_id(0), steps, micro, *args, proj, out, gains, xn, qkv, h, yn)


def mlp_forward_kernel(n, steps, *refs):
    args, gate, up, down, rest = parted(refs, 3, n, n, n)
    mlp_forward_step(pl.program_id(0), steps, *args, gate, up, down, *rest)


def mlp_backward_kernel(n, steps, *refs):
    args, (one, two), gains, gate, up, down, rest = parted(refs, 3, 2, n, n, n, n)
    dzr, dg, dv, dh, da, total = rest
    weights = (gains, gate, up, down)
    step = pl.program_id(0)

    @pl.when(step == 0)
    def _():
        dzr[...] = dot(args[0][...], args[2][...]).astype(BF)

    mlp_backward_step(step, steps, dzr, *args, one[...], two[...], *weights, dh, da, total, (dg, dv))


def heads_backward_kernel(n, micro, *refs):
    args, out, (dqkv,) = parted(refs, 8, n)
    width = refs[0].shape[1]

    def put(part, at, value):
        dqkv[at, part * width : (part + 1) * width] = value

    heads_backward_step(micro, *args, out, put)


def middle_kernel(n, micro, *refs):
    args, proj, out, gains, gate, up, down, outs, scratch = parted(refs, 7, n, n, n, n, n, n, 11)
    u, dz, order, cos, sin, col, row = args
    xn, qkv, lse, attended, h, yn, mid, one, two, z, du = outs
    total, dzr, dh, da, dqkv = scratch
    step = pl.program_id(0)
    turns = (cos, sin, col, row)

    @pl.when(step < 3)
    def _():
        attn_forward_step(step, 3, micro, u, order, *turns, proj, out, gains, xn, qkv, h, yn, (lse, attended))

    @pl.when((step >= 3) & (step < 6))
    def _():
        mlp_forward_step(step - 3, 3, yn, h, order, gate, up, down, z, total, (mid, one, two))

    @pl.when(step == 6)
    def _():
        dzr[...] = dot(dz[...], order[...]).astype(BF)

    @pl.when((step >= 6) & (step < 9))
    def _():
        at = pl.ds(pl.multiple_of((8 - step) * MLP_TILE, 128), MLP_TILE)
        weights = (gains, gate, up, down)
        mlp_backward_step(step - 6, 3, dzr, dz, h, order, one[:, at], two[:, at], *weights, dh, da, total)

    @pl.when(step == 9)
    def _():
        def put(part, at, value):
            dqkv[part, at] = value

        heads_backward_step(micro, da, order, *turns, qkv, lse, out, put)

    @pl.when(step >= 9)
    def _():
        qkv_backward_step(step - 9, 3, dqkv[11 - step], dh, u, order, gains, proj, du, total)


def qkv_backward_kernel(n, steps, *refs):
    (dqkv, *args), gains, proj, (du, total) = parted(refs, 4, n, n)
    qkv_backward_step(pl.program_id(0), steps, dqkv[...], *args, gains, proj, du, total)


def gain_grad(weight, grad, gain):
    return jnp.sum(weight.astype(F32) * grad, 1) / gain.astype(F32)


def columns(pieces, tile, place):
    return [pl.BlockSpec((p.shape[0], tile), lambda j: (0, place(j))) for p in pieces]


def whole(array):
    return pl.BlockSpec(array.shape, lambda j: (0,) * array.ndim)


def shape_of(rows, cols, kind=BF):
    return jax.ShapeDtypeStruct((rows, cols), kind)


def fixed(rows, cols):
    return pl.BlockSpec((rows, cols), lambda j: (0, 0))


def tiled(rows, cols, start=0, count=None):
    if count is None:
        return pl.BlockSpec((rows, cols), lambda j: (0, j))
    return pl.BlockSpec((rows, cols), lambda j: (0, jnp.clip(j - start, 0, count - 1)))


def cost(flops, weights):
    return pl.CostEstimate(flops=int(flops) // 64, bytes_accessed=int(weights * 2) // 64, transcendentals=0)


def attn_forward(u, pieces, common):
    n, (tokens, width) = len(pieces), u.shape
    steps = 3 * width // ATTN_TILE
    args = (u, *common)
    return pl.pallas_call(
        functools.partial(attn_forward_kernel, n, common[-1].shape[0], steps),
        grid=(steps,),
        in_specs=[whole(a) for a in args]
        + columns(pieces, ATTN_TILE, lambda j: j)
        + columns(pieces, width, lambda j: 3)
        + columns(pieces, 128, lambda j: 4 * width // 128),
        out_specs=[fixed(tokens, width), fixed(tokens, width)],
        out_shape=[shape_of(tokens, width, F32), shape_of(tokens, width)],
        scratch_shapes=[pltpu.VMEM((steps, tokens, ATTN_TILE), BF), pltpu.VMEM((tokens, width), BF)],
        compiler_params=PARAMS,
        cost_estimate=cost(2 * tokens * 6 * width * width, 5 * width * width),
    )(*args, *pieces, *pieces, *pieces)


def mlp_forward(yn, h, pieces, order):
    n, (tokens, width) = len(pieces), yn.shape
    hidden = pieces[0].shape[1] // 3
    steps = hidden // MLP_TILE
    args = (yn, h, order)
    return pl.pallas_call(
        functools.partial(mlp_forward_kernel, n, steps),
        grid=(steps,),
        in_specs=[whole(a) for a in args]
        + columns(pieces, MLP_TILE, lambda j: j)
        + columns(pieces, MLP_TILE, lambda j: steps + j)
        + columns(pieces, MLP_TILE, lambda j: 2 * steps + j),
        out_specs=fixed(tokens, width),
        out_shape=shape_of(tokens, width),
        scratch_shapes=[pltpu.VMEM((tokens, width), F32)],
        compiler_params=PARAMS,
        cost_estimate=cost(6 * tokens * hidden * width, 4 * hidden * width),
    )(*args, *pieces, *pieces, *pieces)


def middle(u, dz, common, pieces_a, pieces_m):
    n, (tokens, width) = len(pieces_a), u.shape
    hidden = pieces_m[0].shape[1] // 3
    args = (u, dz, *common)

    def proj_at(j):
        return jnp.where(j < 3, j, jnp.where(j < 9, 2, 11 - j))

    def mlp_at(j):
        return jnp.where(j < 6, jnp.maximum(j - 3, 0), jnp.maximum(8 - j, 0))

    kinds = [(width, BF), None, (128, F32), (width, BF), (width, F32), (width, BF)]
    kinds += [(hidden, BF)] * 3 + [(width, BF)] * 2
    cube = (3, tokens, width)
    return pl.pallas_call(
        functools.partial(middle_kernel, n, common[-1].shape[0]),
        grid=(12,),
        in_specs=[whole(a) for a in args]
        + columns(pieces_a, ATTN_TILE, proj_at)
        + columns(pieces_a, width, lambda j: 3)
        + columns(pieces_a, 128, lambda j: 4 * width // 128)
        + columns(pieces_m, MLP_TILE, mlp_at)
        + columns(pieces_m, MLP_TILE, lambda j: 3 + mlp_at(j))
        + columns(pieces_m, MLP_TILE, lambda j: 6 + mlp_at(j)),
        out_specs=[fixed(tokens, k[0]) if k else pl.BlockSpec(cube, lambda j: (0, 0, 0)) for k in kinds],
        out_shape=[shape_of(tokens, *k) if k else jax.ShapeDtypeStruct(cube, BF) for k in kinds],
        scratch_shapes=[
            pltpu.VMEM((tokens, width), F32),
            pltpu.VMEM((tokens, width), BF),
            pltpu.VMEM((tokens, width), F32),
            pltpu.VMEM((tokens, width), BF),
            pltpu.VMEM(cube, BF),
        ],
        compiler_params=PARAMS,
        cost_estimate=cost(12 * tokens * (hidden + width) * width, 12 * hidden * width),
    )(*args, *pieces_a, *pieces_a, *pieces_a, *pieces_m, *pieces_m, *pieces_m)


def mlp_backward(dz, h, one, two, pieces_a, pieces, order):
    n, (tokens, width) = len(pieces), dz.shape
    hidden = pieces[0].shape[1] // 3
    steps = hidden // MLP_TILE
    args = (dz, h, order)
    return pl.pallas_call(
        functools.partial(mlp_backward_kernel, n, steps),
        grid=(steps,),
        in_specs=[whole(a) for a in args]
        + [tiled(tokens, MLP_TILE)] * 2
        + columns(pieces_a, 128, lambda j: 4 * width // 128)
        + columns(pieces, MLP_TILE, lambda j: j)
        + columns(pieces, MLP_TILE, lambda j: steps + j)
        + columns(pieces, MLP_TILE, lambda j: 2 * steps + j),
        out_specs=[fixed(tokens, width)] + [tiled(tokens, MLP_TILE)] * 2 + [fixed(tokens, width)] * 2,
        out_shape=[shape_of(tokens, width)]
        + [shape_of(tokens, hidden)] * 2
        + [shape_of(tokens, width, F32), shape_of(tokens, width)],
        scratch_shapes=[pltpu.VMEM((tokens, width), F32)],
        compiler_params=PARAMS,
        cost_estimate=cost(6 * tokens * hidden * width, 4 * hidden * width),
    )(*args, one, two, *pieces_a, *pieces, *pieces, *pieces)


def heads_backward(da, common, qkv, lse, pieces):
    n, (tokens, width) = len(pieces), da.shape
    args = (da, *common, qkv, lse)
    return pl.pallas_call(
        functools.partial(heads_backward_kernel, n, common[-1].shape[0]),
        grid=(1,),
        in_specs=[whole(a) for a in args] + columns(pieces, width, lambda j: 3),
        out_specs=fixed(tokens, 3 * width),
        out_shape=shape_of(tokens, 3 * width),
        compiler_params=PARAMS,
        cost_estimate=cost(2 * tokens * width * width, width * width),
    )(*args, *pieces)


def qkv_backward(dqkv, dh, u, order, pieces):
    n, (tokens, width) = len(pieces), u.shape
    steps = 3 * width // ATTN_TILE
    args = (dh, u, order)
    return pl.pallas_call(
        functools.partial(qkv_backward_kernel, n, steps),
        grid=(steps,),
        in_specs=[tiled(tokens, ATTN_TILE)]
        + [whole(a) for a in args]
        + columns(pieces, 128, lambda j: 4 * width // 128)
        + columns(pieces, ATTN_TILE, lambda j: j),
        out_specs=fixed(tokens, width),
        out_shape=shape_of(tokens, width),
        scratch_shapes=[pltpu.VMEM((tokens, width), F32)],
        compiler_params=PARAMS,
        cost_estimate=cost(2 * tokens * 3 * width * width, 3 * width * width),
    )(dqkv, *args, *pieces, *pieces)


def product_kernel(counts, uses, *refs):
    count = len(counts)
    lefts, rights, rest = parted(refs, max(uses) + 1, count)
    outs, turned = rest[:-1], rest[-1]
    step = pl.program_id(0)

    @pl.when(step == 0)
    def _():
        for k, left in enumerate(lefts):
            turned[k] = left[...].T

    begin = 0
    for which in range(count):

        @pl.when((step >= begin) & (step < begin + counts[which]))
        def _(which=which):
            value = dot(turned[uses[which]], rights[which][...])
            low = 0
            for out in outs:
                out[...] = value[low : low + out.shape[0]].astype(BF)
                low += out.shape[0]

        begin += counts[which]


def make_product(lefts, rights, tile, uses):
    tokens = lefts[0].shape[0]
    counts = [r.shape[1] // tile for r in rights]
    steps = sum(counts)
    starts = [sum(counts[:k]) for k in range(len(counts))]

    def product(part, sizes):
        span = sum(sizes)
        return pl.pallas_call(
            functools.partial(product_kernel, counts, uses),
            grid=(steps,),
            in_specs=[pl.BlockSpec((tokens, span), lambda j: (0, part)) for _ in lefts]
            + [tiled(tokens, tile, s, c) for s, c in zip(starts, counts)],
            out_specs=[tiled(r, tile) for r in sizes],
            out_shape=[shape_of(r, steps * tile) for r in sizes],
            scratch_shapes=[pltpu.VMEM((len(lefts), span, tokens), BF)],
            compiler_params=PARAMS,
            cost_estimate=cost(2 * tokens * span * steps * tile, span * steps * tile),
        )(*lefts, *rights)

    return product


def shards(tokens_in, attn_proj, attn_out, mlp_in, mlp_out, gain_attn, gain_mlp, lengths, cotangent):
    section = lax.axis_index("section")
    micro, slots, width = tokens_in.shape
    tokens = micro * slots
    three, hidden = attn_proj.shape[2], mlp_out.shape[2]
    padded = -(-hidden // MLP_TILE) * MLP_TILE
    gains = jnp.zeros((gain_attn.shape[1], GAIN_TILE), BF)
    gains = gains.at[:, 0].set(gain_attn[0]).at[:, 1].set(gain_mlp[0])
    gap = jnp.zeros((gain_attn.shape[1], padded - hidden), BF)
    order = relative_order(lax.axis_index("fsdp"))
    pieces_a, pieces_m, order = gather(
        jnp.concatenate([attn_proj[0], attn_out[0], gains], 1),
        jnp.concatenate([mlp_in[0, :, :hidden], gap, mlp_in[0, :, hidden:], gap, mlp_out[0], gap], 1),
        order,
    )
    base = jnp.where(section == 0, 10000.0, 160000.0).astype(F32)
    reach = jnp.where(section == 0, WINDOW / 2.0, 4.0 * slots).astype(F32)
    segment, inner = segment_info(lengths[:, 0], slots)
    half = HEAD_DIM // 2
    freqs = jnp.exp(-jnp.log(base) * (jnp.arange(half, dtype=F32) * (2.0 / HEAD_DIM)))
    angles = jnp.tile(inner.reshape(tokens, 1).astype(F32) * freqs, (1, 128 // half))
    col = jnp.stack([segment.reshape(tokens).astype(F32), inner.reshape(tokens).astype(F32)], 1)
    col = jnp.concatenate([col, jnp.broadcast_to(reach, (tokens, 126))], 1)
    row = jnp.stack([segment, inner] + [inner] * 6, 1).astype(F32)
    common = (order, jnp.cos(angles), jnp.sin(angles), col, row)

    first_in = tokens_in.reshape(tokens, width)
    hid, yn = attn_forward(first_in, pieces_a, common)
    m_block, m_near, m_near2 = pieces_m
    m_near, m_near2, yn = tie(m_near, m_near2, yn)
    m_far, m_far2 = far(m_near, m_near2)
    near_core = core(m_block, m_near, m_near2)
    far_core = core(m_far, m_far2)
    pieces_m = (m_block, m_near, m_far, m_far2, m_near2, *near_core[:2], *far_core, near_core[2])
    middle_out = mlp_forward(yn, hid, pieces_m, order)
    received = lax.ppermute(middle_out, "section", [(0, 1)])
    layer_in = jnp.where(section == 0, first_in, received)
    last_grad = cotangent.reshape(tokens, width)
    xn, qkv, lse, attended, hid, yn, mid, one, two, result, middle_grad = middle(
        layer_in, last_grad, common, pieces_a, pieces_m
    )
    received = lax.ppermute(middle_grad, "section", [(1, 0)])
    grad_out = jnp.where(section == 1, last_grad, received)
    half = width // 2
    dzr, dg, dv, dh, da = mlp_backward(grad_out, hid, one, two, pieces_a, pieces_m, order)
    product = make_product((yn, dzr), (dg, dv, mid), MLP_TILE, (0, 0, 1))
    sent_m, yn = tie(product(1, (half,))[0], yn)
    got_m = send(sent_m, "core")
    product = make_product((yn, dzr), (dg, dv, mid), MLP_TILE, (0, 0, 1))
    own_m = product(0, cut(half))
    got_m, da = tie(got_m, da)
    here_m, after_m, far_m, far_m2, before_m = ring_start(own_m, got_m)
    far_m, far_m2 = send(far_m.astype(BF), "first", 1), send(far_m2.astype(BF), "first", -1)
    dqkv = heads_backward(da, common, qkv, lse, pieces_a)
    far_m, far_m2, dqkv = tie(far_m, far_m2, dqkv)
    *mix_m, dqkv = tie(*ring_mix(after_m, before_m, far_m, far_m2), dqkv)
    near_m = send(mix_m[0], "first", 1), send(mix_m[1], "first", -1)
    grad_in = qkv_backward(dqkv, dh, layer_in, order, pieces_a)
    dqkv, grad_in = tie(dqkv, grad_in)
    *own_a, sent_a = make_product((xn, attended), (dqkv, da), width, (0, 1))(0, (*cut(half), half))
    got_a = send(sent_a, "core")
    here_a, after_a, far_a, far_a2, before_a = ring_start(own_a, got_a)
    far_a, far_a2 = send(far_a.astype(BF), "first", 1), send(far_a2.astype(BF), "first", -1)
    ends_m = direct(ring_close(here_m, *near_m))
    mix_a = ring_mix(after_a, before_a, far_a, far_a2)
    *ends_m, mix_a, mix_a2 = tie(*ends_m, *mix_a)
    near_a = send(mix_a, "first", 1), send(mix_a2, "first", -1)
    sum_m = close_z(*ends_m)
    sum_a = close_z(*direct(ring_close(here_a, *near_a)))
    grad_proj, grad_out_proj = sum_a[:, :three], sum_a[:, three:]
    grad_up = jnp.concatenate([sum_m[:, :hidden], sum_m[:, padded : padded + hidden]], 1)
    return (
        result.reshape(1, micro, slots, width),
        grad_in.reshape(1, micro, slots, width),
        grad_proj[None],
        grad_out_proj[None],
        grad_up[None],
        sum_m[:, 2 * padded : 2 * padded + hidden][None],
        gain_grad(attn_proj[0], grad_proj, gain_attn[0])[None],
        gain_grad(mlp_in[0], grad_up, gain_mlp[0])[None],
    )


def solution(mesh):
    in_specs = (
        P(None, "fsdp", None),
        P("section", "fsdp", None),
        P("section", "fsdp", None),
        P("section", "fsdp", None),
        P("section", "fsdp", None),
        P("section", "fsdp"),
        P("section", "fsdp"),
        P(None, "fsdp", None),
        P(None, "fsdp", None),
    )
    out_specs = (
        P("section", None, "fsdp", None),
        P("section", None, "fsdp", None),
        P("section", "fsdp", None),
        P("section", "fsdp", None),
        P("section", "fsdp", None),
        P("section", "fsdp", None),
        P("section", "fsdp"),
        P("section", "fsdp"),
    )
    return jax.shard_map(shards, mesh=mesh, in_specs=in_specs, out_specs=out_specs, check_vma=False)
```
